32 devices in a mesh: vol: 2 (over x), row: 4 (over y, core), col: 4 (over z).
Axes of the slice: x: 2, y: 2, z: 4, core: 2. Of those that a mesh axis runs over, the one named last changes fastest.
Arguments:
- source: float32 [16, 16, 32, 512], P(None, 'vol', 'row', 'col'), may hold values from -8 to 8
- labels: int32 [16, 32, 512], P('vol', 'row', 'col'), may hold values from 0 to 7
- region_coeff: float32 [8], replicated, may hold values from 0.3 to 3
- node_cell: int32 [4096], P(('vol', 'row', 'col')), may hold values from 0 to 8191
- node_pos: float32 [3, 4096], P(None, ('vol', 'row', 'col')), may hold values from 0 to 1
- incident: float32 [16, 4096], P(None, ('vol', 'row', 'col')), may hold values from -6 to 6
Outputs:
- field: float32 [16, 16, 32, 512], P(None, 'vol', 'row', 'col')
- flux: float32 [16, 4096], P(None, ('vol', 'row', 'col'))
The draws below stay inside these ranges and needn't reach their ends.
Inputs may be any that keep to these rules, and one draw needn't show every extreme that they name: `node_cell`: cell of node j inside its volume block, several nodes may share a cell.
All inputs are finite; a program needn't handle non-finite values.
Results may differ from the reference program's by a relative error of at most 0.0029.
Values may be sent and summed in bfloat16 or wider, within the bound.
No kernel may reach another device: no remote copies, remote signals or barrier semaphores. Data moves between devices by JAX's collectives and lax.ppermute only.
A program may use at most 64 MiB of HBM per device.

```python
import math
import jax
import jax.numpy as jnp
from jax import lax

E = 16
REGIONS = 8
NODE_DEV = 128
CX = 8
CY = 8
CZ = 128
SWEEPS = 4
ITERS = 2
NX = 16
NY = 32
NZ = 512
M = 4096
N_ROW = 4
N_COL = 4


def with_ends(array, rng, least, largest):
    place = [jax.random.randint(jax.random.fold_in(rng, axis), (), 0, length) for axis, length in enumerate(array.shape)]
    longest = array.shape.index(max(array.shape))
    neighbour = place[:longest] + [(place[longest] + 1) % array.shape[longest]] + place[longest + 1:]
    return array.at[tuple(place)].set(least).at[tuple(neighbour)].set(largest)


def levels(stream_key, dims, cuts, least, top_value):
    level, own = 1.0, jax.random.fold_in(stream_key, 6)
    for dim, blocks in cuts:
        heights = jnp.exp(jax.random.uniform(jax.random.fold_in(own, dim), (blocks,), jnp.float32, least / len(cuts), top_value / len(cuts)))
        level = level * jnp.repeat(heights, dims[dim] // blocks).reshape([-1 if axis == dim else 1 for axis in range(len(dims))])
    return level


def gaussian(stream_key, extent, spread, limit, shards=(), held_as=jnp.bfloat16):
    drawn = jax.random.normal(stream_key, extent, jnp.float32) * spread
    if len(shards) > 0:
        drawn = levels(stream_key, extent, shards, -0.22, 0.18) * drawn
    return jnp.clip(drawn, min=-limit, max=limit).astype(held_as)


def setup_inputs(seed: int = 0) -> dict:
    arg_keys = jax.random.split(jax.random.key(seed), 7)
    return {
        "source": gaussian(arg_keys[0], (E, NX, NY, NZ), 1.0, 8.0, ((1, 2), (2, 4), (3, 4)), jnp.float32),
        "labels": with_ends(jax.random.randint(arg_keys[1], (NX, NY, NZ), 0, REGIONS), jax.random.fold_in(arg_keys[1], 1), 0, REGIONS - 1).astype(jnp.int32),
        "region_coeff": jnp.clip(jnp.exp(jax.random.uniform(arg_keys[2], (REGIONS,), jnp.float32, math.log(0.3), math.log(3.0))), 0.3, 3.0),
        "node_cell": with_ends(jax.random.randint(arg_keys[3], (M,), 0, CX * CY * CZ), jax.random.fold_in(arg_keys[3], 1), 0, (CX * CY * CZ) - 1).astype(jnp.int32),
        "node_pos": jnp.clip(1.0 * jax.random.uniform(arg_keys[4], (3, M), jnp.float32) ** levels(arg_keys[4], (3, M), ((1, 32),), -0.2, 0.2), 0.0, 1.0),
        "incident": gaussian(arg_keys[5], (E, M), 1.0, 6.0, ((1, 32),), jnp.float32),
    }


MASS_TERM = 0.05
SOFTENING = 0.05
KERNEL_GAIN = 2.0
COUPLING = 1.0

def sweep_weights(count):
    return [1.0 / (1.05 - 0.95 * math.cos(math.pi * (2 * sweep + 1) / (2 * count))) for sweep in range(count)]

def face_terms(kcoef):
    padded = jnp.pad(kcoef, 1)
    neighbours = [padded[2:, 1:-1, 1:-1], padded[:-2, 1:-1, 1:-1], padded[1:-1, 2:, 1:-1], padded[1:-1, :-2, 1:-1], padded[1:-1, 1:-1, 2:], padded[1:-1, 1:-1, :-2]]
    faces = [0.5 * (kcoef + other) for other in neighbours]
    diag = MASS_TERM + faces[0]
    for other in faces[1:]:
        diag = diag + other
    return (faces, diag)

def operate(values, faces, diag):
    padded = jnp.pad(values, ((0, 0), (1, 1), (1, 1), (1, 1)))
    neighbours = [padded[:, 2:, 1:-1, 1:-1], padded[:, :-2, 1:-1, 1:-1], padded[:, 1:-1, 2:, 1:-1], padded[:, 1:-1, :-2, 1:-1], padded[:, 1:-1, 1:-1, 2:], padded[:, 1:-1, 1:-1, :-2]]
    total = faces[0] * neighbours[0]
    for number in range(1, 6):
        total = total + faces[number] * neighbours[number]
    return diag * values - total

def node_index(node_cell):
    nodes = jnp.arange(M, dtype=jnp.int32)
    block = nodes // NODE_DEV
    block_x = block // (N_ROW * N_COL)
    block_y = block // N_COL % N_ROW
    block_z = block % N_COL
    local_x = node_cell // (CY * CZ)
    local_y = node_cell // CZ % CY
    local_z = node_cell % CZ
    global_x = block_x * CX + local_x
    global_y = block_y * CY + local_y
    global_z = block_z * CZ + local_z
    return ((global_x * NY + global_y) * NZ + global_z).astype(jnp.int32)

def surface_product(traces, node_pos):
    scale = KERNEL_GAIN / math.sqrt(M)
    blocking = math.gcd(M, 1024)
    blocks = node_pos.reshape(3, M // blocking, blocking).transpose(1, 0, 2)
    wide_traces = lax.optimization_barrier(traces).astype(jnp.float32)

    def one_block(block_pos):
        delta_x = node_pos[0][:, None] - block_pos[0][None, :]
        delta_y = node_pos[1][:, None] - block_pos[1][None, :]
        delta_z = node_pos[2][:, None] - block_pos[2][None, :]
        squared = delta_x * delta_x + delta_y * delta_y + delta_z * delta_z
        tile = (scale * lax.rsqrt(squared + SOFTENING * SOFTENING)).astype(jnp.bfloat16)
        wide_tile = lax.optimization_barrier(tile).astype(jnp.float32)
        return jnp.dot(wide_traces, wide_tile, preferred_element_type=jnp.float32)
    result = lax.map(one_block, blocks)
    return result.transpose(1, 0, 2).reshape(traces.shape[0], M)

def reference(source, labels, region_coeff, node_cell, node_pos, incident):
    kcoef = region_coeff[labels]
    faces, diag = face_terms(kcoef)
    flat = node_index(node_cell)
    field = jnp.zeros(source.shape, jnp.float32)
    flux = incident
    weights = sweep_weights(SWEEPS)
    for outer in range(ITERS):
        rhs = source.reshape(E, -1).at[:, flat].add(COUPLING * flux).reshape(source.shape)
        for weight in weights:
            field = field + weight * (rhs - operate(field, faces, diag)) / diag
        traces = field.reshape(E, -1)[:, flat].astype(jnp.bfloat16)
        flux = incident + surface_product(traces, node_pos)
    return (field, flux)
```

```python
import functools
import math

import jax
import jax.numpy as jnp
from jax import lax
from jax.experimental import pallas as pl
from jax.experimental.pallas import tpu as pltpu
from jax.sharding import PartitionSpec as P

SWEEPS = 4
ITERS = 2

MASS_TERM = 0.05
SOFTENING = 0.05
KERNEL_GAIN = 2.0

HALO = SWEEPS
RHS_HALO = SWEEPS - 1
STRIP = 2 * HALO
AXES = ("vol", "row", "col")
F32, BF16 = jnp.float32, jnp.bfloat16
NT = (((1,), (1,)), ((), ()))


def sweep_weights(count):
    return [
        1.0 / (1.05 - 0.95 * math.cos(math.pi * (2 * sweep + 1) / (2 * count)))
        for sweep in range(count)
    ]


def iota(shape, dim):
    return lax.broadcasted_iota(jnp.int32, shape, dim)


def kernel_call(body, out_shape, scratch=(), smem=0, operands=(), name=None):
    specs = [pl.BlockSpec(memory_space=pltpu.SMEM)] * smem
    specs += [pl.BlockSpec(memory_space=pltpu.VMEM)] * (len(operands) - smem)
    return pl.pallas_call(
        body,
        out_shape=out_shape,
        in_specs=specs,
        out_specs=jax.tree.map(lambda _: pl.BlockSpec(memory_space=pltpu.VMEM), out_shape),
        scratch_shapes=list(scratch),
        compiler_params=pltpu.CompilerParams(vmem_limit_bytes=56 * 1024 * 1024),
        name=name,
    )(*operands)


def pick(refs, low, even, rows, size):
    first = refs[0][pl.ds(rows, size), :]
    second = refs[1][pl.ds(rows, size), :] if len(refs) > 1 else jnp.zeros_like(first)
    flag = jnp.full(first.shape, even, jnp.int32).astype(first.dtype)
    mine, other = (1 - flag, flag) if low else (flag, 1 - flag)
    return first * mine + second * other


def exchange(array, axis, arrays=None):
    count = lax.axis_size(axis)
    arrays = arrays or [array] * 2
    out = []
    for which in range(2 if count > 2 else 1):
        pairs = []
        for i in range(which, count - 1, 2):
            pairs += [(i, i + 1), (i + 1, i)]
        out.append(lax.ppermute(arrays[which], axis, pairs))
    return out


def edge_picker(cz, lanes):
    z, lane = iota((cz, lanes), 0), iota((cz, lanes), 1)
    k = lane % STRIP
    wanted = jnp.where(k < HALO, HALO - 1 - k, cz - 1 - k + HALO)
    return (z == wanted).astype(F32), lane // STRIP - HALO


def strip_rows(read, cx, cy, cz):
    base, lane_y = edge_picker(cz, cz)
    total = None
    for y in range(cy):
        rows = jnp.concatenate([read(x, y).astype(BF16) for x in range(cx)], axis=0)
        picked = jnp.where(lane_y == y, base, 0.0).astype(BF16)
        part = jnp.dot(rows, picked, preferred_element_type=F32)
        total = part if total is None else total + part
    return total.astype(BF16)


def first_kernel(dims, source, labels, incident, cells, rhs_out, send_out, left):
    cx, cy, cz, ch, nodes = dims
    cell = cells[...]
    row, z = cell // cz, cell % cz
    hits = (iota((cz, nodes), 0) == z).astype(BF16)
    flux = incident[...]
    top = flux.astype(BF16).astype(F32)
    rest = flux - top
    for r in range(cx * cy):
        here = jnp.broadcast_to(row == r, (ch, nodes))
        left[r * ch:(r + 1) * ch, :nodes] = jnp.where(here, top, 0.0).astype(BF16)
        left[r * ch:(r + 1) * ch, nodes:] = jnp.where(here, rest, 0.0).astype(BF16)
    added = lax.dot_general(
        left[...], jnp.concatenate([hits, hits], axis=1), NT, preferred_element_type=F32
    )
    rhs_out[...] = added
    for r in range(cx * cy):
        rhs_out[r * ch:(r + 1) * ch, :] += source[pl.ds(r, ch, stride=cx * cy), :]

    def read(x, y):
        start = (x * cy + y) * ch
        return rhs_out[start:start + ch, :]

    send_out[:cx * ch, :] = strip_rows(read, cx, cy, cz)
    base, lane_y = edge_picker(cz, cz)
    codes = (labels[...] + 1).astype(F32).astype(BF16)
    strips = jnp.dot(codes, base.astype(BF16), preferred_element_type=F32)
    own = (iota(strips.shape, 0) % cy) == lane_y[:1, :]
    strips = jnp.where(own, strips, 0.0).reshape(cx, cy, cz).sum(axis=1)
    send_out[cx * ch:, :] = jnp.concatenate(
        [strips, jnp.zeros((16 - cx, cz), F32)], axis=0
    ).astype(BF16)


def second_kernel(dims, width, with_labels, nz, nx, place, *refs):
    cx, cy, cz, ch, nodes = dims
    main, refs = refs[0], refs[1:]
    if with_labels:
        labels, refs = refs[0], refs[1:]
    zrecv, refs = refs[:nz], refs[nz:]
    strip_out, sends, refs = refs[0], refs[1:1 + nx], refs[1 + nx:]
    even_x = 1 - place[0] % 2
    even_z = 1 - place[2] % 2
    rows = cx * ch + (16 if with_labels else 0)
    lane = iota((rows, cz), 1)
    upper = pick(zrecv, False, even_z, 0, rows)
    lower = pick(zrecv, True, even_z, 0, rows)
    strip_out[...] = jnp.where(
        lane % STRIP < HALO, upper.astype(F32), lower.astype(F32)
    ).astype(BF16)
    if with_labels:
        (codes,) = refs
        codes[...] = jnp.zeros_like(codes)
        codes[:16, :] = strip_out[cx * ch:, :].astype(F32)
    slab = width * cy * ch
    for which in range(nx):
        upward = even_x if which == 0 else 1 - even_x
        x0 = upward * (cx - width)
        send = sends[which]
        send[:slab, :] = main[pl.ds(pl.multiple_of(x0 * (cy * ch), 16), slab), :].astype(BF16)
        send[slab:slab + width * ch, :] = strip_out[
            pl.ds(pl.multiple_of(x0 * ch, 16), width * ch), :
        ]
        if with_labels:
            start = slab + width * ch
            x0 = upward * (cx - HALO)
            send[start:start + HALO * cy, :] = (
                labels[pl.ds(pl.multiple_of(x0 * cy, 8), HALO * cy), :] + 1
            ).astype(F32).astype(BF16)
            send[start + HALO * cy:, :] = codes[pl.ds(x0, 16), :].astype(BF16)


def third_kernel(dims, width, with_labels, nx, ny, place, *refs):
    cx, cy, cz, ch, nodes = dims
    main, refs = refs[0], refs[1:]
    if with_labels:
        labels, refs = refs[0], refs[1:]
    strip, refs = refs[0], refs[1:]
    xrecv, refs = refs[:nx], refs[nx:]
    sends, refs = refs[:ny], refs[ny:]
    even_x = 1 - place[0] % 2
    even_y = 1 - place[1] % 2
    ex = cx + 2 * width
    slab = width * cy * ch
    if with_labels:
        codes, strip_codes, picked = refs
        fill_codes(dims, labels, strip, xrecv, slab + width * ch, even_x, codes, strip_codes)
    for which in range(ny):
        send = sends[which]
        upward = even_y if which == 0 else 1 - even_y
        y0 = upward * (cy - width)
        size = width * ch
        for x in range(ex):
            if width <= x < width + cx:
                start = pl.multiple_of(((x - width) * cy + y0) * ch, 16)
                piece = main[pl.ds(start, size), :].astype(BF16)
            else:
                low = x < width
                start = pl.multiple_of(((x if low else x - width - cx) * cy + y0) * ch, 16)
                piece = pick(xrecv, low, even_x, start, size)
            send[x * size:(x + 1) * size, :] = piece
        start = ex * size
        send[start:start + width * ch, :] = pick(xrecv, True, even_x, slab, width * ch)
        send[start + width * ch:start + (width + cx) * ch, :] = strip[:cx * ch, :]
        send[start + (width + cx) * ch:start + ex * ch, :] = pick(
            xrecv, False, even_x, slab, width * ch
        )
        if with_labels:
            start += ex * ch
            y0 = upward * (cy - HALO)
            tall = cx + 2 * HALO
            for x in range(tall):
                picked[x * HALO:(x + 1) * HALO, :] = codes[pl.ds(x * cy + y0, HALO), :]
            send[start:start + tall * HALO, :] = picked[...].astype(BF16)
            send[start + tall * HALO:, :] = strip_codes[...].astype(BF16)


def fill_codes(dims, labels, strip, xrecv, start, even_x, codes, strip_codes):
    cx, cy, cz, ch, nodes = dims
    side = HALO * cy
    codes[:side, :] = pick(xrecv, True, even_x, start, side).astype(F32)
    codes[side:side + cx * cy, :] = (labels[...] + 1).astype(F32)
    codes[side + cx * cy:, :] = pick(xrecv, False, even_x, start, side).astype(F32)
    strip_codes[:HALO, :] = pick(xrecv, True, even_x, start + side, 16).astype(F32)[:HALO]
    strip_codes[HALO:HALO + cx, :] = strip[cx * ch:cx * ch + 16, :].astype(F32)[:cx]
    strip_codes[HALO + cx:, :] = pick(xrecv, False, even_x, start + side, 16).astype(F32)[:HALO]


def assemble(dims, width, main, strip, xrecv, yrecv, even_x, even_y, out, out_strip):
    cx, cy, cz, ch, nodes = dims
    ex = cx + 2 * width
    out[HALO:HALO + cx, HALO:HALO + cy] = main[...].reshape(cx, cy, ch, cz)
    slab = width * cy * ch
    low = pick(xrecv, True, even_x, 0, slab).astype(F32)
    out[HALO - width:HALO, HALO:HALO + cy] = low.reshape(width, cy, ch, cz)
    high = pick(xrecv, False, even_x, 0, slab).astype(F32)
    out[HALO + cx:HALO + cx + width, HALO:HALO + cy] = high.reshape(width, cy, ch, cz)
    size = ex * width * ch
    low = pick(yrecv, True, even_y, 0, size).astype(F32)
    out[HALO - width:HALO + cx + width, HALO - width:HALO] = low.reshape(ex, width, ch, cz)
    high = pick(yrecv, False, even_y, 0, size).astype(F32)
    out[HALO - width:HALO + cx + width, HALO + cy:HALO + cy + width] = high.reshape(
        ex, width, ch, cz
    )
    own = jnp.concatenate(
        [
            pick(xrecv, True, even_x, slab, width * ch),
            strip[:cx * ch, :],
            pick(xrecv, False, even_x, slab, width * ch),
        ],
        axis=0,
    ).astype(F32)
    low = pick(yrecv, True, even_y, size, ex * ch).astype(F32)
    high = pick(yrecv, False, even_y, size, ex * ch).astype(F32)
    full = join_strips(own, low, high, cy)
    out_strip[HALO - width:HALO + cx + width] = full.reshape(ex, ch, cz)


def join_strips(own, low, high, cy):
    lane = iota(own.shape, 1)
    shift = cy * STRIP
    lanes = own.shape[1]
    low = pltpu.roll(low, lanes - shift, 1)
    high = pltpu.roll(high, shift, 1)
    return jnp.where(
        lane < HALO * STRIP, low, jnp.where(lane < (HALO + cy) * STRIP, own, high)
    )


def sweep(dims, reach, weight, src, src_strip, dst, dst_strip, r, r_strip, c, c_strip):
    cx, cy, cz, ch, nodes = dims
    lane = iota((ch, cz), 1)
    first, last = lane == 0, lane == cz - 1

    def spread(ref, k, x, y):
        return jnp.broadcast_to(ref[k, x, y:y + 1, :], (ch, cz))

    def column(x, _):
        beyond = src_strip[x]
        for y in range(HALO - reach, HALO + cy + reach):
            here = src[x, y]
            ends = pltpu.roll(beyond, (2 * cz - (y * STRIP + HALO)) % cz, 1)
            above = jnp.where(last, ends, pltpu.roll(here, cz - 1, 1))
            below = jnp.where(first, ends, pltpu.roll(here, 1, 1))
            total = r[x, y] - here
            total += spread(c, 0, x, y) * src[x + 1, y]
            total += spread(c, 1, x, y) * src[x - 1, y]
            total += spread(c, 2, x, y) * src[x, y + 1]
            total += spread(c, 3, x, y) * src[x, y - 1]
            total += spread(c, 4, x, y) * above
            total += spread(c, 5, x, y) * below
            dst[x, y] = here + weight * total
        return _

    lax.fori_loop(HALO - reach, HALO + cx + reach, column, 0)
    if reach == 0:
        return

    k = lane % STRIP
    group = lane // STRIP
    touching = (k == HALO) | (k == HALO - 1)

    def strip_column(x, _):
        here = src_strip[x]
        ends = jnp.zeros_like(here)
        for y in range(HALO - reach + 1, HALO + cy + reach - 1):
            moved = pltpu.roll(src[x, y], (y * STRIP + HALO) % cz, 1)
            ends = jnp.where(touching & (group == y), moved, ends)

        def spread_strip(k):
            return jnp.broadcast_to(c_strip[k, pl.ds(x, 1), :], (ch, cz))

        above = jnp.where(k == HALO, ends, pltpu.roll(here, 1, 1))
        below = jnp.where(k == HALO - 1, ends, pltpu.roll(here, cz - 1, 1))
        total = r_strip[x] - here
        total += spread_strip(0) * src_strip[x + 1]
        total += spread_strip(1) * src_strip[x - 1]
        total += spread_strip(2) * pltpu.roll(here, cz - STRIP, 1)
        total += spread_strip(3) * pltpu.roll(here, STRIP, 1)
        total += spread_strip(4) * above
        total += spread_strip(5) * below
        dst_strip[x] = here + weight * total
        return _

    lax.fori_loop(HALO - reach + 1, HALO + cx + reach - 1, strip_column, 0)


def coefficients(dims, kc, kc_strip, c, c_strip):
    cx, cy, cz, ch, nodes = dims
    tx, ty = cx + 2 * HALO, cy + 2 * HALO
    lane = iota((ty, cz), 1)
    y = iota((ty, cz), 0)
    here = kc_strip[8:8 + tx, :]
    group = lane // STRIP
    k = lane % STRIP
    touching = ((k == HALO) | (k == HALO - 1)) & (group == y)
    ends = []
    for x in range(tx):
        own = kc[x + 1, 8:8 + ty, :]
        moved = pltpu.roll(own, HALO, 1, stride=STRIP, stride_axis=0)
        ends.append(jnp.sum(jnp.where(touching, moved, 0.0), axis=0, keepdims=True))
        beyond = jnp.broadcast_to(kc_strip[8 + x:9 + x, :], (ty, cz))
        upper = jnp.where((group == y) & (k == HALO - 1), beyond, 0.0).sum(axis=1, keepdims=True)
        lower = jnp.where((group == y) & (k == HALO), beyond, 0.0).sum(axis=1, keepdims=True)
        others = [
            kc[x + 2, 8:8 + ty, :],
            kc[x, 8:8 + ty, :],
            kc[x + 1, 9:9 + ty, :],
            kc[x + 1, 7:7 + ty, :],
            jnp.where(lane == cz - 1, upper, pltpu.roll(own, cz - 1, 1)),
            jnp.where(lane == 0, lower, pltpu.roll(own, 1, 1)),
        ]
        finish(own, others, [c.at[i, x] for i in range(7)])
    ends = jnp.concatenate(ends, axis=0)
    lane = iota((tx, cz), 1)
    k = lane % STRIP
    others = [
        kc_strip[9:9 + tx, :],
        kc_strip[7:7 + tx, :],
        pltpu.roll(here, cz - STRIP, 1),
        pltpu.roll(here, STRIP, 1),
        jnp.where(k == HALO, ends, pltpu.roll(here, 1, 1)),
        jnp.where(k == HALO - 1, ends, pltpu.roll(here, cz - 1, 1)),
    ]
    finish(here, others, [c_strip.at[i] for i in range(7)])


def finish(own, others, outs):
    faces = [0.5 * (own + other) for other in others]
    diag = MASS_TERM + faces[0]
    for face in faces[1:]:
        diag = diag + face
    inverse = jnp.where(own > 0.0, 1.0 / diag, 0.0)
    for face, out in zip(faces, outs[:6], strict=True):
        out[...] = face * inverse
    outs[6][...] = inverse


def smooth(dims, start, fields, strips, r, r_strip, c, c_strip):
    weights = sweep_weights(SWEEPS)
    now = 0
    for number in range(start, SWEEPS):
        sweep(
            dims, SWEEPS - 1 - number, weights[number], fields[now], strips[now],
            fields[1 - now], strips[1 - now], r, r_strip, c, c_strip,
        )
        now = 1 - now
    return fields[now]


def gather_nodes(dims, field, row, z):
    cx, cy, cz, ch, nodes = dims
    hits = (iota((cz, nodes), 0) == z).astype(BF16)
    rows = field[HALO:HALO + cx, HALO:HALO + cy].reshape(cx * cy * ch, cz).astype(BF16)
    at_z = jnp.dot(rows, hits, preferred_element_type=F32)
    total = jnp.zeros((ch, nodes), F32)
    for r in range(cx * cy):
        here = jnp.broadcast_to(row == r, (ch, nodes))
        total = jnp.where(here, at_z[r * ch:(r + 1) * ch], total)
    return total.astype(BF16)


def fourth_kernel(dims, nx, ny, place, region_coeff, main, labels, cells, pos, strip, *refs):
    cx, cy, cz, ch, nodes = dims
    xrecv, yrecv, refs = refs[:nx], refs[nx:nx + ny], refs[nx + ny:]
    field_out, block_out, send_out, r, r_strip, c, c_strip, refs = *refs[:7], refs[7:]
    fa, fb, sa, sb, kc, kc_strip, codes, strip_codes, side_codes = refs
    even_x = 1 - place[0] % 2
    even_y = 1 - place[1] % 2
    tx, ty = cx + 2 * HALO, cy + 2 * HALO
    width = RHS_HALO
    ex = cx + 2 * width

    fill_codes(
        dims, labels, strip, xrecv, width * cy * ch + width * ch, even_x, codes, strip_codes
    )
    kc[...] = jnp.zeros_like(kc)
    kc_strip[...] = jnp.zeros_like(kc_strip)

    def conductivity(code):
        value = jnp.zeros_like(code)
        for region in range(region_coeff.shape[0]):
            value = jnp.where(code == region + 1, region_coeff[region], value)
        return value

    kc[1:1 + tx, 8 + HALO:8 + HALO + cy] = conductivity(codes[...]).reshape(tx, cy, cz)
    start = ex * width * ch + ex * ch
    for low in (True, False):
        got = pick(yrecv, low, even_y, start, tx * HALO).astype(F32)
        side_codes[...] = conductivity(got)
        y0 = 8 if low else 8 + HALO + cy
        for x in range(tx):
            kc[1 + x, y0:y0 + HALO, :] = side_codes[x * HALO:(x + 1) * HALO, :]
    start += tx * HALO
    low = pick(yrecv, True, even_y, start, 16).astype(F32)
    high = pick(yrecv, False, even_y, start, 16).astype(F32)
    kc_strip[8:8 + tx, :] = conductivity(join_strips(strip_codes[...], low, high, cy))
    coefficients(dims, kc, kc_strip, c, c_strip)

    r[...] = jnp.zeros_like(r)
    r_strip[...] = jnp.zeros_like(r_strip)
    assemble(dims, width, main, strip, xrecv, yrecv, even_x, even_y, r, r_strip)
    weight = sweep_weights(SWEEPS)[0]

    def column(x, _):
        for y in range(HALO - width, HALO + cy + width):
            value = r[x, y] * jnp.broadcast_to(c[6, x, y:y + 1, :], (ch, cz))
            r[x, y] = value
            fa[x, y] = weight * value
        value = r_strip[x] * jnp.broadcast_to(c_strip[6, pl.ds(x, 1), :], (ch, cz))
        r_strip[x] = value
        sa[x] = weight * value
        return _

    lax.fori_loop(HALO - width, HALO + cx + width, column, 0)
    field = smooth(dims, 1, (fa, fb), (sa, sb), r, r_strip, c, c_strip)

    field_out[...] = field[HALO:HALO + cx, HALO:HALO + cy].reshape(cx * cy * ch, cz)
    send_out[...] = strip_rows(lambda x, y: field[HALO + x, HALO + y], cx, cy, cz)
    cell = cells[...]
    row, z = cell // cz, cell % cz
    block_out[:ch, :] = gather_nodes(dims, field, row, z)
    rows = []
    for axis in range(3):
        value = pos[axis:axis + 1, :]
        for _ in range(3):
            part = value.astype(BF16).astype(F32)
            rows.append(part)
            value = value - part
    rows += [row.astype(F32), z.astype(F32), jnp.zeros((5, nodes), F32)]
    block_out[ch:, :] = jnp.concatenate(rows, axis=0).astype(BF16)


def boundary_kernel(dims, count, scale, pos, recv, kernel_out, sum_out, half_out):
    cx, cy, cz, ch, nodes = dims
    own = [jnp.broadcast_to(pos[k:k + 1, :], (nodes, nodes)).T for k in range(3)]

    def block(b, total):
        parts = recv[b, ch:ch + 16, :].astype(F32)
        squared = None
        for k in range(3):
            other = parts[3 * k:3 * k + 1] + parts[3 * k + 1:3 * k + 2] + parts[3 * k + 2:3 * k + 3]
            delta = own[k] - jnp.broadcast_to(other, (nodes, nodes))
            squared = delta * delta if squared is None else squared + delta * delta
        tile = (scale * lax.rsqrt(squared + SOFTENING * SOFTENING)).astype(BF16)
        kernel_out[b] = tile
        return total + lax.dot_general(recv[b, :ch, :], tile, NT, preferred_element_type=F32)

    total = lax.fori_loop(0, count, block, jnp.zeros((ch, nodes), F32))
    sum_out[...] = total
    half_out[...] = total.astype(BF16)


def last_kernel(dims, count, incident, recv, tiles, flux_out):
    cx, cy, cz, ch, nodes = dims

    def block(b, total):
        return total + lax.dot_general(recv[b], tiles[b], NT, preferred_element_type=F32)

    flux_out[...] = incident[...] + lax.fori_loop(0, count, block, jnp.zeros((ch, nodes), F32))


def fifth_kernel(dims, sizes, nx, ny, place, main, sums, cells, recv, blocks, strip, *refs):
    cx, cy, cz, ch, nodes = dims
    xrecv, yrecv, refs = refs[:nx], refs[nx:nx + ny], refs[nx + ny:]
    r_in, rs_in, c, c_strip, refs = *refs[:4], refs[4:]
    field_out, block_out, refs = *refs[:2], refs[2:]
    r, r_strip, fa, fb, sa, sb, left = refs
    even_x = 1 - place[0] % 2
    even_y = 1 - place[1] % 2
    width = RHS_HALO
    r[...] = r_in[...]
    r_strip[...] = rs_in[...]
    fa[...] = jnp.zeros_like(fa)
    sa[...] = jnp.zeros_like(sa)
    assemble(dims, HALO, main, strip, xrecv, yrecv, even_x, even_y, fa, sa)

    def neighbour(dx, dy, dz):
        at = [place[i] + d for i, d in enumerate((dx, dy, dz))]
        good = None
        for i, size in enumerate(sizes):
            ok = (at[i] >= 0) & (at[i] < size)
            good = ok if good is None else good & ok
            at[i] = jnp.clip(at[i], 0, size - 1)
        index = (at[0] * sizes[1] + at[1]) * sizes[2] + at[2]
        info = blocks[index, ch:ch + 16, :].astype(F32)
        good = jnp.full((1, nodes), good.astype(jnp.int32), jnp.int32) > 0
        row = jnp.where(good, info[9:10].astype(jnp.int32), -1)
        return recv[index].astype(F32), row, info[10:11].astype(jnp.int32)

    spans = {
        -1: (HALO - width, HALO, cx), 0: (HALO, HALO + cx, 0), 1: (HALO + cx, HALO + cx + width, -cx),
    }
    cell = cells[...]
    own_row, own_z = cell // cz, cell % cz
    strip_lane = iota((cz, nodes), 0)
    for dx in (-1, 0, 1):
        x0, x1, back_x = spans[dx]
        edge = []
        hits_edge = []
        for dy in (-1, 0, 1):
            y0, y1, back_y = spans[dy]
            parts = []
            if dx == 0 and dy == 0:
                top = sums[...].astype(BF16).astype(F32)
                row, z = own_row, own_z
                parts = [top, sums[...] - top]
            else:
                value, row, z = neighbour(dx, dy, 0)
                parts = [value]
            hits = (iota((cz, nodes), 0) == z).astype(BF16)
            hits = jnp.concatenate([hits] * len(parts), axis=1)
            count = (x1 - x0) * (y1 - y0)
            at = 0
            for x in range(x0, x1):
                for y in range(y0, y1):
                    wanted = (x - HALO + back_x) * cy + (y - HALO + back_y)
                    here = jnp.broadcast_to(row == wanted, (ch, nodes))
                    for i, value in enumerate(parts):
                        left[at:at + ch, i * nodes:(i + 1) * nodes] = jnp.where(
                            here, value, 0.0
                        ).astype(BF16)
                    at += ch
            added = lax.dot_general(
                left[:at, :len(parts) * nodes], hits, NT, preferred_element_type=F32
            )
            at = 0
            for x in range(x0, x1):
                for y in range(y0, y1):
                    inverse = jnp.broadcast_to(c[6, x, y:y + 1, :], (ch, cz))
                    r[x, y] += added[at:at + ch] * inverse
                    at += ch
            for dz in (-1, 1):
                value, row, z = neighbour(dx, dy, dz)
                y = row % cy + cy * dy + HALO
                k = HALO - 1 - z if dz > 0 else HALO + cz - 1 - z
                good = (row >= 0) & (y >= 0) & (y < cy + 2 * HALO) & (k >= 0) & (k < STRIP)
                good = good & ((k < HALO) if dz > 0 else (k >= HALO))
                lane = jnp.where(good, y * STRIP + k, -1)
                hits_edge.append((strip_lane == lane).astype(BF16))
                edge.append((value, jnp.where(row >= 0, row // cy, -1)))
        for x in range(x0, x1):
            at = (x - x0) * ch
            for i, (value, node_x) in enumerate(edge):
                here = jnp.broadcast_to(node_x == x - HALO + back_x, (ch, nodes))
                left[at:at + ch, i * nodes:(i + 1) * nodes] = jnp.where(here, value, 0.0).astype(BF16)
        added = lax.dot_general(
            left[:(x1 - x0) * ch, :len(edge) * nodes], jnp.concatenate(hits_edge, axis=1), NT,
            preferred_element_type=F32,
        )
        for x in range(x0, x1):
            inverse = jnp.broadcast_to(c_strip[6, x:x + 1, :], (ch, cz))
            r_strip[x] += added[(x - x0) * ch:(x - x0 + 1) * ch] * inverse

    field = smooth(dims, 0, (fa, fb), (sa, sb), r, r_strip, c, c_strip)
    for x in range(cx):
        for y in range(cy):
            field_out[pl.ds(x * cy + y, ch, stride=cx * cy), :] = field[HALO + x, HALO + y]
    block_out[...] = gather_nodes(dims, field, own_row, own_z)


def per_device(source, labels, region_coeff, node_cell, node_pos, incident):
    ch, cx, cy, cz = source.shape
    nodes = node_cell.shape[0]
    dims = (cx, cy, cz, ch, nodes)
    sizes = tuple(lax.axis_size(axis) for axis in AXES)
    count = math.prod(sizes)
    nx, ny, nz = (2 if size > 2 else 1 for size in sizes)
    scale = KERNEL_GAIN / math.sqrt(nodes * count)
    tx, ty = cx + 2 * HALO, cy + 2 * HALO
    place = jnp.stack([lax.axis_index(axis) for axis in AXES]).astype(jnp.int32)
    rows = cx * cy * ch
    flat = source.reshape(ch * cx * cy, cz)
    marks = labels.reshape(cx * cy, cz)
    cells = node_cell.reshape(1, nodes)
    shape = jax.ShapeDtypeStruct
    vmem = pltpu.VMEM

    rhs, send = kernel_call(
        functools.partial(first_kernel, dims),
        (shape((rows, cz), F32), shape((cx * ch + 16, cz), BF16)),
        [vmem((rows, 2 * nodes), BF16)],
        operands=(flat, marks, incident, cells),
        name="scatter_first",
    )

    def halo(main, send, width, with_labels, between=(lambda x: x, lambda x: x)):
        zrecv = exchange(send, "col")
        zrecv = between[0](zrecv)
        extra = HALO * cy + 16 if with_labels else 0
        strip_rows_ = cx * ch + (16 if with_labels else 0)
        own = (main, marks) if with_labels else (main,)
        strip, *sends = kernel_call(
            functools.partial(second_kernel, dims, width, with_labels, nz, nx),
            (shape((strip_rows_, cz), BF16),)
            + (shape((width * cy * ch + width * ch + extra, cz), BF16),) * nx,
            [vmem((32, cz), F32)] if with_labels else [],
            smem=1,
            operands=(place, *own, *zrecv),
            name="pack_x",
        )
        xrecv = exchange(None, "vol", sends)
        xrecv = between[1](xrecv)
        ex = cx + 2 * width
        extra = tx * HALO + 16 if with_labels else 0
        sends = kernel_call(
            functools.partial(third_kernel, dims, width, with_labels, nx, ny),
            (shape((ex * width * ch + ex * ch + extra, cz), BF16),) * ny,
            [vmem((tx * cy, cz), F32), vmem((tx, cz), F32), vmem((tx * HALO, cz), F32)]
            if with_labels else [],
            smem=1,
            operands=(place, *own, strip, *xrecv),
            name="pack_y",
        )
        yrecv = exchange(None, "row", sends)
        return strip, xrecv, yrecv

    strip, xrecv, yrecv = halo(rhs, send, RHS_HALO, True)
    field, block, send, r, r_strip, c, c_strip = kernel_call(
        functools.partial(fourth_kernel, dims, nx, ny),
        (
            shape((rows, cz), F32),
            shape((ch + 16, nodes), BF16),
            shape((cx * ch, cz), BF16),
            shape((tx, ty, ch, cz), F32),
            shape((tx, ch, cz), F32),
            shape((7, tx, ty, cz), F32),
            shape((7, tx, cz), F32),
        ),
        [
            vmem((tx, ty, ch, cz), F32),
            vmem((tx, ty, ch, cz), F32),
            vmem((tx, ch, cz), F32),
            vmem((tx, ch, cz), F32),
            vmem((tx + 2, ty + 16, cz), F32),
            vmem((tx + 16, cz), F32),
            vmem((tx * cy, cz), F32),
            vmem((tx, cz), F32),
            vmem((tx * HALO, cz), F32),
        ],
        smem=2,
        operands=(place, region_coeff, rhs, marks, cells, node_pos, strip, *xrecv, *yrecv),
        name="sweeps_first",
    )

    def to_all(value):
        spread = jnp.broadcast_to(value[None], (count,) + value.shape)
        return lax.all_to_all(spread, AXES, 0, 0, tiled=True)

    blocks = to_all(block)
    tiles, sums, half = kernel_call(
        functools.partial(boundary_kernel, dims, count, scale),
        (
            shape((count, nodes, nodes), BF16),
            shape((ch, nodes), F32),
            shape((ch, nodes), BF16),
        ),
        operands=(node_pos, blocks),
        name="boundary",
    )
    recv = to_all(half)
    strip, xrecv, yrecv = halo(field, send, HALO, False)
    field, block = kernel_call(
        functools.partial(fifth_kernel, dims, sizes, nx, ny),
        (shape((ch * cx * cy, cz), F32), shape((ch, nodes), BF16)),
        [
            vmem((tx, ty, ch, cz), F32),
            vmem((tx, ch, cz), F32),
            vmem((tx, ty, ch, cz), F32),
            vmem((tx, ty, ch, cz), F32),
            vmem((tx, ch, cz), F32),
            vmem((tx, ch, cz), F32),
            vmem((rows, 6 * nodes), BF16),
        ],
        smem=1,
        operands=(
            place, field, sums, cells, recv, blocks, strip, *xrecv, *yrecv, r, r_strip, c, c_strip
        ),
        name="sweeps_last",
    )
    flux = kernel_call(
        functools.partial(last_kernel, dims, count),
        shape((ch, nodes), F32),
        operands=(incident, to_all(block), tiles),
        name="flux_last",
    )
    return field.reshape(source.shape), flux


def solution(mesh):
    placed = (
        P(None, "vol", "row", "col"),
        P("vol", "row", "col"),
        P(),
        P(("vol", "row", "col")),
        P(None, ("vol", "row", "col")),
        P(None, ("vol", "row", "col")),
    )
    return jax.shard_map(
        per_device,
        mesh=mesh,
        in_specs=placed,
        out_specs=(P(None, "vol", "row", "col"), P(None, ("vol", "row", "col"))),
        check_vma=False,
    )
```

```python
import functools
import math

import jax
import jax.numpy as jnp
from jax import lax
from jax.experimental import pallas as pl
from jax.experimental.pallas import tpu as pltpu
from jax.sharding import PartitionSpec as P

SWEEPS = 4
ITERS = 2

MASS_TERM = 0.05
SOFTENING = 0.05
KERNEL_GAIN = 2.0

HALO = SWEEPS
RHS_HALO = SWEEPS - 1
STRIP = 2 * HALO
AXES = ("vol", "row", "col")
F32, BF16 = jnp.float32, jnp.bfloat16
ROW, LAYER, REGION, INCIDENT = 3, 4, 5, 8
SPARE = 4 * 1024 * 1024
NT = (((1,), (1,)), ((), ()))


def sweep_weights(count):
    return [
        1.0 / (1.05 - 0.95 * math.cos(math.pi * (2 * sweep + 1) / (2 * count)))
        for sweep in range(count)
    ]


def iota(shape, dim):
    return lax.broadcasted_iota(jnp.int32, shape, dim)


def kernel_call(body, out_shape, scratch=(), smem=0, operands=(), name=None):
    held = [jnp.shape(leaf) + (leaf.dtype,) for leaf in jax.tree.leaves((out_shape, operands))]
    held += [ref.shape + (ref.dtype,) for ref in scratch]
    need = sum(math.prod(entry[:-1]) * jnp.dtype(entry[-1]).itemsize for entry in held)
    specs = [pl.BlockSpec(memory_space=pltpu.SMEM)] * smem
    specs += [pl.BlockSpec(memory_space=pltpu.VMEM)] * (len(operands) - smem)
    return pl.pallas_call(
        body,
        out_shape=out_shape,
        in_specs=specs,
        out_specs=jax.tree.map(lambda _: pl.BlockSpec(memory_space=pltpu.VMEM), out_shape),
        scratch_shapes=list(scratch),
        compiler_params=pltpu.CompilerParams(vmem_limit_bytes=need + SPARE),
        name=name,
    )(*operands)


def pick(refs, low, even, rows, size):
    first = refs[0][pl.ds(rows, size), :]
    second = refs[1][pl.ds(rows, size), :] if len(refs) > 1 else jnp.zeros_like(first)
    flag = jnp.full(first.shape, even, jnp.int32).astype(first.dtype)
    mine, other = (1 - flag, flag) if low else (flag, 1 - flag)
    return first * mine + second * other


def exchange(array, axis, arrays=None):
    count = lax.axis_size(axis)
    arrays = arrays or [array] * 2
    out = []
    for which in range(2 if count > 2 else 1):
        pairs = []
        for i in range(which, count - 1, 2):
            pairs += [(i, i + 1), (i + 1, i)]
        out.append(lax.ppermute(arrays[which], axis, pairs))
    return out


def edge_picker(cz, lanes):
    z, lane = iota((cz, lanes), 0), iota((cz, lanes), 1)
    k = lane % STRIP
    wanted = jnp.where(k < HALO, HALO - 1 - k, cz - 1 - k + HALO)
    return (z == wanted).astype(F32), lane // STRIP - HALO


def strip_rows(read, cx, cy, cz):
    base, lane_y = edge_picker(cz, cz)
    total = None
    for y in range(cy):
        rows = jnp.concatenate([read(x, y).astype(BF16) for x in range(cx)], axis=0)
        picked = jnp.where(lane_y == y, base, 0.0).astype(BF16)
        part = jnp.dot(rows, picked, preferred_element_type=F32)
        total = part if total is None else total + part
    return total.astype(BF16)


def node_places(small):
    return (small[at:at + 1, :].astype(jnp.int32) for at in (ROW, LAYER))


def first_kernel(dims, source, small, rhs_out, send_out, left):
    cx, cy, cz, ch, nodes = dims
    row, z = node_places(small)
    hits = (iota((cz, nodes), 0) == z).astype(BF16)
    flux = small[INCIDENT:INCIDENT + ch, :]
    top = flux.astype(BF16).astype(F32)
    rest = flux - top
    for r in range(cx * cy):
        here = jnp.broadcast_to(row == r, (ch, nodes))
        left[r * ch:(r + 1) * ch, :nodes] = jnp.where(here, top, 0.0).astype(BF16)
        left[r * ch:(r + 1) * ch, nodes:] = jnp.where(here, rest, 0.0).astype(BF16)
    added = lax.dot_general(
        left[...], jnp.concatenate([hits, hits], axis=1), NT, preferred_element_type=F32
    )
    rhs_out[...] = added
    for r in range(cx * cy):
        rhs_out[r * ch:(r + 1) * ch, :] += source[pl.ds(r, ch, stride=cx * cy), :]

    def read(x, y):
        start = (x * cy + y) * ch
        return rhs_out[start:start + ch, :]

    send_out[:cx * ch, :] = strip_rows(read, cx, cy, cz)
    base, lane_y = edge_picker(cz, cz)
    codes = small[INCIDENT + ch:, :].astype(BF16)
    strips = jnp.dot(codes, base.astype(BF16), preferred_element_type=F32)
    own = (iota(strips.shape, 0) % cy) == lane_y[:1, :]
    strips = jnp.where(own, strips, 0.0).reshape(cx, cy, cz).sum(axis=1)
    send_out[cx * ch:, :] = jnp.concatenate(
        [strips, jnp.zeros((16 - cx, cz), F32)], axis=0
    ).astype(BF16)


def second_kernel(dims, width, with_labels, nz, nx, place, *refs):
    cx, cy, cz, ch, nodes = dims
    main, refs = refs[0], refs[1:]
    if with_labels:
        small, refs = refs[0], refs[1:]
    zrecv, refs = refs[:nz], refs[nz:]
    strip_out, sends, refs = refs[0], refs[1:1 + nx], refs[1 + nx:]
    even_x = 1 - place[0] % 2
    even_z = 1 - place[2] % 2
    rows = cx * ch + (16 if with_labels else 0)
    lane = iota((rows, cz), 1)
    upper = pick(zrecv, False, even_z, 0, rows)
    lower = pick(zrecv, True, even_z, 0, rows)
    strip_out[...] = jnp.where(
        lane % STRIP < HALO, upper.astype(F32), lower.astype(F32)
    ).astype(BF16)
    if with_labels:
        (codes,) = refs
        codes[...] = jnp.zeros_like(codes)
        codes[:16, :] = strip_out[cx * ch:, :].astype(F32)
    slab = width * cy * ch
    for which in range(nx):
        upward = even_x if which == 0 else 1 - even_x
        x0 = upward * (cx - width)
        send = sends[which]
        send[:slab, :] = main[pl.ds(pl.multiple_of(x0 * (cy * ch), 16), slab), :].astype(BF16)
        send[slab:slab + width * ch, :] = strip_out[
            pl.ds(pl.multiple_of(x0 * ch, 16), width * ch), :
        ]
        if with_labels:
            start = slab + width * ch
            x0 = upward * (cx - HALO)
            send[start:start + HALO * cy, :] = (
                small[pl.ds(pl.multiple_of(INCIDENT + ch + x0 * cy, 8), HALO * cy), :]
            ).astype(BF16)
            send[start + HALO * cy:, :] = codes[pl.ds(x0, 16), :].astype(BF16)


def third_kernel(dims, width, with_labels, nx, ny, place, *refs):
    cx, cy, cz, ch, nodes = dims
    main, refs = refs[0], refs[1:]
    if with_labels:
        small, refs = refs[0], refs[1:]
    strip, refs = refs[0], refs[1:]
    xrecv, refs = refs[:nx], refs[nx:]
    sends, refs = refs[:ny], refs[ny:]
    even_x = 1 - place[0] % 2
    even_y = 1 - place[1] % 2
    ex = cx + 2 * width
    slab = width * cy * ch
    if with_labels:
        codes, strip_codes, picked = refs
        fill_codes(dims, small, strip, xrecv, slab + width * ch, even_x, codes, strip_codes)
    for which in range(ny):
        send = sends[which]
        upward = even_y if which == 0 else 1 - even_y
        y0 = upward * (cy - width)
        size = width * ch
        for x in range(ex):
            if width <= x < width + cx:
                start = pl.multiple_of(((x - width) * cy + y0) * ch, 16)
                piece = main[pl.ds(start, size), :].astype(BF16)
            else:
                low = x < width
                start = pl.multiple_of(((x if low else x - width - cx) * cy + y0) * ch, 16)
                piece = pick(xrecv, low, even_x, start, size)
            send[x * size:(x + 1) * size, :] = piece
        start = ex * size
        send[start:start + width * ch, :] = pick(xrecv, True, even_x, slab, width * ch)
        send[start + width * ch:start + (width + cx) * ch, :] = strip[:cx * ch, :]
        send[start + (width + cx) * ch:start + ex * ch, :] = pick(
            xrecv, False, even_x, slab, width * ch
        )
        if with_labels:
            start += ex * ch
            y0 = upward * (cy - HALO)
            tall = cx + 2 * HALO
            for x in range(tall):
                picked[x * HALO:(x + 1) * HALO, :] = codes[pl.ds(x * cy + y0, HALO), :]
            send[start:start + tall * HALO, :] = picked[...].astype(BF16)
            send[start + tall * HALO:, :] = strip_codes[...].astype(BF16)


def fill_codes(dims, small, strip, xrecv, start, even_x, codes, strip_codes):
    cx, cy, cz, ch, nodes = dims
    side = HALO * cy
    codes[:side, :] = pick(xrecv, True, even_x, start, side).astype(F32)
    codes[side:side + cx * cy, :] = small[INCIDENT + ch:, :]
    codes[side + cx * cy:, :] = pick(xrecv, False, even_x, start, side).astype(F32)
    strip_codes[:HALO, :] = pick(xrecv, True, even_x, start + side, 16).astype(F32)[:HALO]
    strip_codes[HALO:HALO + cx, :] = strip[cx * ch:cx * ch + 16, :].astype(F32)[:cx]
    strip_codes[HALO + cx:, :] = pick(xrecv, False, even_x, start + side, 16).astype(F32)[:HALO]


def assemble(dims, width, main, strip, xrecv, yrecv, even_x, even_y, out, out_strip):
    cx, cy, cz, ch, nodes = dims
    ex = cx + 2 * width
    out[HALO:HALO + cx, HALO:HALO + cy] = main[...].reshape(cx, cy, ch, cz)
    slab = width * cy * ch
    low = pick(xrecv, True, even_x, 0, slab).astype(F32)
    out[HALO - width:HALO, HALO:HALO + cy] = low.reshape(width, cy, ch, cz)
    high = pick(xrecv, False, even_x, 0, slab).astype(F32)
    out[HALO + cx:HALO + cx + width, HALO:HALO + cy] = high.reshape(width, cy, ch, cz)
    size = ex * width * ch
    low = pick(yrecv, True, even_y, 0, size).astype(F32)
    out[HALO - width:HALO + cx + width, HALO - width:HALO] = low.reshape(ex, width, ch, cz)
    high = pick(yrecv, False, even_y, 0, size).astype(F32)
    out[HALO - width:HALO + cx + width, HALO + cy:HALO + cy + width] = high.reshape(
        ex, width, ch, cz
    )
    own = jnp.concatenate(
        [
            pick(xrecv, True, even_x, slab, width * ch),
            strip[:cx * ch, :],
            pick(xrecv, False, even_x, slab, width * ch),
        ],
        axis=0,
    ).astype(F32)
    low = pick(yrecv, True, even_y, size, ex * ch).astype(F32)
    high = pick(yrecv, False, even_y, size, ex * ch).astype(F32)
    full = join_strips(own, low, high, cy)
    out_strip[HALO - width:HALO + cx + width] = full.reshape(ex, ch, cz)


def join_strips(own, low, high, cy):
    lane = iota(own.shape, 1)
    shift = cy * STRIP
    lanes = own.shape[1]
    low = pltpu.roll(low, lanes - shift, 1)
    high = pltpu.roll(high, shift, 1)
    return jnp.where(
        lane < HALO * STRIP, low, jnp.where(lane < (HALO + cy) * STRIP, own, high)
    )


def sweep(dims, reach, weight, src, src_strip, dst, dst_strip, r, r_strip, c, c_strip):
    cx, cy, cz, ch, nodes = dims
    lane = iota((ch, cz), 1)
    first, last = lane == 0, lane == cz - 1

    def spread(ref, k, x, y):
        return jnp.broadcast_to(ref[k, x, y:y + 1, :], (ch, cz))

    def column(x, _):
        beyond = src_strip[x]
        for y in range(HALO - reach, HALO + cy + reach):
            here = src[x, y]
            ends = pltpu.roll(beyond, (2 * cz - (y * STRIP + HALO)) % cz, 1)
            above = jnp.where(last, ends, pltpu.roll(here, cz - 1, 1))
            below = jnp.where(first, ends, pltpu.roll(here, 1, 1))
            total = r[x, y] - here
            total += spread(c, 0, x, y) * src[x + 1, y]
            total += spread(c, 1, x, y) * src[x - 1, y]
            total += spread(c, 2, x, y) * src[x, y + 1]
            total += spread(c, 3, x, y) * src[x, y - 1]
            total += spread(c, 4, x, y) * above
            total += spread(c, 5, x, y) * below
            dst[x, y] = here + weight * total
        return _

    lax.fori_loop(HALO - reach, HALO + cx + reach, column, 0)
    if reach == 0:
        return

    k = lane % STRIP
    group = lane // STRIP
    touching = (k == HALO) | (k == HALO - 1)

    def strip_column(x, _):
        here = src_strip[x]
        ends = jnp.zeros_like(here)
        for y in range(HALO - reach + 1, HALO + cy + reach - 1):
            moved = pltpu.roll(src[x, y], (y * STRIP + HALO) % cz, 1)
            ends = jnp.where(touching & (group == y), moved, ends)

        def spread_strip(k):
            return jnp.broadcast_to(c_strip[k, pl.ds(x, 1), :], (ch, cz))

        above = jnp.where(k == HALO, ends, pltpu.roll(here, 1, 1))
        below = jnp.where(k == HALO - 1, ends, pltpu.roll(here, cz - 1, 1))
        total = r_strip[x] - here
        total += spread_strip(0) * src_strip[x + 1]
        total += spread_strip(1) * src_strip[x - 1]
        total += spread_strip(2) * pltpu.roll(here, cz - STRIP, 1)
        total += spread_strip(3) * pltpu.roll(here, STRIP, 1)
        total += spread_strip(4) * above
        total += spread_strip(5) * below
        dst_strip[x] = here + weight * total
        return _

    lax.fori_loop(HALO - reach + 1, HALO + cx + reach - 1, strip_column, 0)


def coefficients(dims, kc, kc_strip, c, c_strip):
    cx, cy, cz, ch, nodes = dims
    tx, ty = cx + 2 * HALO, cy + 2 * HALO
    lane = iota((ty, cz), 1)
    y = iota((ty, cz), 0)
    here = kc_strip[8:8 + tx, :]
    group = lane // STRIP
    k = lane % STRIP
    touching = ((k == HALO) | (k == HALO - 1)) & (group == y)
    ends = []
    for x in range(tx):
        own = kc[x + 1, 8:8 + ty, :]
        moved = pltpu.roll(own, HALO, 1, stride=STRIP, stride_axis=0)
        ends.append(jnp.sum(jnp.where(touching, moved, 0.0), axis=0, keepdims=True))
        beyond = jnp.broadcast_to(kc_strip[8 + x:9 + x, :], (ty, cz))
        upper = jnp.where((group == y) & (k == HALO - 1), beyond, 0.0).sum(axis=1, keepdims=True)
        lower = jnp.where((group == y) & (k == HALO), beyond, 0.0).sum(axis=1, keepdims=True)
        others = [
            kc[x + 2, 8:8 + ty, :],
            kc[x, 8:8 + ty, :],
            kc[x + 1, 9:9 + ty, :],
            kc[x + 1, 7:7 + ty, :],
            jnp.where(lane == cz - 1, upper, pltpu.roll(own, cz - 1, 1)),
            jnp.where(lane == 0, lower, pltpu.roll(own, 1, 1)),
        ]
        finish(own, others, [c.at[i, x] for i in range(7)])
    ends = jnp.concatenate(ends, axis=0)
    lane = iota((tx, cz), 1)
    k = lane % STRIP
    others = [
        kc_strip[9:9 + tx, :],
        kc_strip[7:7 + tx, :],
        pltpu.roll(here, cz - STRIP, 1),
        pltpu.roll(here, STRIP, 1),
        jnp.where(k == HALO, ends, pltpu.roll(here, 1, 1)),
        jnp.where(k == HALO - 1, ends, pltpu.roll(here, cz - 1, 1)),
    ]
    finish(here, others, [c_strip.at[i] for i in range(7)])


def finish(own, others, outs):
    faces = [0.5 * (own + other) for other in others]
    diag = MASS_TERM + faces[0]
    for face in faces[1:]:
        diag = diag + face
    inverse = jnp.where(own > 0.0, 1.0 / diag, 0.0)
    for face, out in zip(faces, outs[:6], strict=True):
        out[...] = face * inverse
    outs[6][...] = inverse


def smooth(dims, start, fields, strips, r, r_strip, c, c_strip):
    weights = sweep_weights(SWEEPS)
    now = 0
    for number in range(start, SWEEPS):
        sweep(
            dims, SWEEPS - 1 - number, weights[number], fields[now], strips[now],
            fields[1 - now], strips[1 - now], r, r_strip, c, c_strip,
        )
        now = 1 - now
    return fields[now]


def gather_nodes(dims, field, row, z):
    cx, cy, cz, ch, nodes = dims
    hits = (iota((cz, nodes), 0) == z).astype(BF16)
    rows = field[HALO:HALO + cx, HALO:HALO + cy].reshape(cx * cy * ch, cz).astype(BF16)
    at_z = jnp.dot(rows, hits, preferred_element_type=F32)
    total = jnp.zeros((ch, nodes), F32)
    for r in range(cx * cy):
        here = jnp.broadcast_to(row == r, (ch, nodes))
        total = jnp.where(here, at_z[r * ch:(r + 1) * ch], total)
    return total.astype(BF16)


def fourth_kernel(dims, regions, nx, ny, place, main, small, strip, *refs):
    cx, cy, cz, ch, nodes = dims
    xrecv, yrecv, refs = refs[:nx], refs[nx:nx + ny], refs[nx + ny:]
    field_out, block_out, send_out, r, r_strip, c, c_strip, refs = *refs[:7], refs[7:]
    fa, fb, sa, sb, kc, kc_strip, codes, strip_codes, side_codes = refs
    even_x = 1 - place[0] % 2
    even_y = 1 - place[1] % 2
    tx, ty = cx + 2 * HALO, cy + 2 * HALO
    width = RHS_HALO
    ex = cx + 2 * width

    fill_codes(
        dims, small, strip, xrecv, width * cy * ch + width * ch, even_x, codes, strip_codes
    )
    kc[...] = jnp.zeros_like(kc)
    kc_strip[...] = jnp.zeros_like(kc_strip)

    def conductivity(code):
        value = jnp.zeros_like(code)
        for region in range(regions):
            coeff = jnp.broadcast_to(small[REGION:REGION + 1, region:region + 1], code.shape)
            value = jnp.where(code == region + 1, coeff, value)
        return value

    kc[1:1 + tx, 8 + HALO:8 + HALO + cy] = conductivity(codes[...]).reshape(tx, cy, cz)
    start = ex * width * ch + ex * ch
    for low in (True, False):
        got = pick(yrecv, low, even_y, start, tx * HALO).astype(F32)
        side_codes[...] = conductivity(got)
        y0 = 8 if low else 8 + HALO + cy
        for x in range(tx):
            kc[1 + x, y0:y0 + HALO, :] = side_codes[x * HALO:(x + 1) * HALO, :]
    start += tx * HALO
    low = pick(yrecv, True, even_y, start, 16).astype(F32)
    high = pick(yrecv, False, even_y, start, 16).astype(F32)
    kc_strip[8:8 + tx, :] = conductivity(join_strips(strip_codes[...], low, high, cy))
    coefficients(dims, kc, kc_strip, c, c_strip)

    r[...] = jnp.zeros_like(r)
    r_strip[...] = jnp.zeros_like(r_strip)
    assemble(dims, width, main, strip, xrecv, yrecv, even_x, even_y, r, r_strip)
    weight = sweep_weights(SWEEPS)[0]

    def column(x, _):
        for y in range(HALO - width, HALO + cy + width):
            value = r[x, y] * jnp.broadcast_to(c[6, x, y:y + 1, :], (ch, cz))
            r[x, y] = value
            fa[x, y] = weight * value
        value = r_strip[x] * jnp.broadcast_to(c_strip[6, pl.ds(x, 1), :], (ch, cz))
        r_strip[x] = value
        sa[x] = weight * value
        return _

    lax.fori_loop(HALO - width, HALO + cx + width, column, 0)
    field = smooth(dims, 1, (fa, fb), (sa, sb), r, r_strip, c, c_strip)

    field_out[...] = field[HALO:HALO + cx, HALO:HALO + cy].reshape(cx * cy * ch, cz)
    send_out[...] = strip_rows(lambda x, y: field[HALO + x, HALO + y], cx, cy, cz)
    row, z = node_places(small)
    block_out[:ch, :] = gather_nodes(dims, field, row, z)
    rows = []
    for axis in range(3):
        value = small[axis:axis + 1, :]
        for _ in range(3):
            part = value.astype(BF16).astype(F32)
            rows.append(part)
            value = value - part
    rows += [row.astype(F32), z.astype(F32), jnp.zeros((5, nodes), F32)]
    block_out[ch:, :] = jnp.concatenate(rows, axis=0).astype(BF16)


def boundary_kernel(dims, count, scale, small, recv, kernel_out, sum_out, half_out):
    cx, cy, cz, ch, nodes = dims
    own = [jnp.broadcast_to(small[k:k + 1, :], (nodes, nodes)).T for k in range(3)]

    def block(b, _):
        parts = recv[b, ch:ch + 16, :].astype(F32)
        squared = None
        for k in range(3):
            other = parts[3 * k:3 * k + 1] + parts[3 * k + 1:3 * k + 2] + parts[3 * k + 2:3 * k + 3]
            delta = own[k] - jnp.broadcast_to(other, (nodes, nodes))
            squared = delta * delta if squared is None else squared + delta * delta
        tile = (scale * lax.rsqrt(squared + SOFTENING * SOFTENING)).astype(BF16)
        kernel_out[:, pl.ds(pl.multiple_of(b * nodes, nodes), nodes)] = tile
        return _

    lax.fori_loop(0, count, block, 0)
    total = product(recv, kernel_out, count, dims)
    sum_out[...] = total
    half_out[...] = total.astype(BF16)


def product(recv, tiles, count, dims):
    cx, cy, cz, ch, nodes = dims
    group = math.gcd(count, 32)

    def part(at):
        traces = jnp.concatenate([recv[at + i, :ch, :] for i in range(group)], axis=1)
        start = at * nodes
        if not isinstance(at, int):
            start = pl.multiple_of(start, nodes)
        return lax.dot_general(
            traces, tiles[:, pl.ds(start, group * nodes)], NT, preferred_element_type=F32
        )

    if group == count:
        return part(0)
    return lax.fori_loop(
        0, count // group, lambda i, total: total + part(i * group), jnp.zeros((ch, nodes), F32)
    )


def last_kernel(dims, count, small, recv, tiles, flux_out):
    cx, cy, cz, ch, nodes = dims
    incident = small[INCIDENT:INCIDENT + ch, :]
    flux_out[...] = incident + product(recv, tiles, count, dims)


def fifth_kernel(dims, sizes, nx, ny, place, main, sums, small, recv, blocks, strip, *refs):
    cx, cy, cz, ch, nodes = dims
    xrecv, yrecv, refs = refs[:nx], refs[nx:nx + ny], refs[nx + ny:]
    r_in, rs_in, c, c_strip, refs = *refs[:4], refs[4:]
    field_out, block_out, refs = *refs[:2], refs[2:]
    r, r_strip, fa, fb, sa, sb, left = refs
    even_x = 1 - place[0] % 2
    even_y = 1 - place[1] % 2
    width = RHS_HALO
    r[...] = r_in[...]
    r_strip[...] = rs_in[...]
    fa[...] = jnp.zeros_like(fa)
    sa[...] = jnp.zeros_like(sa)
    assemble(dims, HALO, main, strip, xrecv, yrecv, even_x, even_y, fa, sa)

    def neighbour(dx, dy, dz):
        at = [place[i] + d for i, d in enumerate((dx, dy, dz))]
        good = None
        for i, size in enumerate(sizes):
            ok = (at[i] >= 0) & (at[i] < size)
            good = ok if good is None else good & ok
            at[i] = jnp.clip(at[i], 0, size - 1)
        index = (at[0] * sizes[1] + at[1]) * sizes[2] + at[2]
        info = blocks[index, ch:ch + 16, :].astype(F32)
        good = jnp.full((1, nodes), good.astype(jnp.int32), jnp.int32) > 0
        row = jnp.where(good, info[9:10].astype(jnp.int32), -1)
        return recv[index].astype(F32), row, info[10:11].astype(jnp.int32)

    spans = {
        -1: (HALO - width, HALO, cx), 0: (HALO, HALO + cx, 0), 1: (HALO + cx, HALO + cx + width, -cx),
    }
    own_row, own_z = node_places(small)
    strip_lane = iota((cz, nodes), 0)
    for dx in (-1, 0, 1):
        x0, x1, back_x = spans[dx]
        edge = []
        hits_edge = []
        for dy in (-1, 0, 1):
            y0, y1, back_y = spans[dy]
            parts = []
            if dx == 0 and dy == 0:
                top = sums[...].astype(BF16).astype(F32)
                row, z = own_row, own_z
                parts = [top, sums[...] - top]
            else:
                value, row, z = neighbour(dx, dy, 0)
                parts = [value]
            hits = (iota((cz, nodes), 0) == z).astype(BF16)
            hits = jnp.concatenate([hits] * len(parts), axis=1)
            count = (x1 - x0) * (y1 - y0)
            at = 0
            for x in range(x0, x1):
                for y in range(y0, y1):
                    wanted = (x - HALO + back_x) * cy + (y - HALO + back_y)
                    here = jnp.broadcast_to(row == wanted, (ch, nodes))
                    for i, value in enumerate(parts):
                        left[at:at + ch, i * nodes:(i + 1) * nodes] = jnp.where(
                            here, value, 0.0
                        ).astype(BF16)
                    at += ch
            added = lax.dot_general(
                left[:at, :len(parts) * nodes], hits, NT, preferred_element_type=F32
            )
            at = 0
            for x in range(x0, x1):
                for y in range(y0, y1):
                    inverse = jnp.broadcast_to(c[6, x, y:y + 1, :], (ch, cz))
                    r[x, y] += added[at:at + ch] * inverse
                    at += ch
            for dz in (-1, 1):
                value, row, z = neighbour(dx, dy, dz)
                y = row % cy + cy * dy + HALO
                k = HALO - 1 - z if dz > 0 else HALO + cz - 1 - z
                good = (row >= 0) & (y >= 0) & (y < cy + 2 * HALO) & (k >= 0) & (k < STRIP)
                good = good & ((k < HALO) if dz > 0 else (k >= HALO))
                lane = jnp.where(good, y * STRIP + k, -1)
                hits_edge.append((strip_lane == lane).astype(BF16))
                edge.append((value, jnp.where(row >= 0, row // cy, -1)))
        for x in range(x0, x1):
            at = (x - x0) * ch
            for i, (value, node_x) in enumerate(edge):
                here = jnp.broadcast_to(node_x == x - HALO + back_x, (ch, nodes))
                left[at:at + ch, i * nodes:(i + 1) * nodes] = jnp.where(here, value, 0.0).astype(BF16)
        added = lax.dot_general(
            left[:(x1 - x0) * ch, :len(edge) * nodes], jnp.concatenate(hits_edge, axis=1), NT,
            preferred_element_type=F32,
        )
        for x in range(x0, x1):
            inverse = jnp.broadcast_to(c_strip[6, x:x + 1, :], (ch, cz))
            r_strip[x] += added[(x - x0) * ch:(x - x0 + 1) * ch] * inverse

    field = smooth(dims, 0, (fa, fb), (sa, sb), r, r_strip, c, c_strip)
    for x in range(cx):
        for y in range(cy):
            field_out[pl.ds(x * cy + y, ch, stride=cx * cy), :] = field[HALO + x, HALO + y]
    block_out[...] = gather_nodes(dims, field, own_row, own_z)


def per_device(source, labels, region_coeff, node_cell, node_pos, incident):
    ch, cx, cy, cz = source.shape
    nodes = node_cell.shape[0]
    dims = (cx, cy, cz, ch, nodes)
    sizes = tuple(lax.axis_size(axis) for axis in AXES)
    count = math.prod(sizes)
    nx, ny, nz = (2 if size > 2 else 1 for size in sizes)
    scale = KERNEL_GAIN / math.sqrt(nodes * count)
    tx, ty = cx + 2 * HALO, cy + 2 * HALO
    place = jnp.stack([lax.axis_index(axis) for axis in AXES]).astype(jnp.int32)
    rows = cx * cy * ch
    flat = source.reshape(ch * cx * cy, cz)
    marks = labels.reshape(cx * cy, cz)
    cells = node_cell.reshape(1, nodes)
    shape = jax.ShapeDtypeStruct
    vmem = pltpu.VMEM

    height = INCIDENT + ch + cx * cy
    small = jnp.zeros((height, cz), F32)
    for value, row in (
        (node_pos, 0),
        ((cells // cz).astype(F32), ROW),
        ((cells % cz).astype(F32), LAYER),
        (region_coeff[None], REGION),
        (incident, INCIDENT),
        ((marks + 1).astype(F32), INCIDENT + ch),
    ):
        sides = ((row, height - row - value.shape[0], 0), (0, cz - value.shape[1], 0))
        small += lax.pad(value, jnp.float32(0), sides)
    rhs, send = kernel_call(
        functools.partial(first_kernel, dims),
        (shape((rows, cz), F32), shape((cx * ch + 16, cz), BF16)),
        [vmem((rows, 2 * nodes), BF16)],
        operands=(flat, small),
        name="scatter_first",
    )

    def halo(main, send, width, with_labels, between=(lambda x: x, lambda x: x)):
        zrecv = exchange(send, "col")
        zrecv = between[0](zrecv)
        extra = HALO * cy + 16 if with_labels else 0
        strip_rows_ = cx * ch + (16 if with_labels else 0)
        own = (main, small) if with_labels else (main,)
        strip, *sends = kernel_call(
            functools.partial(second_kernel, dims, width, with_labels, nz, nx),
            (shape((strip_rows_, cz), BF16),)
            + (shape((width * cy * ch + width * ch + extra, cz), BF16),) * nx,
            [vmem((32, cz), F32)] if with_labels else [],
            smem=1,
            operands=(place, *own, *zrecv),
            name="pack_x",
        )
        xrecv = exchange(None, "vol", sends)
        xrecv = between[1](xrecv)
        ex = cx + 2 * width
        extra = tx * HALO + 16 if with_labels else 0
        sends = kernel_call(
            functools.partial(third_kernel, dims, width, with_labels, nx, ny),
            (shape((ex * width * ch + ex * ch + extra, cz), BF16),) * ny,
            [vmem((tx * cy, cz), F32), vmem((tx, cz), F32), vmem((tx * HALO, cz), F32)]
            if with_labels else [],
            smem=1,
            operands=(place, *own, strip, *xrecv),
            name="pack_y",
        )
        yrecv = exchange(None, "row", sends)
        return strip, xrecv, yrecv

    strip, xrecv, yrecv = halo(rhs, send, RHS_HALO, True)
    field, block, send, r, r_strip, c, c_strip = kernel_call(
        functools.partial(fourth_kernel, dims, region_coeff.shape[0], nx, ny),
        (
            shape((rows, cz), F32),
            shape((ch + 16, nodes), BF16),
            shape((cx * ch, cz), BF16),
            shape((tx, ty, ch, cz), F32),
            shape((tx, ch, cz), F32),
            shape((7, tx, ty, cz), F32),
            shape((7, tx, cz), F32),
        ),
        [
            vmem((tx, ty, ch, cz), F32),
            vmem((tx, ty, ch, cz), F32),
            vmem((tx, ch, cz), F32),
            vmem((tx, ch, cz), F32),
            vmem((tx + 2, ty + 16, cz), F32),
            vmem((tx + 16, cz), F32),
            vmem((tx * cy, cz), F32),
            vmem((tx, cz), F32),
            vmem((tx * HALO, cz), F32),
        ],
        smem=1,
        operands=(place, rhs, small, strip, *xrecv, *yrecv),
        name="sweeps_first",
    )

    def to_all(value):
        spread = jnp.broadcast_to(value[None], (count,) + value.shape)
        return lax.all_to_all(spread, AXES, 0, 0, tiled=True)

    blocks = to_all(block)
    tiles, sums, half = kernel_call(
        functools.partial(boundary_kernel, dims, count, scale),
        (
            shape((nodes, count * nodes), BF16),
            shape((ch, nodes), F32),
            shape((ch, nodes), BF16),
        ),
        operands=(small, blocks),
        name="boundary",
    )

    def after_boundary(arrays):
        return lax.optimization_barrier((arrays, half))[0]

    strip, xrecv, yrecv = halo(field, send, HALO, False, (lambda x: x, after_boundary))
    recv = to_all(half)
    field, block = kernel_call(
        functools.partial(fifth_kernel, dims, sizes, nx, ny),
        (shape((ch * cx * cy, cz), F32), shape((ch, nodes), BF16)),
        [
            vmem((tx, ty, ch, cz), F32),
            vmem((tx, ch, cz), F32),
            vmem((tx, ty, ch, cz), F32),
            vmem((tx, ty, ch, cz), F32),
            vmem((tx, ch, cz), F32),
            vmem((tx, ch, cz), F32),
            vmem((rows, 6 * nodes), BF16),
        ],
        smem=1,
        operands=(
            place, field, sums, small, recv, blocks, strip, *xrecv, *yrecv, r, r_strip, c, c_strip
        ),
        name="sweeps_last",
    )
    flux = kernel_call(
        functools.partial(last_kernel, dims, count),
        shape((ch, nodes), F32),
        operands=(small, to_all(block), tiles),
        name="flux_last",
    )
    return field.reshape(source.shape), flux


def solution(mesh):
    placed = (
        P(None, "vol", "row", "col"),
        P("vol", "row", "col"),
        P(),
        P(("vol", "row", "col")),
        P(None, ("vol", "row", "col")),
        P(None, ("vol", "row", "col")),
    )
    return jax.shard_map(
        per_device,
        mesh=mesh,
        in_specs=placed,
        out_specs=(P(None, "vol", "row", "col"), P(None, ("vol", "row", "col"))),
        check_vma=False,
    )
```

```python
import functools
import math

import jax
import jax.numpy as jnp
from jax import lax
from jax.experimental import pallas as pl
from jax.experimental.pallas import tpu as pltpu
from jax.sharding import PartitionSpec as P

SWEEPS = 4
ITERS = 2

MASS_TERM = 0.05
SOFTENING = 0.05
KERNEL_GAIN = 2.0

HALO = SWEEPS
RHS_HALO = SWEEPS - 1
STRIP = 2 * HALO
AXES = ("vol", "row", "col")
F32, BF16 = jnp.float32, jnp.bfloat16
ROW, LAYER, REGION, INCIDENT = 3, 4, 5, 8
SPARE = 4 * 1024 * 1024
NT = (((1,), (1,)), ((), ()))


def sweep_weights(count):
    return [
        1.0 / (1.05 - 0.95 * math.cos(math.pi * (2 * sweep + 1) / (2 * count)))
        for sweep in range(count)
    ]


def iota(shape, dim):
    return lax.broadcasted_iota(jnp.int32, shape, dim)


def kernel_call(body, out_shape, scratch=(), smem=0, operands=(), name=None):
    held = [jnp.shape(leaf) + (leaf.dtype,) for leaf in jax.tree.leaves((out_shape, operands))]
    held += [ref.shape + (ref.dtype,) for ref in scratch]
    need = sum(math.prod(entry[:-1]) * jnp.dtype(entry[-1]).itemsize for entry in held)
    specs = [pl.BlockSpec(memory_space=pltpu.SMEM)] * smem
    specs += [pl.BlockSpec(memory_space=pltpu.VMEM)] * (len(operands) - smem)
    return pl.pallas_call(
        body,
        out_shape=out_shape,
        in_specs=specs,
        out_specs=jax.tree.map(lambda _: pl.BlockSpec(memory_space=pltpu.VMEM), out_shape),
        scratch_shapes=list(scratch),
        compiler_params=pltpu.CompilerParams(vmem_limit_bytes=need + SPARE),
        name=name,
    )(*operands)


def pick(refs, low, even, rows, size):
    first = refs[0][pl.ds(rows, size), :]
    second = refs[1][pl.ds(rows, size), :] if len(refs) > 1 else jnp.zeros_like(first)
    flag = jnp.full(first.shape, even, jnp.int32).astype(first.dtype)
    mine, other = (1 - flag, flag) if low else (flag, 1 - flag)
    return first * mine + second * other


def exchange(array, axis, arrays=None):
    count = lax.axis_size(axis)
    arrays = arrays or [array] * 2
    out = []
    for which in range(2 if count > 2 else 1):
        pairs = []
        for i in range(which, count - 1, 2):
            pairs += [(i, i + 1), (i + 1, i)]
        out.append(lax.ppermute(arrays[which], axis, pairs))
    return out


def edge_picker(cz, lanes):
    z, lane = iota((cz, lanes), 0), iota((cz, lanes), 1)
    k = lane % STRIP
    wanted = jnp.where(k < HALO, HALO - 1 - k, cz - 1 - k + HALO)
    return (z == wanted).astype(F32), lane // STRIP - HALO


def strip_rows(read, cx, cy, cz):
    base, lane_y = edge_picker(cz, cz)
    total = None
    for y in range(cy):
        rows = jnp.concatenate([read(x, y).astype(BF16) for x in range(cx)], axis=0)
        picked = jnp.where(lane_y == y, base, 0.0).astype(BF16)
        part = jnp.dot(rows, picked, preferred_element_type=F32)
        total = part if total is None else total + part
    return total.astype(BF16)


def node_places(small):
    return (small[at:at + 1, :].astype(jnp.int32) for at in (ROW, LAYER))


def first_kernel(dims, source, small, rhs_out, send_out, left):
    cx, cy, cz, ch, nodes = dims
    row, z = node_places(small)
    hits = (iota((cz, nodes), 0) == z).astype(BF16)
    flux = small[INCIDENT:INCIDENT + ch, :]
    top = flux.astype(BF16).astype(F32)
    rest = flux - top
    for r in range(cx * cy):
        here = jnp.broadcast_to(row == r, (ch, nodes))
        left[r * ch:(r + 1) * ch, :nodes] = jnp.where(here, top, 0.0).astype(BF16)
        left[r * ch:(r + 1) * ch, nodes:] = jnp.where(here, rest, 0.0).astype(BF16)
    added = lax.dot_general(
        left[...], jnp.concatenate([hits, hits], axis=1), NT, preferred_element_type=F32
    )
    rhs_out[...] = added
    for r in range(cx * cy):
        rhs_out[r * ch:(r + 1) * ch, :] += source[pl.ds(r, ch, stride=cx * cy), :]

    def read(x, y):
        start = (x * cy + y) * ch
        return rhs_out[start:start + ch, :]

    send_out[:cx * ch, :] = strip_rows(read, cx, cy, cz)
    base, lane_y = edge_picker(cz, cz)
    codes = small[INCIDENT + ch:, :].astype(BF16)
    strips = jnp.dot(codes, base.astype(BF16), preferred_element_type=F32)
    own = (iota(strips.shape, 0) % cy) == lane_y[:1, :]
    strips = jnp.where(own, strips, 0.0).reshape(cx, cy, cz).sum(axis=1)
    send_out[cx * ch:, :] = jnp.concatenate(
        [strips, jnp.zeros((16 - cx, cz), F32)], axis=0
    ).astype(BF16)


def second_kernel(dims, width, with_labels, nz, nx, place, *refs):
    cx, cy, cz, ch, nodes = dims
    main, refs = refs[0], refs[1:]
    if with_labels:
        small, refs = refs[0], refs[1:]
    zrecv, refs = refs[:nz], refs[nz:]
    strip_out, sends, refs = refs[0], refs[1:1 + nx], refs[1 + nx:]
    even_x = 1 - place[0] % 2
    even_z = 1 - place[2] % 2
    rows = cx * ch + (16 if with_labels else 0)
    lane = iota((rows, cz), 1)
    upper = pick(zrecv, False, even_z, 0, rows)
    lower = pick(zrecv, True, even_z, 0, rows)
    strip_out[...] = jnp.where(
        lane % STRIP < HALO, upper.astype(F32), lower.astype(F32)
    ).astype(BF16)
    if with_labels:
        (codes,) = refs
        codes[...] = jnp.zeros_like(codes)
        codes[:16, :] = strip_out[cx * ch:, :].astype(F32)
    slab = width * cy * ch
    for which in range(nx):
        upward = even_x if which == 0 else 1 - even_x
        x0 = upward * (cx - width)
        send = sends[which]
        send[:slab, :] = main[pl.ds(pl.multiple_of(x0 * (cy * ch), 16), slab), :].astype(BF16)
        send[slab:slab + width * ch, :] = strip_out[
            pl.ds(pl.multiple_of(x0 * ch, 16), width * ch), :
        ]
        if with_labels:
            start = slab + width * ch
            x0 = upward * (cx - HALO)
            send[start:start + HALO * cy, :] = (
                small[pl.ds(pl.multiple_of(INCIDENT + ch + x0 * cy, 8), HALO * cy), :]
            ).astype(BF16)
            send[start + HALO * cy:, :] = codes[pl.ds(x0, 16), :].astype(BF16)


def third_kernel(dims, width, with_labels, nx, ny, place, *refs):
    cx, cy, cz, ch, nodes = dims
    main, refs = refs[0], refs[1:]
    if with_labels:
        small, refs = refs[0], refs[1:]
    strip, refs = refs[0], refs[1:]
    xrecv, refs = refs[:nx], refs[nx:]
    sends, refs = refs[:ny], refs[ny:]
    even_x = 1 - place[0] % 2
    even_y = 1 - place[1] % 2
    ex = cx + 2 * width
    slab = width * cy * ch
    if with_labels:
        codes, strip_codes, picked = refs
        fill_codes(dims, small, strip, xrecv, slab + width * ch, even_x, codes, strip_codes)
    for which in range(ny):
        send = sends[which]
        upward = even_y if which == 0 else 1 - even_y
        y0 = upward * (cy - width)
        size = width * ch
        for x in range(ex):
            if width <= x < width + cx:
                start = pl.multiple_of(((x - width) * cy + y0) * ch, 16)
                piece = main[pl.ds(start, size), :].astype(BF16)
            else:
                low = x < width
                start = pl.multiple_of(((x if low else x - width - cx) * cy + y0) * ch, 16)
                piece = pick(xrecv, low, even_x, start, size)
            send[x * size:(x + 1) * size, :] = piece
        start = ex * size
        send[start:start + width * ch, :] = pick(xrecv, True, even_x, slab, width * ch)
        send[start + width * ch:start + (width + cx) * ch, :] = strip[:cx * ch, :]
        send[start + (width + cx) * ch:start + ex * ch, :] = pick(
            xrecv, False, even_x, slab, width * ch
        )
        if with_labels:
            start += ex * ch
            y0 = upward * (cy - HALO)
            tall = cx + 2 * HALO
            for x in range(tall):
                picked[x * HALO:(x + 1) * HALO, :] = codes[pl.ds(x * cy + y0, HALO), :]
            send[start:start + tall * HALO, :] = picked[...].astype(BF16)
            send[start + tall * HALO:, :] = strip_codes[...].astype(BF16)


def fill_codes(dims, small, strip, xrecv, start, even_x, codes, strip_codes):
    cx, cy, cz, ch, nodes = dims
    side = HALO * cy
    codes[:side, :] = pick(xrecv, True, even_x, start, side).astype(F32)
    codes[side:side + cx * cy, :] = small[INCIDENT + ch:, :]
    codes[side + cx * cy:, :] = pick(xrecv, False, even_x, start, side).astype(F32)
    strip_codes[:HALO, :] = pick(xrecv, True, even_x, start + side, 16).astype(F32)[:HALO]
    strip_codes[HALO:HALO + cx, :] = strip[cx * ch:cx * ch + 16, :].astype(F32)[:cx]
    strip_codes[HALO + cx:, :] = pick(xrecv, False, even_x, start + side, 16).astype(F32)[:HALO]


def assemble(dims, width, main, strip, xrecv, yrecv, even_x, even_y, out, out_strip):
    cx, cy, cz, ch, nodes = dims
    ex = cx + 2 * width
    out[HALO:HALO + cx, HALO:HALO + cy] = main[...].reshape(cx, cy, ch, cz)
    slab = width * cy * ch
    low = pick(xrecv, True, even_x, 0, slab).astype(F32)
    out[HALO - width:HALO, HALO:HALO + cy] = low.reshape(width, cy, ch, cz)
    high = pick(xrecv, False, even_x, 0, slab).astype(F32)
    out[HALO + cx:HALO + cx + width, HALO:HALO + cy] = high.reshape(width, cy, ch, cz)
    size = ex * width * ch
    low = pick(yrecv, True, even_y, 0, size).astype(F32)
    out[HALO - width:HALO + cx + width, HALO - width:HALO] = low.reshape(ex, width, ch, cz)
    high = pick(yrecv, False, even_y, 0, size).astype(F32)
    out[HALO - width:HALO + cx + width, HALO + cy:HALO + cy + width] = high.reshape(
        ex, width, ch, cz
    )
    own = jnp.concatenate(
        [
            pick(xrecv, True, even_x, slab, width * ch),
            strip[:cx * ch, :],
            pick(xrecv, False, even_x, slab, width * ch),
        ],
        axis=0,
    ).astype(F32)
    low = pick(yrecv, True, even_y, size, ex * ch).astype(F32)
    high = pick(yrecv, False, even_y, size, ex * ch).astype(F32)
    full = join_strips(own, low, high, cy)
    out_strip[HALO - width:HALO + cx + width] = full.reshape(ex, ch, cz)


def join_strips(own, low, high, cy):
    lane = iota(own.shape, 1)
    shift = cy * STRIP
    lanes = own.shape[1]
    low = pltpu.roll(low, lanes - shift, 1)
    high = pltpu.roll(high, shift, 1)
    return jnp.where(
        lane < HALO * STRIP, low, jnp.where(lane < (HALO + cy) * STRIP, own, high)
    )


def sweep(dims, reach, weight, src, src_strip, dst, dst_strip, r, r_strip, c, c_strip):
    cx, cy, cz, ch, nodes = dims
    lane = iota((ch, cz), 1)
    first, last = lane == 0, lane == cz - 1
    k = lane % STRIP
    group = lane // STRIP
    touching = (k == HALO) | (k == HALO - 1)

    def spread(ref, k, x, y):
        return jnp.broadcast_to(ref[k, x, y:y + 1, :], (ch, cz))

    def column(x):
        far = reach - max(HALO - x, x - (HALO + cx - 1), 0)
        low, high = HALO - far, HALO + cy + far
        beyond = src_strip[x]
        ends = jnp.zeros_like(beyond)
        behind, here = src[x, low - 1], src[x, low]
        for y in range(low, high):
            ahead = src[x, y + 1]
            edge = pltpu.roll(beyond, (2 * cz - (y * STRIP + HALO)) % cz, 1)
            above = jnp.where(last, edge, pltpu.roll(here, cz - 1, 1))
            below = jnp.where(first, edge, pltpu.roll(here, 1, 1))
            total = r[x, y] - here
            total += spread(c, 0, x, y) * src[x + 1, y]
            total += spread(c, 1, x, y) * src[x - 1, y]
            total += spread(c, 2, x, y) * ahead
            total += spread(c, 3, x, y) * behind
            total += spread(c, 4, x, y) * above
            total += spread(c, 5, x, y) * below
            dst[x, y] = here + weight * total
            if far > 0 and low < y < high - 1:
                moved = pltpu.roll(here, (y * STRIP + HALO) % cz, 1)
                ends = jnp.where(touching & (group == y), moved, ends)
            behind, here = here, ahead
        if far > 0:
            strip_column(x, beyond, ends)

    def strip_column(x, here, ends):
        def spread_strip(k):
            return jnp.broadcast_to(c_strip[k, x:x + 1, :], (ch, cz))

        above = jnp.where(k == HALO, ends, pltpu.roll(here, 1, 1))
        below = jnp.where(k == HALO - 1, ends, pltpu.roll(here, cz - 1, 1))
        total = r_strip[x] - here
        total += spread_strip(0) * src_strip[x + 1]
        total += spread_strip(1) * src_strip[x - 1]
        total += spread_strip(2) * pltpu.roll(here, cz - STRIP, 1)
        total += spread_strip(3) * pltpu.roll(here, STRIP, 1)
        total += spread_strip(4) * above
        total += spread_strip(5) * below
        dst_strip[x] = here + weight * total

    for x in range(HALO - reach, HALO + cx + reach):
        column(x)


def coefficients(dims, kc, kc_strip, c, c_strip):
    cx, cy, cz, ch, nodes = dims
    tx, ty = cx + 2 * HALO, cy + 2 * HALO
    lane = iota((ty, cz), 1)
    y = iota((ty, cz), 0)
    here = kc_strip[8:8 + tx, :]
    group = lane // STRIP
    k = lane % STRIP
    touching = ((k == HALO) | (k == HALO - 1)) & (group == y)
    ends = []
    for x in range(tx):
        own = kc[x + 1, 8:8 + ty, :]
        moved = pltpu.roll(own, HALO, 1, stride=STRIP, stride_axis=0)
        ends.append(jnp.sum(jnp.where(touching, moved, 0.0), axis=0, keepdims=True))
        beyond = jnp.broadcast_to(kc_strip[8 + x:9 + x, :], (ty, cz))
        upper = jnp.where((group == y) & (k == HALO - 1), beyond, 0.0).sum(axis=1, keepdims=True)
        lower = jnp.where((group == y) & (k == HALO), beyond, 0.0).sum(axis=1, keepdims=True)
        others = [
            kc[x + 2, 8:8 + ty, :],
            kc[x, 8:8 + ty, :],
            kc[x + 1, 9:9 + ty, :],
            kc[x + 1, 7:7 + ty, :],
            jnp.where(lane == cz - 1, upper, pltpu.roll(own, cz - 1, 1)),
            jnp.where(lane == 0, lower, pltpu.roll(own, 1, 1)),
        ]
        finish(own, others, [c.at[i, x] for i in range(7)])
    ends = jnp.concatenate(ends, axis=0)
    lane = iota((tx, cz), 1)
    k = lane % STRIP
    others = [
        kc_strip[9:9 + tx, :],
        kc_strip[7:7 + tx, :],
        pltpu.roll(here, cz - STRIP, 1),
        pltpu.roll(here, STRIP, 1),
        jnp.where(k == HALO, ends, pltpu.roll(here, 1, 1)),
        jnp.where(k == HALO - 1, ends, pltpu.roll(here, cz - 1, 1)),
    ]
    finish(here, others, [c_strip.at[i] for i in range(7)])


def finish(own, others, outs):
    faces = [0.5 * (own + other) for other in others]
    diag = MASS_TERM + faces[0]
    for face in faces[1:]:
        diag = diag + face
    inverse = jnp.where(own > 0.0, 1.0 / diag, 0.0)
    for face, out in zip(faces, outs[:6], strict=True):
        out[...] = face * inverse
    outs[6][...] = inverse


def smooth(dims, start, fields, strips, r, r_strip, c, c_strip):
    weights = sweep_weights(SWEEPS)
    now = 0
    for number in range(start, SWEEPS):
        sweep(
            dims, SWEEPS - 1 - number, weights[number], fields[now], strips[now],
            fields[1 - now], strips[1 - now], r, r_strip, c, c_strip,
        )
        now = 1 - now
    return fields[now]


def gather_nodes(dims, field, row, z):
    cx, cy, cz, ch, nodes = dims
    hits = (iota((cz, nodes), 0) == z).astype(BF16)
    rows = field[HALO:HALO + cx, HALO:HALO + cy].reshape(cx * cy * ch, cz).astype(BF16)
    at_z = jnp.dot(rows, hits, preferred_element_type=F32)
    total = jnp.zeros((ch, nodes), F32)
    for r in range(cx * cy):
        here = jnp.broadcast_to(row == r, (ch, nodes))
        total = jnp.where(here, at_z[r * ch:(r + 1) * ch], total)
    return total.astype(BF16)


def fourth_kernel(dims, regions, nx, ny, place, main, small, strip, *refs):
    cx, cy, cz, ch, nodes = dims
    xrecv, yrecv, refs = refs[:nx], refs[nx:nx + ny], refs[nx + ny:]
    field_out, block_out, send_out, r, r_strip, c, c_strip, refs = *refs[:7], refs[7:]
    fa, fb, sa, sb, kc, kc_strip, codes, strip_codes, side_codes = refs
    even_x = 1 - place[0] % 2
    even_y = 1 - place[1] % 2
    tx, ty = cx + 2 * HALO, cy + 2 * HALO
    width = RHS_HALO
    ex = cx + 2 * width

    fill_codes(
        dims, small, strip, xrecv, width * cy * ch + width * ch, even_x, codes, strip_codes
    )
    kc[...] = jnp.zeros_like(kc)
    kc_strip[...] = jnp.zeros_like(kc_strip)

    def conductivity(code):
        value = jnp.zeros_like(code)
        for region in range(regions):
            coeff = jnp.broadcast_to(small[REGION:REGION + 1, region:region + 1], code.shape)
            value = jnp.where(code == region + 1, coeff, value)
        return value

    kc[1:1 + tx, 8 + HALO:8 + HALO + cy] = conductivity(codes[...]).reshape(tx, cy, cz)
    start = ex * width * ch + ex * ch
    for low in (True, False):
        got = pick(yrecv, low, even_y, start, tx * HALO).astype(F32)
        side_codes[...] = conductivity(got)
        y0 = 8 if low else 8 + HALO + cy
        for x in range(tx):
            kc[1 + x, y0:y0 + HALO, :] = side_codes[x * HALO:(x + 1) * HALO, :]
    start += tx * HALO
    low = pick(yrecv, True, even_y, start, 16).astype(F32)
    high = pick(yrecv, False, even_y, start, 16).astype(F32)
    kc_strip[8:8 + tx, :] = conductivity(join_strips(strip_codes[...], low, high, cy))
    coefficients(dims, kc, kc_strip, c, c_strip)

    r[...] = jnp.zeros_like(r)
    r_strip[...] = jnp.zeros_like(r_strip)
    assemble(dims, width, main, strip, xrecv, yrecv, even_x, even_y, r, r_strip)
    weight = sweep_weights(SWEEPS)[0]

    def column(x, _):
        for y in range(HALO - width, HALO + cy + width):
            value = r[x, y] * jnp.broadcast_to(c[6, x, y:y + 1, :], (ch, cz))
            r[x, y] = value
            fa[x, y] = weight * value
        value = r_strip[x] * jnp.broadcast_to(c_strip[6, pl.ds(x, 1), :], (ch, cz))
        r_strip[x] = value
        sa[x] = weight * value
        return _

    lax.fori_loop(HALO - width, HALO + cx + width, column, 0)
    field = smooth(dims, 1, (fa, fb), (sa, sb), r, r_strip, c, c_strip)

    field_out[...] = field[HALO:HALO + cx, HALO:HALO + cy].reshape(cx * cy * ch, cz)
    send_out[...] = strip_rows(lambda x, y: field[HALO + x, HALO + y], cx, cy, cz)
    row, z = node_places(small)
    block_out[:ch, :] = gather_nodes(dims, field, row, z)
    rows = []
    for axis in range(3):
        value = small[axis:axis + 1, :]
        for _ in range(3):
            part = value.astype(BF16).astype(F32)
            rows.append(part)
            value = value - part
    rows += [row.astype(F32), z.astype(F32), jnp.zeros((5, nodes), F32)]
    block_out[ch:, :] = jnp.concatenate(rows, axis=0).astype(BF16)


def boundary_kernel(dims, count, scale, small, recv, kernel_out, sum_out, half_out):
    cx, cy, cz, ch, nodes = dims
    own = [jnp.broadcast_to(small[k:k + 1, :], (nodes, nodes)).T for k in range(3)]

    def block(b, _):
        parts = recv[b, ch:ch + 16, :].astype(F32)
        squared = None
        for k in range(3):
            other = parts[3 * k:3 * k + 1] + parts[3 * k + 1:3 * k + 2] + parts[3 * k + 2:3 * k + 3]
            delta = own[k] - jnp.broadcast_to(other, (nodes, nodes))
            squared = delta * delta if squared is None else squared + delta * delta
        tile = (scale * lax.rsqrt(squared + SOFTENING * SOFTENING)).astype(BF16)
        kernel_out[:, pl.ds(pl.multiple_of(b * nodes, nodes), nodes)] = tile
        return _

    lax.fori_loop(0, count, block, 0)
    total = product(recv, kernel_out, count, dims)
    sum_out[...] = total
    half_out[...] = total.astype(BF16)


def product(recv, tiles, count, dims):
    cx, cy, cz, ch, nodes = dims
    group = math.gcd(count, 32)

    def part(at):
        traces = jnp.concatenate([recv[at + i, :ch, :] for i in range(group)], axis=1)
        start = at * nodes
        if not isinstance(at, int):
            start = pl.multiple_of(start, nodes)
        return lax.dot_general(
            traces, tiles[:, pl.ds(start, group * nodes)], NT, preferred_element_type=F32
        )

    if group == count:
        return part(0)
    return lax.fori_loop(
        0, count // group, lambda i, total: total + part(i * group), jnp.zeros((ch, nodes), F32)
    )


def last_kernel(dims, count, small, recv, tiles, flux_out):
    cx, cy, cz, ch, nodes = dims
    incident = small[INCIDENT:INCIDENT + ch, :]
    flux_out[...] = incident + product(recv, tiles, count, dims)


def fifth_kernel(dims, sizes, nx, ny, place, main, sums, small, recv, blocks, strip, *refs):
    cx, cy, cz, ch, nodes = dims
    xrecv, yrecv, refs = refs[:nx], refs[nx:nx + ny], refs[nx + ny:]
    r_in, rs_in, c, c_strip, refs = *refs[:4], refs[4:]
    field_out, block_out, refs = *refs[:2], refs[2:]
    r, r_strip, fa, fb, sa, sb, left = refs
    even_x = 1 - place[0] % 2
    even_y = 1 - place[1] % 2
    width = RHS_HALO
    r[...] = r_in[...]
    r_strip[...] = rs_in[...]
    fa[...] = jnp.zeros_like(fa)
    sa[...] = jnp.zeros_like(sa)
    assemble(dims, HALO, main, strip, xrecv, yrecv, even_x, even_y, fa, sa)

    def neighbour(dx, dy, dz):
        at = [place[i] + d for i, d in enumerate((dx, dy, dz))]
        good = None
        for i, size in enumerate(sizes):
            ok = (at[i] >= 0) & (at[i] < size)
            good = ok if good is None else good & ok
            at[i] = jnp.clip(at[i], 0, size - 1)
        index = (at[0] * sizes[1] + at[1]) * sizes[2] + at[2]
        info = blocks[index, ch:ch + 16, :].astype(F32)
        good = jnp.full((1, nodes), good.astype(jnp.int32), jnp.int32) > 0
        row = jnp.where(good, info[9:10].astype(jnp.int32), -1)
        return recv[index].astype(F32), row, info[10:11].astype(jnp.int32)

    spans = {
        -1: (HALO - width, HALO, cx), 0: (HALO, HALO + cx, 0), 1: (HALO + cx, HALO + cx + width, -cx),
    }
    own_row, own_z = node_places(small)
    strip_lane = iota((cz, nodes), 0)
    for dx in (-1, 0, 1):
        x0, x1, back_x = spans[dx]
        edge = []
        hits_edge = []
        for dy in (-1, 0, 1):
            y0, y1, back_y = spans[dy]
            parts = []
            if dx == 0 and dy == 0:
                top = sums[...].astype(BF16).astype(F32)
                row, z = own_row, own_z
                parts = [top, sums[...] - top]
            else:
                value, row, z = neighbour(dx, dy, 0)
                parts = [value]
            hits = (iota((cz, nodes), 0) == z).astype(BF16)
            hits = jnp.concatenate([hits] * len(parts), axis=1)
            count = (x1 - x0) * (y1 - y0)
            at = 0
            for x in range(x0, x1):
                for y in range(y0, y1):
                    wanted = (x - HALO + back_x) * cy + (y - HALO + back_y)
                    here = jnp.broadcast_to(row == wanted, (ch, nodes))
                    for i, value in enumerate(parts):
                        left[at:at + ch, i * nodes:(i + 1) * nodes] = jnp.where(
                            here, value, 0.0
                        ).astype(BF16)
                    at += ch
            added = lax.dot_general(
                left[:at, :len(parts) * nodes], hits, NT, preferred_element_type=F32
            )
            at = 0
            for x in range(x0, x1):
                for y in range(y0, y1):
                    inverse = jnp.broadcast_to(c[6, x, y:y + 1, :], (ch, cz))
                    r[x, y] += added[at:at + ch] * inverse
                    at += ch
            for dz in (-1, 1):
                value, row, z = neighbour(dx, dy, dz)
                y = row % cy + cy * dy + HALO
                k = HALO - 1 - z if dz > 0 else HALO + cz - 1 - z
                good = (row >= 0) & (y >= 0) & (y < cy + 2 * HALO) & (k >= 0) & (k < STRIP)
                good = good & ((k < HALO) if dz > 0 else (k >= HALO))
                lane = jnp.where(good, y * STRIP + k, -1)
                hits_edge.append((strip_lane == lane).astype(BF16))
                edge.append((value, jnp.where(row >= 0, row // cy, -1)))
        for x in range(x0, x1):
            at = (x - x0) * ch
            for i, (value, node_x) in enumerate(edge):
                here = jnp.broadcast_to(node_x == x - HALO + back_x, (ch, nodes))
                left[at:at + ch, i * nodes:(i + 1) * nodes] = jnp.where(here, value, 0.0).astype(BF16)
        added = lax.dot_general(
            left[:(x1 - x0) * ch, :len(edge) * nodes], jnp.concatenate(hits_edge, axis=1), NT,
            preferred_element_type=F32,
        )
        for x in range(x0, x1):
            inverse = jnp.broadcast_to(c_strip[6, x:x + 1, :], (ch, cz))
            r_strip[x] += added[(x - x0) * ch:(x - x0 + 1) * ch] * inverse

    field = smooth(dims, 0, (fa, fb), (sa, sb), r, r_strip, c, c_strip)
    for x in range(cx):
        for y in range(cy):
            field_out[pl.ds(x * cy + y, ch, stride=cx * cy), :] = field[HALO + x, HALO + y]
    block_out[...] = gather_nodes(dims, field, own_row, own_z)


def per_device(source, labels, region_coeff, node_cell, node_pos, incident):
    ch, cx, cy, cz = source.shape
    nodes = node_cell.shape[0]
    dims = (cx, cy, cz, ch, nodes)
    sizes = tuple(lax.axis_size(axis) for axis in AXES)
    count = math.prod(sizes)
    nx, ny, nz = (2 if size > 2 else 1 for size in sizes)
    scale = KERNEL_GAIN / math.sqrt(nodes * count)
    tx, ty = cx + 2 * HALO, cy + 2 * HALO
    place = jnp.stack([lax.axis_index(axis) for axis in AXES]).astype(jnp.int32)
    rows = cx * cy * ch
    flat = source.reshape(ch * cx * cy, cz)
    marks = labels.reshape(cx * cy, cz)
    cells = node_cell.reshape(1, nodes)
    shape = jax.ShapeDtypeStruct
    vmem = pltpu.VMEM

    height = INCIDENT + ch + cx * cy
    small = jnp.zeros((height, cz), F32)
    for value, row in (
        (node_pos, 0),
        ((cells // cz).astype(F32), ROW),
        ((cells % cz).astype(F32), LAYER),
        (region_coeff[None], REGION),
        (incident, INCIDENT),
        ((marks + 1).astype(F32), INCIDENT + ch),
    ):
        sides = ((row, height - row - value.shape[0], 0), (0, cz - value.shape[1], 0))
        small += lax.pad(value, jnp.float32(0), sides)
    rhs, send = kernel_call(
        functools.partial(first_kernel, dims),
        (shape((rows, cz), F32), shape((cx * ch + 16, cz), BF16)),
        [vmem((rows, 2 * nodes), BF16)],
        operands=(flat, small),
        name="scatter_first",
    )

    def halo(main, send, width, with_labels, between=(lambda x: x, lambda x: x)):
        zrecv = exchange(send, "col")
        zrecv = between[0](zrecv)
        extra = HALO * cy + 16 if with_labels else 0
        strip_rows_ = cx * ch + (16 if with_labels else 0)
        own = (main, small) if with_labels else (main,)
        strip, *sends = kernel_call(
            functools.partial(second_kernel, dims, width, with_labels, nz, nx),
            (shape((strip_rows_, cz), BF16),)
            + (shape((width * cy * ch + width * ch + extra, cz), BF16),) * nx,
            [vmem((32, cz), F32)] if with_labels else [],
            smem=1,
            operands=(place, *own, *zrecv),
            name="pack_x",
        )
        xrecv = exchange(None, "vol", sends)
        xrecv = between[1](xrecv)
        ex = cx + 2 * width
        extra = tx * HALO + 16 if with_labels else 0
        sends = kernel_call(
            functools.partial(third_kernel, dims, width, with_labels, nx, ny),
            (shape((ex * width * ch + ex * ch + extra, cz), BF16),) * ny,
            [vmem((tx * cy, cz), F32), vmem((tx, cz), F32), vmem((tx * HALO, cz), F32)]
            if with_labels else [],
            smem=1,
            operands=(place, *own, strip, *xrecv),
            name="pack_y",
        )
        yrecv = exchange(None, "row", sends)
        return strip, xrecv, yrecv

    strip, xrecv, yrecv = halo(rhs, send, RHS_HALO, True)
    field, block, send, r, r_strip, c, c_strip = kernel_call(
        functools.partial(fourth_kernel, dims, region_coeff.shape[0], nx, ny),
        (
            shape((rows, cz), F32),
            shape((ch + 16, nodes), BF16),
            shape((cx * ch, cz), BF16),
            shape((tx, ty, ch, cz), F32),
            shape((tx, ch, cz), F32),
            shape((7, tx, ty, cz), F32),
            shape((7, tx, cz), F32),
        ),
        [
            vmem((tx, ty, ch, cz), F32),
            vmem((tx, ty, ch, cz), F32),
            vmem((tx, ch, cz), F32),
            vmem((tx, ch, cz), F32),
            vmem((tx + 2, ty + 16, cz), F32),
            vmem((tx + 16, cz), F32),
            vmem((tx * cy, cz), F32),
            vmem((tx, cz), F32),
            vmem((tx * HALO, cz), F32),
        ],
        smem=1,
        operands=(place, rhs, small, strip, *xrecv, *yrecv),
        name="sweeps_first",
    )

    def to_all(value):
        spread = jnp.broadcast_to(value[None], (count,) + value.shape)
        return lax.all_to_all(spread, AXES, 0, 0, tiled=True)

    blocks = to_all(block)
    tiles, sums, half = kernel_call(
        functools.partial(boundary_kernel, dims, count, scale),
        (
            shape((nodes, count * nodes), BF16),
            shape((ch, nodes), F32),
            shape((ch, nodes), BF16),
        ),
        operands=(small, blocks),
        name="boundary",
    )

    def after_boundary(arrays):
        return lax.optimization_barrier((arrays, half))[0]

    strip, xrecv, yrecv = halo(field, send, HALO, False, (lambda x: x, after_boundary))
    recv = to_all(half)
    field, block = kernel_call(
        functools.partial(fifth_kernel, dims, sizes, nx, ny),
        (shape((ch * cx * cy, cz), F32), shape((ch, nodes), BF16)),
        [
            vmem((tx, ty, ch, cz), F32),
            vmem((tx, ch, cz), F32),
            vmem((tx, ty, ch, cz), F32),
            vmem((tx, ty, ch, cz), F32),
            vmem((tx, ch, cz), F32),
            vmem((tx, ch, cz), F32),
            vmem((rows, 6 * nodes), BF16),
        ],
        smem=1,
        operands=(
            place, field, sums, small, recv, blocks, strip, *xrecv, *yrecv, r, r_strip, c, c_strip
        ),
        name="sweeps_last",
    )
    flux = kernel_call(
        functools.partial(last_kernel, dims, count),
        shape((ch, nodes), F32),
        operands=(small, to_all(block), tiles),
        name="flux_last",
    )
    return field.reshape(source.shape), flux


def solution(mesh):
    placed = (
        P(None, "vol", "row", "col"),
        P("vol", "row", "col"),
        P(),
        P(("vol", "row", "col")),
        P(None, ("vol", "row", "col")),
        P(None, ("vol", "row", "col")),
    )
    return jax.shard_map(
        per_device,
        mesh=mesh,
        in_specs=placed,
        out_specs=(P(None, "vol", "row", "col"), P(None, ("vol", "row", "col"))),
        check_vma=False,
    )
```

```python
import functools
import math

import jax
import jax.numpy as jnp
from jax import lax
from jax.experimental import pallas as pl
from jax.experimental.pallas import tpu as pltpu
from jax.sharding import PartitionSpec as P

SWEEPS = 4
ITERS = 2

MASS_TERM = 0.05
SOFTENING = 0.05
KERNEL_GAIN = 2.0

HALO = SWEEPS
RHS_HALO = SWEEPS - 1
STRIP = 2 * HALO
AXES = ("vol", "row", "col")
F32, BF16 = jnp.float32, jnp.bfloat16
ROW, LAYER, REGION, INCIDENT = 3, 4, 5, 8
SPARE = 4 * 1024 * 1024
NT = (((1,), (1,)), ((), ()))


def sweep_weights(count):
    return [
        1.0 / (1.05 - 0.95 * math.cos(math.pi * (2 * sweep + 1) / (2 * count)))
        for sweep in range(count)
    ]


def iota(shape, dim):
    return lax.broadcasted_iota(jnp.int32, shape, dim)


def kernel_call(body, out_shape, scratch=(), smem=0, operands=(), cost=None, name=None):
    held = [jnp.shape(leaf) + (leaf.dtype,) for leaf in jax.tree.leaves((out_shape, operands))]
    held += [ref.shape + (ref.dtype,) for ref in scratch]
    need = sum(math.prod(entry[:-1]) * jnp.dtype(entry[-1]).itemsize for entry in held)
    specs = [pl.BlockSpec(memory_space=pltpu.SMEM)] * smem
    specs += [pl.BlockSpec(memory_space=pltpu.VMEM)] * (len(operands) - smem)
    return pl.pallas_call(
        body,
        out_shape=out_shape,
        in_specs=specs,
        out_specs=jax.tree.map(lambda _: pl.BlockSpec(memory_space=pltpu.VMEM), out_shape),
        scratch_shapes=list(scratch),
        compiler_params=pltpu.CompilerParams(vmem_limit_bytes=need + SPARE),
        cost_estimate=cost,
        name=name,
    )(*operands)


def layers_left(dims, x, reach):
    cx = dims[0]
    return reach - max(HALO - x, x - (HALO + cx - 1), 0)


@functools.lru_cache
def held_rows(dims):
    cx, cy, cz, ch, nodes = dims
    starts, total = {}, 0
    for x in range(cx + 2 * HALO):
        far = layers_left(dims, x, RHS_HALO)
        if far >= 0:
            starts[x] = (total, HALO - far, HALO + cy + far)
            total += cy + 2 * far
    return starts, total


def row_of(dims, x, y):
    first, y0, y1 = held_rows(dims)[0][x]
    return first + y - y0


@functools.lru_cache(maxsize=None)
def kept_row(dims, x, y):
    cx, cy, cz, ch, nodes = dims
    starts, total = held_rows(dims)
    if HALO <= x < HALO + cx and HALO <= y < HALO + cy:
        return True, (x - HALO) * cy + y - HALO
    before = 0
    for other in sorted(starts):
        first, y0, y1 = starts[other]
        for at in range(y0, y1):
            if (other, at) == (x, y):
                return False, before
            before += not (HALO <= other < HALO + cx and HALO <= at < HALO + cy)
    raise KeyError(x, y)


def x_sizes(dims, width):
    cx, cy, cz, ch, nodes = dims
    return width * cy * ch, (width - 1) * ch


def y_sizes(dims, width):
    cx, cy, cz, ch, nodes = dims
    return [(cx + 2 * (width - d)) * ch for d in range(1, width + 1)], (cx + 2 * (width - 2)) * ch


def pick(refs, low, even, rows, size):
    first = refs[0][pl.ds(rows, size), :]
    second = refs[1][pl.ds(rows, size), :] if len(refs) > 1 else jnp.zeros_like(first)
    flag = jnp.full(first.shape, even, jnp.int32).astype(first.dtype)
    mine, other = (1 - flag, flag) if low else (flag, 1 - flag)
    return first * mine + second * other


def exchange(array, axis, arrays=None):
    count = lax.axis_size(axis)
    arrays = arrays or [array] * 2
    out = []
    for which in range(2 if count > 2 else 1):
        pairs = []
        for i in range(which, count - 1, 2):
            pairs += [(i, i + 1), (i + 1, i)]
        out.append(lax.ppermute(arrays[which], axis, pairs))
    return out


def edge_picker(cz, lanes):
    z, lane = iota((cz, lanes), 0), iota((cz, lanes), 1)
    k = lane % STRIP
    wanted = jnp.where(k < HALO, HALO - 1 - k, cz - 1 - k + HALO)
    return (z == wanted).astype(F32), lane // STRIP - HALO


def strip_rows(read, cx, cy, cz):
    base, lane_y = edge_picker(cz, cz)
    total = None
    for y in range(cy):
        rows = jnp.concatenate([read(x, y).astype(BF16) for x in range(cx)], axis=0)
        picked = jnp.where(lane_y == y, base, 0.0).astype(BF16)
        part = jnp.dot(rows, picked, preferred_element_type=F32)
        total = part if total is None else total + part
    return total.astype(BF16)


def node_places(small):
    return (small[at:at + 1, :].astype(jnp.int32) for at in (ROW, LAYER))


def first_kernel(dims, source, small, rhs_out, send_out, left):
    cx, cy, cz, ch, nodes = dims
    row, z = node_places(small)
    hits = (iota((cz, nodes), 0) == z).astype(BF16)
    flux = small[INCIDENT:INCIDENT + ch, :]
    top = flux.astype(BF16).astype(F32)
    rest = flux - top
    for r in range(cx * cy):
        here = jnp.broadcast_to(row == r, (ch, nodes))
        left[r * ch:(r + 1) * ch, :nodes] = jnp.where(here, top, 0.0).astype(BF16)
        left[r * ch:(r + 1) * ch, nodes:] = jnp.where(here, rest, 0.0).astype(BF16)
    added = lax.dot_general(
        left[...], jnp.concatenate([hits, hits], axis=1), NT, preferred_element_type=F32
    )
    rhs_out[...] = added
    for r in range(cx * cy):
        rhs_out[r * ch:(r + 1) * ch, :] += source[pl.ds(r, ch, stride=cx * cy), :]

    def read(x, y):
        start = (x * cy + y) * ch
        return rhs_out[start:start + ch, :]

    send_out[:cx * ch, :] = strip_rows(read, cx, cy, cz)
    base, lane_y = edge_picker(cz, cz)
    codes = small[INCIDENT + ch:, :].astype(BF16)
    strips = jnp.dot(codes, base.astype(BF16), preferred_element_type=F32)
    own = (iota(strips.shape, 0) % cy) == lane_y[:1, :]
    strips = jnp.where(own, strips, 0.0).reshape(cx, cy, cz).sum(axis=1)
    send_out[cx * ch:, :] = jnp.concatenate(
        [strips, jnp.zeros((16 - cx, cz), F32)], axis=0
    ).astype(BF16)


def second_kernel(dims, width, with_labels, nz, nx, place, *refs):
    cx, cy, cz, ch, nodes = dims
    main, refs = refs[0], refs[1:]
    if with_labels:
        small, refs = refs[0], refs[1:]
    zrecv, refs = refs[:nz], refs[nz:]
    strip_out, sends, refs = refs[0], refs[1:1 + nx], refs[1 + nx:]
    even_x = 1 - place[0] % 2
    even_z = 1 - place[2] % 2
    rows = cx * ch + (16 if with_labels else 0)
    lane = iota((rows, cz), 1)
    upper = pick(zrecv, False, even_z, 0, rows)
    lower = pick(zrecv, True, even_z, 0, rows)
    strip_out[...] = jnp.where(
        lane % STRIP < HALO, upper.astype(F32), lower.astype(F32)
    ).astype(BF16)
    if with_labels:
        (codes,) = refs
        codes[...] = jnp.zeros_like(codes)
        codes[:16, :] = strip_out[cx * ch:, :].astype(F32)
    slab, edge = x_sizes(dims, width)
    for which in range(nx):
        upward = even_x if which == 0 else 1 - even_x
        x0 = upward * (cx - width)
        send = sends[which]
        send[:slab, :] = main[pl.ds(pl.multiple_of(x0 * (cy * ch), 16), slab), :].astype(BF16)
        x0 = upward * (cx - width + 1)
        send[slab:slab + edge, :] = strip_out[pl.ds(pl.multiple_of(x0 * ch, 16), edge), :]
        if with_labels:
            start = slab + edge
            x0 = upward * (cx - HALO)
            send[start:start + HALO * cy, :] = (
                small[pl.ds(pl.multiple_of(INCIDENT + ch + x0 * cy, 8), HALO * cy), :]
            ).astype(BF16)
            send[start + HALO * cy:, :] = codes[pl.ds(x0, 16), :].astype(BF16)


def third_kernel(dims, width, with_labels, nx, ny, place, *refs):
    cx, cy, cz, ch, nodes = dims
    main, refs = refs[0], refs[1:]
    if with_labels:
        small, refs = refs[0], refs[1:]
    strip, refs = refs[0], refs[1:]
    xrecv, refs = refs[:nx], refs[nx:]
    sends, refs = refs[:ny], refs[ny:]
    even_x = 1 - place[0] % 2
    even_y = 1 - place[1] % 2
    slab, edge = x_sizes(dims, width)
    if with_labels:
        codes, strip_codes, picked = refs
        fill_codes(dims, small, strip, xrecv, slab + edge, even_x, codes, strip_codes)
    for which in range(ny):
        send = sends[which]
        upward = even_y if which == 0 else 1 - even_y
        start = 0
        for d in range(1, width + 1):
            y = d - 1 + upward * (cy - 2 * d + 1)
            for x in range(d - width, cx + width - d):
                if 0 <= x < cx:
                    at = pl.multiple_of((x * cy + y) * ch, 16)
                    piece = main[pl.ds(at, ch), :].astype(BF16)
                else:
                    at = pl.multiple_of(((x + width if x < 0 else x - cx) * cy + y) * ch, 16)
                    piece = pick(xrecv, x < 0, even_x, at, ch)
                send[start:start + ch, :] = piece
                start += ch
        side = (width - 2) * ch
        send[start:start + side, :] = pick(xrecv, True, even_x, slab + edge - side, side)
        send[start + side:start + side + cx * ch, :] = strip[:cx * ch, :]
        start += side + cx * ch
        send[start:start + side, :] = pick(xrecv, False, even_x, slab, side)
        start += side
        if with_labels:
            y0 = upward * (cy - HALO)
            tall = cx + 2 * HALO
            for x in range(tall):
                picked[x * HALO:(x + 1) * HALO, :] = codes[pl.ds(x * cy + y0, HALO), :]
            send[start:start + tall * HALO, :] = picked[...].astype(BF16)
            send[start + tall * HALO:, :] = strip_codes[...].astype(BF16)


def fill_codes(dims, small, strip, xrecv, start, even_x, codes, strip_codes):
    cx, cy, cz, ch, nodes = dims
    side = HALO * cy
    codes[:side, :] = pick(xrecv, True, even_x, start, side).astype(F32)
    codes[side:side + cx * cy, :] = small[INCIDENT + ch:, :]
    codes[side + cx * cy:, :] = pick(xrecv, False, even_x, start, side).astype(F32)
    strip_codes[:HALO, :] = pick(xrecv, True, even_x, start + side, 16).astype(F32)[:HALO]
    strip_codes[HALO:HALO + cx, :] = strip[cx * ch:cx * ch + 16, :].astype(F32)[:cx]
    strip_codes[HALO + cx:, :] = pick(xrecv, False, even_x, start + side, 16).astype(F32)[:HALO]


def assemble(dims, width, main, strip, xrecv, yrecv, even_x, even_y, put, out_strip):
    cx, cy, cz, ch, nodes = dims
    slab, edge = x_sizes(dims, width)
    blocks, y_edge = y_sizes(dims, width)
    column = cy * ch
    for x in range(cx):
        put(HALO + x, HALO, main[x * column:(x + 1) * column, :].reshape(cy, ch, cz))
    for low in (True, False):
        x0 = HALO - width if low else HALO + cx
        for i in range(width):
            got = pick(xrecv, low, even_x, i * column, column).astype(F32)
            put(x0 + i, HALO, got.reshape(cy, ch, cz))
        start = 0
        for d, size in enumerate(blocks, 1):
            got = pick(yrecv, low, even_y, start, size).astype(F32).reshape(size // ch, 1, ch, cz)
            for i in range(size // ch):
                put(HALO + d - width + i, HALO - d if low else HALO + cy + d - 1, got[i])
            start += size
    own = jnp.concatenate(
        [
            pick(xrecv, True, even_x, slab, edge),
            strip[:cx * ch, :],
            pick(xrecv, False, even_x, slab, edge),
        ],
        axis=0,
    ).astype(F32)
    blank = jnp.zeros((ch, cz), F32)
    low, high = (
        jnp.concatenate([blank, pick(yrecv, low, even_y, start, y_edge).astype(F32), blank], axis=0)
        for low in (True, False)
    )
    full = join_strips(own, low, high, cy)
    out_strip[HALO - width + 1:HALO + cx + width - 1] = full.reshape(cx + 2 * width - 2, ch, cz)


def join_strips(own, low, high, cy):
    lane = iota(own.shape, 1)
    shift = cy * STRIP
    lanes = own.shape[1]
    low = pltpu.roll(low, lanes - shift, 1)
    high = pltpu.roll(high, shift, 1)
    return jnp.where(
        lane < HALO * STRIP, low, jnp.where(lane < (HALO + cy) * STRIP, own, high)
    )


def coefficient(dims, state, k, at):
    cx, cy, cz, ch, nodes = dims
    at += cx * cy * ch + held_rows(dims)[1] * k
    return jnp.broadcast_to(state[at:at + 1, :], (ch, cz))


def sweep(dims, reach, weight, src, src_strip, dst, dst_strip, r, r_strip, state, c_strip):
    cx, cy, cz, ch, nodes = dims
    lane = iota((ch, cz), 1)
    first, last = lane == 0, lane == cz - 1
    k = lane % STRIP
    group = lane // STRIP
    touching = (k == HALO) | (k == HALO - 1)

    def column(x):
        far = layers_left(dims, x, reach)
        low, high = HALO - far, HALO + cy + far
        beyond = src_strip[x]
        ends = jnp.zeros_like(beyond)
        behind, here = src[x, low - 1], src[x, low]
        for y in range(low, high):
            ahead = src[x, y + 1]
            edge = pltpu.roll(beyond, (2 * cz - (y * STRIP + HALO)) % cz, 1)
            above = jnp.where(last, edge, pltpu.roll(here, cz - 1, 1))
            below = jnp.where(first, edge, pltpu.roll(here, 1, 1))
            at = row_of(dims, x, y)
            total = r[at * ch:(at + 1) * ch, :] - here
            total += coefficient(dims, state, 0, at) * src[x + 1, y]
            total += coefficient(dims, state, 1, at) * src[x - 1, y]
            total += coefficient(dims, state, 2, at) * ahead
            total += coefficient(dims, state, 3, at) * behind
            total += coefficient(dims, state, 4, at) * above
            total += coefficient(dims, state, 5, at) * below
            dst[x, y] = here + weight * total
            if far > 0 and low < y < high - 1:
                moved = pltpu.roll(here, (y * STRIP + HALO) % cz, 1)
                ends = jnp.where(touching & (group == y), moved, ends)
            behind, here = here, ahead
        if far > 0:
            strip_column(x, beyond, ends)

    def strip_column(x, here, ends):
        def spread_strip(k):
            return jnp.broadcast_to(c_strip[k, x:x + 1, :], (ch, cz))

        above = jnp.where(k == HALO, ends, pltpu.roll(here, 1, 1))
        below = jnp.where(k == HALO - 1, ends, pltpu.roll(here, cz - 1, 1))
        total = r_strip[x] - here
        total += spread_strip(0) * src_strip[x + 1]
        total += spread_strip(1) * src_strip[x - 1]
        total += spread_strip(2) * pltpu.roll(here, cz - STRIP, 1)
        total += spread_strip(3) * pltpu.roll(here, STRIP, 1)
        total += spread_strip(4) * above
        total += spread_strip(5) * below
        dst_strip[x] = here + weight * total

    for x in range(HALO - reach, HALO + cx + reach):
        column(x)


def coefficients(dims, kc, kc_strip, state, c_strip):
    cx, cy, cz, ch, nodes = dims
    tx, ty = cx + 2 * HALO, cy + 2 * HALO
    lane = iota((ty, cz), 1)
    y = iota((ty, cz), 0)
    here = kc_strip[8:8 + tx, :]
    group = lane // STRIP
    k = lane % STRIP
    touching = ((k == HALO) | (k == HALO - 1)) & (group == y)
    starts, total = held_rows(dims)
    ends = [jnp.zeros((1, cz), F32)]
    for x in range(1, tx - 1):
        own = kc[x + 1, 8:8 + ty, :]
        moved = pltpu.roll(own, HALO, 1, stride=STRIP, stride_axis=0)
        ends.append(jnp.sum(jnp.where(touching, moved, 0.0), axis=0, keepdims=True))
        beyond = jnp.broadcast_to(kc_strip[8 + x:9 + x, :], (ty, cz))
        upper = jnp.where((group == y) & (k == HALO - 1), beyond, 0.0).sum(axis=1, keepdims=True)
        lower = jnp.where((group == y) & (k == HALO), beyond, 0.0).sum(axis=1, keepdims=True)
        others = [
            kc[x + 2, 8:8 + ty, :],
            kc[x, 8:8 + ty, :],
            kc[x + 1, 9:9 + ty, :],
            kc[x + 1, 7:7 + ty, :],
            jnp.where(lane == cz - 1, upper, pltpu.roll(own, cz - 1, 1)),
            jnp.where(lane == 0, lower, pltpu.roll(own, 1, 1)),
        ]
        first, y0, y1 = starts[x]
        for i, value in enumerate(finish(own, others)):
            at = cx * cy * ch + total * i + first
            state[at:at + y1 - y0, :] = value[y0:y1, :]
    ends = jnp.concatenate(ends + [jnp.zeros((1, cz), F32)], axis=0)
    lane = iota((tx, cz), 1)
    k = lane % STRIP
    others = [
        kc_strip[9:9 + tx, :],
        kc_strip[7:7 + tx, :],
        pltpu.roll(here, cz - STRIP, 1),
        pltpu.roll(here, STRIP, 1),
        jnp.where(k == HALO, ends, pltpu.roll(here, 1, 1)),
        jnp.where(k == HALO - 1, ends, pltpu.roll(here, cz - 1, 1)),
    ]
    for i, value in enumerate(finish(here, others)):
        c_strip[i] = value


def finish(own, others):
    faces = [0.5 * (own + other) for other in others]
    diag = MASS_TERM + faces[0]
    for face in faces[1:]:
        diag = diag + face
    inverse = jnp.where(own > 0.0, 1.0 / diag, 0.0)
    return [face * inverse for face in faces] + [inverse]


def smooth(dims, start, fields, strips, r, r_strip, state, c_strip):
    weights = sweep_weights(SWEEPS)
    now = 0
    for number in range(start, SWEEPS):
        sweep(
            dims, SWEEPS - 1 - number, weights[number], fields[now], strips[now],
            fields[1 - now], strips[1 - now], r, r_strip, state, c_strip,
        )
        now = 1 - now
    return fields[now]


def gather_nodes(dims, field, row, z):
    cx, cy, cz, ch, nodes = dims
    hits = (iota((cz, nodes), 0) == z).astype(BF16)
    rows = field[HALO:HALO + cx, HALO:HALO + cy].reshape(cx * cy * ch, cz).astype(BF16)
    at_z = jnp.dot(rows, hits, preferred_element_type=F32)
    total = jnp.zeros((ch, nodes), F32)
    for r in range(cx * cy):
        here = jnp.broadcast_to(row == r, (ch, nodes))
        total = jnp.where(here, at_z[r * ch:(r + 1) * ch], total)
    return total.astype(BF16)


def fourth_kernel(dims, regions, nx, ny, place, main, small, strip, *refs):
    cx, cy, cz, ch, nodes = dims
    xrecv, yrecv, refs = refs[:nx], refs[nx:nx + ny], refs[nx + ny:]
    field_out, block_out, send_out, state, kept, c_strip, refs = *refs[:6], refs[6:]
    r, r_strip, fa, fb, sa, sb, kc, kc_strip, codes, strip_codes, side_codes = refs
    even_x = 1 - place[0] % 2
    even_y = 1 - place[1] % 2
    tx, ty = cx + 2 * HALO, cy + 2 * HALO
    width = RHS_HALO
    slab, edge = x_sizes(dims, width)
    blocks, y_edge = y_sizes(dims, width)

    fill_codes(
        dims, small, strip, xrecv, slab + edge, even_x, codes, strip_codes
    )
    kc[...] = jnp.zeros_like(kc)
    kc_strip[...] = jnp.zeros_like(kc_strip)

    def conductivity(code):
        value = jnp.zeros_like(code)
        for region in range(regions):
            coeff = jnp.broadcast_to(small[REGION:REGION + 1, region:region + 1], code.shape)
            value = jnp.where(code == region + 1, coeff, value)
        return value

    kc[1:1 + tx, 8 + HALO:8 + HALO + cy] = conductivity(codes[...]).reshape(tx, cy, cz)
    start = sum(blocks) + y_edge
    for low in (True, False):
        got = pick(yrecv, low, even_y, start, tx * HALO).astype(F32)
        side_codes[...] = conductivity(got)
        y0 = 8 if low else 8 + HALO + cy
        for x in range(tx):
            kc[1 + x, y0:y0 + HALO, :] = side_codes[x * HALO:(x + 1) * HALO, :]
    start += tx * HALO
    low = pick(yrecv, True, even_y, start, 16).astype(F32)
    high = pick(yrecv, False, even_y, start, 16).astype(F32)
    kc_strip[8:8 + tx, :] = conductivity(join_strips(strip_codes[...], low, high, cy))
    coefficients(dims, kc, kc_strip, state, c_strip)

    r_strip[...] = jnp.zeros_like(r_strip)
    weight = sweep_weights(SWEEPS)[0]

    def put(x, y, rows):
        for i in range(rows.shape[0]):
            at = row_of(dims, x, y + i)
            value = rows[i] * coefficient(dims, state, 6, at)
            r[at * ch:(at + 1) * ch, :] = value
            fa[x, y + i] = weight * value
            inside, at = kept_row(dims, x, y + i)
            if inside:
                state[at * ch:(at + 1) * ch, :] = value
            else:
                kept[at * ch:(at + 1) * ch, :] = rows[i].astype(BF16)

    assemble(dims, width, main, strip, xrecv, yrecv, even_x, even_y, put, r_strip)
    tx = cx + 2 * HALO
    kept[kept.shape[0] - tx * ch:, :] = r_strip[...].reshape(tx * ch, cz).astype(BF16)
    for x in range(HALO - width, HALO + cx + width):
        value = r_strip[x] * jnp.broadcast_to(c_strip[6, x:x + 1, :], (ch, cz))
        r_strip[x] = value
        sa[x] = weight * value
    field = smooth(dims, 1, (fa, fb), (sa, sb), r, r_strip, state, c_strip)

    field_out[...] = field[HALO:HALO + cx, HALO:HALO + cy].reshape(cx * cy * ch, cz)
    send_out[...] = strip_rows(lambda x, y: field[HALO + x, HALO + y], cx, cy, cz)
    row, z = node_places(small)
    traces = gather_nodes(dims, field, row, z)
    rows = []
    for axis in range(3):
        value = small[axis:axis + 1, :]
        for _ in range(3):
            part = value.astype(BF16).astype(F32)
            rows.append(part)
            value = value - part
    rows += [row.astype(F32), z.astype(F32), jnp.zeros((5, nodes), F32)]
    rest = jnp.concatenate(rows, axis=0).astype(BF16)
    for other in range(block_out.shape[0]):
        block_out[other, :ch, :] = traces
        block_out[other, ch:, :] = rest


def tile_kernel(dims, count, scale, small, recv, tiles):
    cx, cy, cz, ch, nodes = dims
    own = [jnp.broadcast_to(small[k:k + 1, :], (nodes, nodes)).T for k in range(3)]

    def block(b, _):
        parts = recv[b, ch:ch + 16, :].astype(F32)
        squared = None
        for k in range(3):
            other = parts[3 * k:3 * k + 1] + parts[3 * k + 1:3 * k + 2] + parts[3 * k + 2:3 * k + 3]
            delta = own[k] - jnp.broadcast_to(other, (nodes, nodes))
            squared = delta * delta if squared is None else squared + delta * delta
        tile = (scale * lax.rsqrt(squared + SOFTENING * SOFTENING)).astype(BF16)
        tiles[:, pl.ds(pl.multiple_of(b * nodes, nodes), nodes)] = tile
        return _

    lax.fori_loop(0, count, block, 0)


def boundary_kernel(dims, count, scale, small, recv, sum_out, half_out, tiles):
    tile_kernel(dims, count, scale, small, recv, tiles)
    total = product(recv, tiles, count, dims)
    sum_out[...] = total
    for other in range(count):
        half_out[other] = total.astype(BF16)


def product(recv, tiles, count, dims):
    cx, cy, cz, ch, nodes = dims
    group = math.gcd(count, 32)

    def part(at):
        traces = jnp.concatenate([recv[at + i, :ch, :] for i in range(group)], axis=1)
        start = at * nodes
        if not isinstance(at, int):
            start = pl.multiple_of(start, nodes)
        return lax.dot_general(
            traces, tiles[:, pl.ds(start, group * nodes)], NT, preferred_element_type=F32
        )

    if group == count:
        return part(0)
    return lax.fori_loop(
        0, count // group, lambda i, total: total + part(i * group), jnp.zeros((ch, nodes), F32)
    )


def last_kernel(dims, count, small, recv, tiles, flux_out):
    cx, cy, cz, ch, nodes = dims
    incident = small[INCIDENT:INCIDENT + ch, :]
    flux_out[...] = incident + product(recv, tiles, count, dims)


def fifth_kernel(dims, sizes, nx, ny, place, main, sums, small, recv, blocks, strip, *refs):
    cx, cy, cz, ch, nodes = dims
    xrecv, yrecv, refs = refs[:nx], refs[nx:nx + ny], refs[nx + ny:]
    state, kept, c_strip, refs = *refs[:3], refs[3:]
    field_out, block_out, refs = *refs[:2], refs[2:]
    r, r_strip, fa, fb, sa, sb, left = refs
    even_x = 1 - place[0] % 2
    even_y = 1 - place[1] % 2
    width = RHS_HALO
    tx = cx + 2 * HALO
    for x in range(tx):
        at = kept.shape[0] - (tx - x) * ch
        r_strip[x] = kept[at:at + ch, :].astype(F32) * jnp.broadcast_to(
            c_strip[6, x:x + 1, :], (ch, cz)
        )
    sa[...] = jnp.zeros_like(sa)

    def put(x, y, rows):
        fa[x, y:y + rows.shape[0]] = rows

    assemble(dims, HALO, main, strip, xrecv, yrecv, even_x, even_y, put, sa)

    def neighbour(dx, dy, dz):
        at = [place[i] + d for i, d in enumerate((dx, dy, dz))]
        good = None
        for i, size in enumerate(sizes):
            ok = (at[i] >= 0) & (at[i] < size)
            good = ok if good is None else good & ok
            at[i] = jnp.clip(at[i], 0, size - 1)
        index = (at[0] * sizes[1] + at[1]) * sizes[2] + at[2]
        info = blocks[index, ch:ch + 16, :].astype(F32)
        good = jnp.full((1, nodes), good.astype(jnp.int32), jnp.int32) > 0
        row = jnp.where(good, info[9:10].astype(jnp.int32), -1)
        return recv[index].astype(F32), row, info[10:11].astype(jnp.int32)

    spans = {
        -1: (HALO - width, HALO, cx), 0: (HALO, HALO + cx, 0), 1: (HALO + cx, HALO + cx + width, -cx),
    }
    own_row, own_z = node_places(small)
    strip_lane = iota((cz, nodes), 0)
    starts = held_rows(dims)[0]
    for dx in (-1, 0, 1):
        x0, x1, back_x = spans[dx]
        edge = []
        hits_edge = []
        for dy in (-1, 0, 1):
            y0, y1, back_y = spans[dy]
            parts = []
            if dx == 0 and dy == 0:
                top = sums[...].astype(BF16).astype(F32)
                row, z = own_row, own_z
                parts = [top, sums[...] - top]
            else:
                value, row, z = neighbour(dx, dy, 0)
                parts = [value]
            hits = (iota((cz, nodes), 0) == z).astype(BF16)
            hits = jnp.concatenate([hits] * len(parts), axis=1)
            cells = [
                (x, y) for x in range(x0, x1) for y in range(y0, y1)
                if starts[x][1] <= y < starts[x][2]
            ]
            for at, (x, y) in enumerate(cells):
                wanted = (x - HALO + back_x) * cy + (y - HALO + back_y)
                here = jnp.broadcast_to(row == wanted, (ch, nodes))
                for i, value in enumerate(parts):
                    left[at * ch:(at + 1) * ch, i * nodes:(i + 1) * nodes] = jnp.where(
                        here, value, 0.0
                    ).astype(BF16)
            added = lax.dot_general(
                left[:len(cells) * ch, :len(parts) * nodes], hits, NT, preferred_element_type=F32
            )
            for i, (x, y) in enumerate(cells):
                at = row_of(dims, x, y)
                inverse = coefficient(dims, state, 6, at)
                more = added[i * ch:(i + 1) * ch]
                inside, old = kept_row(dims, x, y)
                if inside:
                    value = state[old * ch:(old + 1) * ch, :] + more * inverse
                else:
                    value = (kept[old * ch:(old + 1) * ch, :].astype(F32) + more) * inverse
                r[at * ch:(at + 1) * ch, :] = value
            for dz in (-1, 1):
                value, row, z = neighbour(dx, dy, dz)
                y = row % cy + cy * dy + HALO
                k = HALO - 1 - z if dz > 0 else HALO + cz - 1 - z
                good = (row >= 0) & (y >= 0) & (y < cy + 2 * HALO) & (k >= 0) & (k < STRIP)
                good = good & ((k < HALO) if dz > 0 else (k >= HALO))
                lane = jnp.where(good, y * STRIP + k, -1)
                hits_edge.append((strip_lane == lane).astype(BF16))
                edge.append((value, jnp.where(row >= 0, row // cy, -1)))
        for x in range(x0, x1):
            at = (x - x0) * ch
            for i, (value, node_x) in enumerate(edge):
                here = jnp.broadcast_to(node_x == x - HALO + back_x, (ch, nodes))
                left[at:at + ch, i * nodes:(i + 1) * nodes] = jnp.where(here, value, 0.0).astype(BF16)
        added = lax.dot_general(
            left[:(x1 - x0) * ch, :len(edge) * nodes], jnp.concatenate(hits_edge, axis=1), NT,
            preferred_element_type=F32,
        )
        for x in range(x0, x1):
            inverse = jnp.broadcast_to(c_strip[6, x:x + 1, :], (ch, cz))
            r_strip[x] += added[(x - x0) * ch:(x - x0 + 1) * ch] * inverse

    field = smooth(dims, 0, (fa, fb), (sa, sb), r, r_strip, state, c_strip)
    for x in range(cx):
        for y in range(cy):
            field_out[pl.ds(x * cy + y, ch, stride=cx * cy), :] = field[HALO + x, HALO + y]
    traces = gather_nodes(dims, field, own_row, own_z)
    for other in range(block_out.shape[0]):
        block_out[other] = traces


def per_device(source, labels, region_coeff, node_cell, node_pos, incident):
    ch, cx, cy, cz = source.shape
    nodes = node_cell.shape[0]
    dims = (cx, cy, cz, ch, nodes)
    sizes = tuple(lax.axis_size(axis) for axis in AXES)
    count = math.prod(sizes)
    nx, ny, nz = (2 if size > 2 else 1 for size in sizes)
    scale = KERNEL_GAIN / math.sqrt(nodes * count)
    tx, ty = cx + 2 * HALO, cy + 2 * HALO
    held = held_rows(dims)[1]
    place = jnp.stack([lax.axis_index(axis) for axis in AXES]).astype(jnp.int32)
    rows = cx * cy * ch
    flat = source.reshape(ch * cx * cy, cz)
    marks = labels.reshape(cx * cy, cz)
    cells = node_cell.reshape(1, nodes)
    shape = jax.ShapeDtypeStruct
    vmem = pltpu.VMEM

    height = INCIDENT + ch + cx * cy
    small = jnp.zeros((height, cz), F32)
    for value, row in (
        (node_pos, 0),
        ((cells // cz).astype(F32), ROW),
        ((cells % cz).astype(F32), LAYER),
        (region_coeff[None], REGION),
        (incident, INCIDENT),
        ((marks + 1).astype(F32), INCIDENT + ch),
    ):
        sides = ((row, height - row - value.shape[0], 0), (0, cz - value.shape[1], 0))
        small += lax.pad(value, jnp.float32(0), sides)
    rhs, send = kernel_call(
        functools.partial(first_kernel, dims),
        (shape((rows, cz), F32), shape((cx * ch + 16, cz), BF16)),
        [vmem((rows, 2 * nodes), BF16)],
        operands=(flat, small),
        name="scatter_first",
    )

    def halo(main, send, width, with_labels, between=(lambda x: x, lambda x: x)):
        zrecv = exchange(send, "col")
        zrecv = between[0](zrecv)
        extra = HALO * cy + 16 if with_labels else 0
        strip_rows_ = cx * ch + (16 if with_labels else 0)
        own = (main, small) if with_labels else (main,)
        strip, *sends = kernel_call(
            functools.partial(second_kernel, dims, width, with_labels, nz, nx),
            (shape((strip_rows_, cz), BF16),)
            + (shape((sum(x_sizes(dims, width)) + extra, cz), BF16),) * nx,
            [vmem((32, cz), F32)] if with_labels else [],
            smem=1,
            operands=(place, *own, *zrecv),
            name="pack_x",
        )
        xrecv = exchange(None, "vol", sends)
        xrecv = between[1](xrecv)
        extra = tx * HALO + 16 if with_labels else 0
        blocks, y_edge = y_sizes(dims, width)
        sends = kernel_call(
            functools.partial(third_kernel, dims, width, with_labels, nx, ny),
            (shape((sum(blocks) + y_edge + extra, cz), BF16),) * ny,
            [vmem((tx * cy, cz), F32), vmem((tx, cz), F32), vmem((tx * HALO, cz), F32)]
            if with_labels else [],
            smem=1,
            operands=(place, *own, strip, *xrecv),
            name="pack_y",
        )
        yrecv = exchange(None, "row", sends)
        return strip, xrecv, yrecv

    strip, xrecv, yrecv = halo(rhs, send, RHS_HALO, True)
    field, block, send, state, kept, c_strip = kernel_call(
        functools.partial(fourth_kernel, dims, region_coeff.shape[0], nx, ny),
        (
            shape((rows, cz), F32),
            shape((count, ch + 16, nodes), BF16),
            shape((cx * ch, cz), BF16),
            shape((rows + 7 * held, cz), F32),
            shape(((held - cx * cy + tx) * ch, cz), BF16),
            shape((7, tx, cz), F32),
        ),
        [
            vmem((held * ch, cz), F32),
            vmem((tx, ch, cz), F32),
            vmem((tx, ty, ch, cz), F32),
            vmem((tx, ty, ch, cz), F32),
            vmem((tx, ch, cz), F32),
            vmem((tx, ch, cz), F32),
            vmem((tx + 2, ty + 16, cz), F32),
            vmem((tx + 16, cz), F32),
            vmem((tx * cy, cz), F32),
            vmem((tx, cz), F32),
            vmem((tx * HALO, cz), F32),
        ],
        smem=1,
        operands=(place, rhs, small, strip, *xrecv, *yrecv),
        name="sweeps_first",
    )

    def to_all(value):
        return lax.all_to_all(value, AXES, 0, 0, tiled=True)

    blocks = to_all(block)
    sums, half = kernel_call(
        functools.partial(boundary_kernel, dims, count, scale),
        (
            shape((ch, nodes), F32),
            shape((count, ch, nodes), BF16),
        ),
        [vmem((nodes, count * nodes), BF16)],
        operands=(small, blocks),
        name="boundary",
    )

    def after_boundary(arrays):
        return lax.optimization_barrier((arrays, half))[0]

    strip, xrecv, yrecv = halo(field, send, HALO, False, (lambda x: x, after_boundary))
    recv = to_all(half)
    field, block = kernel_call(
        functools.partial(fifth_kernel, dims, sizes, nx, ny),
        (shape((ch * cx * cy, cz), F32), shape((count, ch, nodes), BF16)),
        [
            vmem((held * ch, cz), F32),
            vmem((tx, ch, cz), F32),
            vmem((tx, ty, ch, cz), F32),
            vmem((tx, ty, ch, cz), F32),
            vmem((tx, ch, cz), F32),
            vmem((tx, ch, cz), F32),
            vmem((rows, 6 * nodes), BF16),
        ],
        smem=1,
        operands=(
            place, field, sums, small, recv, blocks, strip, *xrecv, *yrecv, state, kept, c_strip
        ),
        name="sweeps_last",
    )
    blocks, block = lax.optimization_barrier((blocks, block))
    tiles = kernel_call(
        functools.partial(tile_kernel, dims, count, scale),
        shape((nodes, count * nodes), BF16),
        operands=(small, blocks),
        cost=pl.CostEstimate(flops=10**9, bytes_accessed=10**6, transcendentals=10**6),
        name="tiles_last",
    )
    flux = kernel_call(
        functools.partial(last_kernel, dims, count),
        shape((ch, nodes), F32),
        operands=(small, to_all(block), tiles),
        name="flux_last",
    )
    return field.reshape(source.shape), flux


def solution(mesh):
    placed = (
        P(None, "vol", "row", "col"),
        P("vol", "row", "col"),
        P(),
        P(("vol", "row", "col")),
        P(None, ("vol", "row", "col")),
        P(None, ("vol", "row", "col")),
    )
    return jax.shard_map(
        per_device,
        mesh=mesh,
        in_specs=placed,
        out_specs=(P(None, "vol", "row", "col"), P(None, ("vol", "row", "col"))),
        check_vma=False,
    )
```

```python
import functools
import math

import jax
import jax.numpy as jnp
from jax import lax
from jax.experimental import pallas as pl
from jax.experimental.pallas import tpu as pltpu
from jax.sharding import PartitionSpec as P

SWEEPS = 4
ITERS = 2

MASS_TERM = 0.05
SOFTENING = 0.05
KERNEL_GAIN = 2.0

HALO = SWEEPS
RHS_HALO = SWEEPS - 1
STRIP = 2 * HALO
AXES = ("vol", "row", "col")
F32, BF16 = jnp.float32, jnp.bfloat16
CELL, REGION, INCIDENT = 3, 4, 8
SPARE = 4 * 1024 * 1024
NT = (((1,), (1,)), ((), ()))


def sweep_weights(count):
    return [
        1.0 / (1.05 - 0.95 * math.cos(math.pi * (2 * sweep + 1) / (2 * count)))
        for sweep in range(count)
    ]


def iota(shape, dim):
    return lax.broadcasted_iota(jnp.int32, shape, dim)


def kernel_call(body, out_shape, scratch=(), smem=0, operands=(), cost=None, name=None):
    held = [jnp.shape(leaf) + (leaf.dtype,) for leaf in jax.tree.leaves((out_shape, operands))]
    held += [ref.shape + (ref.dtype,) for ref in scratch]
    need = sum(math.prod(entry[:-1]) * jnp.dtype(entry[-1]).itemsize for entry in held)
    specs = [pl.BlockSpec(memory_space=pltpu.SMEM)] * smem
    specs += [pl.BlockSpec(memory_space=pltpu.VMEM)] * (len(operands) - smem)
    return pl.pallas_call(
        body,
        out_shape=out_shape,
        in_specs=specs,
        out_specs=jax.tree.map(lambda _: pl.BlockSpec(memory_space=pltpu.VMEM), out_shape),
        scratch_shapes=list(scratch),
        compiler_params=pltpu.CompilerParams(vmem_limit_bytes=need + SPARE),
        cost_estimate=cost,
        name=name,
    )(*operands)


def layers_left(dims, x, reach):
    cx = dims[0]
    return reach - max(HALO - x, x - (HALO + cx - 1), 0)


@functools.lru_cache
def held_rows(dims):
    cx, cy, cz, ch, nodes = dims
    starts, total = {}, 0
    for x in range(cx + 2 * HALO):
        far = layers_left(dims, x, RHS_HALO)
        if far >= 0:
            starts[x] = (total, HALO - far, HALO + cy + far)
            total += cy + 2 * far
    return starts, total


def row_of(dims, x, y):
    first, y0, y1 = held_rows(dims)[0][x]
    return first + y - y0


@functools.lru_cache(maxsize=None)
def kept_row(dims, x, y):
    cx, cy, cz, ch, nodes = dims
    starts, total = held_rows(dims)
    if HALO <= x < HALO + cx and HALO <= y < HALO + cy:
        return True, (x - HALO) * cy + y - HALO
    before = 0
    for other in sorted(starts):
        first, y0, y1 = starts[other]
        for at in range(y0, y1):
            if (other, at) == (x, y):
                return False, before
            before += not (HALO <= other < HALO + cx and HALO <= at < HALO + cy)
    raise KeyError(x, y)


def x_sizes(dims, width):
    cx, cy, cz, ch, nodes = dims
    return width * cy * ch, (width - 1) * ch


def y_sizes(dims, width):
    cx, cy, cz, ch, nodes = dims
    return [(cx + 2 * (width - d)) * ch for d in range(1, width + 1)], (cx + 2 * (width - 2)) * ch


def pick(refs, low, even, rows, size):
    first = refs[0][pl.ds(rows, size), :]
    second = refs[1][pl.ds(rows, size), :] if len(refs) > 1 else jnp.zeros_like(first)
    flag = jnp.full(first.shape, even, jnp.int32).astype(first.dtype)
    mine, other = (1 - flag, flag) if low else (flag, 1 - flag)
    return first * mine + second * other


def exchange(array, axis, arrays=None):
    count = lax.axis_size(axis)
    arrays = arrays or [array] * 2
    out = []
    for which in range(2 if count > 2 else 1):
        pairs = []
        for i in range(which, count - 1, 2):
            pairs += [(i, i + 1), (i + 1, i)]
        out.append(lax.ppermute(arrays[which], axis, pairs))
    return out


def edge_picker(cz, lanes):
    z, lane = iota((cz, lanes), 0), iota((cz, lanes), 1)
    k = lane % STRIP
    wanted = jnp.where(k < HALO, HALO - 1 - k, cz - 1 - k + HALO)
    return (z == wanted).astype(F32), lane // STRIP - HALO


def strip_rows(read, cx, cy, cz):
    base, lane_y = edge_picker(cz, cz)
    total = None
    for y in range(cy):
        rows = jnp.concatenate([read(x, y).astype(BF16) for x in range(cx)], axis=0)
        picked = jnp.where(lane_y == y, base, 0.0).astype(BF16)
        part = jnp.dot(rows, picked, preferred_element_type=F32)
        total = part if total is None else total + part
    return total.astype(BF16)


def node_places(small):
    cell = small[CELL:CELL + 1, :].astype(jnp.int32)
    cz = small.shape[1]
    return cell // cz, cell % cz


def first_kernel(dims, source, small, rhs_out, send_out, left):
    cx, cy, cz, ch, nodes = dims
    row, z = node_places(small)
    hits = (iota((cz, nodes), 0) == z).astype(BF16)
    flux = small[INCIDENT:INCIDENT + ch, :]
    top = flux.astype(BF16).astype(F32)
    rest = flux - top
    for r in range(cx * cy):
        here = jnp.broadcast_to(row == r, (ch, nodes))
        left[r * ch:(r + 1) * ch, :nodes] = jnp.where(here, top, 0.0).astype(BF16)
        left[r * ch:(r + 1) * ch, nodes:] = jnp.where(here, rest, 0.0).astype(BF16)
    added = lax.dot_general(
        left[...], jnp.concatenate([hits, hits], axis=1), NT, preferred_element_type=F32
    )
    rhs_out[...] = added
    for r in range(cx * cy):
        rhs_out[r * ch:(r + 1) * ch, :] += source[pl.ds(r, ch, stride=cx * cy), :]

    def read(x, y):
        start = (x * cy + y) * ch
        return rhs_out[start:start + ch, :]

    send_out[:cx * ch, :] = strip_rows(read, cx, cy, cz)
    base, lane_y = edge_picker(cz, cz)
    codes = (small[INCIDENT + ch:, :] + 1.0).astype(BF16)
    strips = jnp.dot(codes, base.astype(BF16), preferred_element_type=F32)
    own = (iota(strips.shape, 0) % cy) == lane_y[:1, :]
    strips = jnp.where(own, strips, 0.0).reshape(cx, cy, cz).sum(axis=1)
    send_out[cx * ch:, :] = jnp.concatenate(
        [strips, jnp.zeros((16 - cx, cz), F32)], axis=0
    ).astype(BF16)


def second_kernel(dims, width, with_labels, nz, nx, place, *refs):
    cx, cy, cz, ch, nodes = dims
    main, refs = refs[0], refs[1:]
    if with_labels:
        small, refs = refs[0], refs[1:]
    zrecv, refs = refs[:nz], refs[nz:]
    strip_out, sends, refs = refs[0], refs[1:1 + nx], refs[1 + nx:]
    even_x = 1 - place[0] % 2
    even_z = 1 - place[2] % 2
    rows = cx * ch + (16 if with_labels else 0)
    lane = iota((rows, cz), 1)
    upper = pick(zrecv, False, even_z, 0, rows)
    lower = pick(zrecv, True, even_z, 0, rows)
    strip_out[...] = jnp.where(
        lane % STRIP < HALO, upper.astype(F32), lower.astype(F32)
    ).astype(BF16)
    if with_labels:
        (codes,) = refs
        codes[...] = jnp.zeros_like(codes)
        codes[:16, :] = strip_out[cx * ch:, :].astype(F32)
    slab, edge = x_sizes(dims, width)
    for which in range(nx):
        upward = even_x if which == 0 else 1 - even_x
        x0 = upward * (cx - width)
        send = sends[which]
        send[:slab, :] = main[pl.ds(pl.multiple_of(x0 * (cy * ch), 16), slab), :].astype(BF16)
        x0 = upward * (cx - width + 1)
        send[slab:slab + edge, :] = strip_out[pl.ds(pl.multiple_of(x0 * ch, 16), edge), :]
        if with_labels:
            start = slab + edge
            x0 = upward * (cx - HALO)
            send[start:start + HALO * cy, :] = (
                small[pl.ds(pl.multiple_of(INCIDENT + ch + x0 * cy, 8), HALO * cy), :] + 1.0
            ).astype(BF16)
            send[start + HALO * cy:, :] = codes[pl.ds(x0, 16), :].astype(BF16)


def third_kernel(dims, width, with_labels, nx, ny, place, *refs):
    cx, cy, cz, ch, nodes = dims
    main, refs = refs[0], refs[1:]
    if with_labels:
        small, refs = refs[0], refs[1:]
    strip, refs = refs[0], refs[1:]
    xrecv, refs = refs[:nx], refs[nx:]
    sends, refs = refs[:ny], refs[ny:]
    even_x = 1 - place[0] % 2
    even_y = 1 - place[1] % 2
    slab, edge = x_sizes(dims, width)
    if with_labels:
        codes, strip_codes, picked = refs
        fill_codes(dims, small, strip, xrecv, slab + edge, even_x, codes, strip_codes)
    for which in range(ny):
        send = sends[which]
        upward = even_y if which == 0 else 1 - even_y
        start = 0
        for d in range(1, width + 1):
            y = d - 1 + upward * (cy - 2 * d + 1)
            for x in range(d - width, cx + width - d):
                if 0 <= x < cx:
                    at = pl.multiple_of((x * cy + y) * ch, 16)
                    piece = main[pl.ds(at, ch), :].astype(BF16)
                else:
                    at = pl.multiple_of(((x + width if x < 0 else x - cx) * cy + y) * ch, 16)
                    piece = pick(xrecv, x < 0, even_x, at, ch)
                send[start:start + ch, :] = piece
                start += ch
        side = (width - 2) * ch
        send[start:start + side, :] = pick(xrecv, True, even_x, slab + edge - side, side)
        send[start + side:start + side + cx * ch, :] = strip[:cx * ch, :]
        start += side + cx * ch
        send[start:start + side, :] = pick(xrecv, False, even_x, slab, side)
        start += side
        if with_labels:
            y0 = upward * (cy - HALO)
            tall = cx + 2 * HALO
            for x in range(tall):
                picked[x * HALO:(x + 1) * HALO, :] = codes[pl.ds(x * cy + y0, HALO), :]
            send[start:start + tall * HALO, :] = picked[...].astype(BF16)
            send[start + tall * HALO:, :] = strip_codes[...].astype(BF16)


def fill_codes(dims, small, strip, xrecv, start, even_x, codes, strip_codes):
    cx, cy, cz, ch, nodes = dims
    side = HALO * cy
    codes[:side, :] = pick(xrecv, True, even_x, start, side).astype(F32)
    codes[side:side + cx * cy, :] = small[INCIDENT + ch:, :] + 1.0
    codes[side + cx * cy:, :] = pick(xrecv, False, even_x, start, side).astype(F32)
    strip_codes[:HALO, :] = pick(xrecv, True, even_x, start + side, 16).astype(F32)[:HALO]
    strip_codes[HALO:HALO + cx, :] = strip[cx * ch:cx * ch + 16, :].astype(F32)[:cx]
    strip_codes[HALO + cx:, :] = pick(xrecv, False, even_x, start + side, 16).astype(F32)[:HALO]


def assemble(dims, width, main, strip, xrecv, yrecv, even_x, even_y, put, out_strip):
    cx, cy, cz, ch, nodes = dims
    slab, edge = x_sizes(dims, width)
    blocks, y_edge = y_sizes(dims, width)
    column = cy * ch
    for x in range(cx):
        put(HALO + x, HALO, main[x * column:(x + 1) * column, :].reshape(cy, ch, cz))
    for low in (True, False):
        x0 = HALO - width if low else HALO + cx
        for i in range(width):
            got = pick(xrecv, low, even_x, i * column, column).astype(F32)
            put(x0 + i, HALO, got.reshape(cy, ch, cz))
        start = 0
        for d, size in enumerate(blocks, 1):
            got = pick(yrecv, low, even_y, start, size).astype(F32).reshape(size // ch, 1, ch, cz)
            for i in range(size // ch):
                put(HALO + d - width + i, HALO - d if low else HALO + cy + d - 1, got[i])
            start += size
    own = jnp.concatenate(
        [
            pick(xrecv, True, even_x, slab, edge),
            strip[:cx * ch, :],
            pick(xrecv, False, even_x, slab, edge),
        ],
        axis=0,
    ).astype(F32)
    blank = jnp.zeros((ch, cz), F32)
    low, high = (
        jnp.concatenate([blank, pick(yrecv, low, even_y, start, y_edge).astype(F32), blank], axis=0)
        for low in (True, False)
    )
    full = join_strips(own, low, high, cy)
    out_strip[HALO - width + 1:HALO + cx + width - 1] = full.reshape(cx + 2 * width - 2, ch, cz)


def join_strips(own, low, high, cy):
    lane = iota(own.shape, 1)
    shift = cy * STRIP
    lanes = own.shape[1]
    low = pltpu.roll(low, lanes - shift, 1)
    high = pltpu.roll(high, shift, 1)
    return jnp.where(
        lane < HALO * STRIP, low, jnp.where(lane < (HALO + cy) * STRIP, own, high)
    )


def coefficient(dims, state, k, at):
    cx, cy, cz, ch, nodes = dims
    at += cx * cy * ch + held_rows(dims)[1] * k
    return jnp.broadcast_to(state[at:at + 1, :], (ch, cz))


def sweep(dims, reach, weight, src, src_strip, dst, dst_strip, r, r_strip, state, c_strip):
    cx, cy, cz, ch, nodes = dims
    lane = iota((ch, cz), 1)
    first, last = lane == 0, lane == cz - 1
    k = lane % STRIP
    group = lane // STRIP
    touching = (k == HALO) | (k == HALO - 1)

    def column(x):
        far = layers_left(dims, x, reach)
        low, high = HALO - far, HALO + cy + far
        beyond = src_strip[x]
        ends = jnp.zeros_like(beyond)
        behind, here = src[x, low - 1], src[x, low]
        for y in range(low, high):
            ahead = src[x, y + 1]
            edge = pltpu.roll(beyond, (2 * cz - (y * STRIP + HALO)) % cz, 1)
            above = jnp.where(last, edge, pltpu.roll(here, cz - 1, 1))
            below = jnp.where(first, edge, pltpu.roll(here, 1, 1))
            at = row_of(dims, x, y)
            total = r[at * ch:(at + 1) * ch, :] - here
            total += coefficient(dims, state, 0, at) * src[x + 1, y]
            total += coefficient(dims, state, 1, at) * src[x - 1, y]
            total += coefficient(dims, state, 2, at) * ahead
            total += coefficient(dims, state, 3, at) * behind
            total += coefficient(dims, state, 4, at) * above
            total += coefficient(dims, state, 5, at) * below
            dst[x, y] = here + weight * total
            if far > 0 and low < y < high - 1:
                moved = pltpu.roll(here, (y * STRIP + HALO) % cz, 1)
                ends = jnp.where(touching & (group == y), moved, ends)
            behind, here = here, ahead
        if far > 0:
            strip_column(x, beyond, ends)

    def strip_column(x, here, ends):
        def spread_strip(k):
            return jnp.broadcast_to(c_strip[k, x:x + 1, :], (ch, cz))

        above = jnp.where(k == HALO, ends, pltpu.roll(here, 1, 1))
        below = jnp.where(k == HALO - 1, ends, pltpu.roll(here, cz - 1, 1))
        total = r_strip[x] - here
        total += spread_strip(0) * src_strip[x + 1]
        total += spread_strip(1) * src_strip[x - 1]
        total += spread_strip(2) * pltpu.roll(here, cz - STRIP, 1)
        total += spread_strip(3) * pltpu.roll(here, STRIP, 1)
        total += spread_strip(4) * above
        total += spread_strip(5) * below
        dst_strip[x] = here + weight * total

    for x in range(HALO - reach, HALO + cx + reach):
        column(x)


def coefficients(dims, kc, kc_strip, state, c_strip):
    cx, cy, cz, ch, nodes = dims
    tx, ty = cx + 2 * HALO, cy + 2 * HALO
    lane = iota((ty, cz), 1)
    y = iota((ty, cz), 0)
    here = kc_strip[8:8 + tx, :]
    group = lane // STRIP
    k = lane % STRIP
    touching = ((k == HALO) | (k == HALO - 1)) & (group == y)
    starts, total = held_rows(dims)
    ends = [jnp.zeros((1, cz), F32)]
    for x in range(1, tx - 1):
        own = kc[x + 1, 8:8 + ty, :]
        moved = pltpu.roll(own, HALO, 1, stride=STRIP, stride_axis=0)
        ends.append(jnp.sum(jnp.where(touching, moved, 0.0), axis=0, keepdims=True))
        beyond = jnp.broadcast_to(kc_strip[8 + x:9 + x, :], (ty, cz))
        upper = jnp.where((group == y) & (k == HALO - 1), beyond, 0.0).sum(axis=1, keepdims=True)
        lower = jnp.where((group == y) & (k == HALO), beyond, 0.0).sum(axis=1, keepdims=True)
        others = [
            kc[x + 2, 8:8 + ty, :],
            kc[x, 8:8 + ty, :],
            kc[x + 1, 9:9 + ty, :],
            kc[x + 1, 7:7 + ty, :],
            jnp.where(lane == cz - 1, upper, pltpu.roll(own, cz - 1, 1)),
            jnp.where(lane == 0, lower, pltpu.roll(own, 1, 1)),
        ]
        first, y0, y1 = starts[x]
        for i, value in enumerate(finish(own, others)):
            at = cx * cy * ch + total * i + first
            state[at:at + y1 - y0, :] = value[y0:y1, :]
    ends = jnp.concatenate(ends + [jnp.zeros((1, cz), F32)], axis=0)
    lane = iota((tx, cz), 1)
    k = lane % STRIP
    others = [
        kc_strip[9:9 + tx, :],
        kc_strip[7:7 + tx, :],
        pltpu.roll(here, cz - STRIP, 1),
        pltpu.roll(here, STRIP, 1),
        jnp.where(k == HALO, ends, pltpu.roll(here, 1, 1)),
        jnp.where(k == HALO - 1, ends, pltpu.roll(here, cz - 1, 1)),
    ]
    for i, value in enumerate(finish(here, others)):
        c_strip[i] = value


def finish(own, others):
    faces = [0.5 * (own + other) for other in others]
    diag = MASS_TERM + faces[0]
    for face in faces[1:]:
        diag = diag + face
    inverse = jnp.where(own > 0.0, 1.0 / diag, 0.0)
    return [face * inverse for face in faces] + [inverse]


def smooth(dims, start, fields, strips, r, r_strip, state, c_strip):
    weights = sweep_weights(SWEEPS)
    now = 0
    for number in range(start, SWEEPS):
        sweep(
            dims, SWEEPS - 1 - number, weights[number], fields[now], strips[now],
            fields[1 - now], strips[1 - now], r, r_strip, state, c_strip,
        )
        now = 1 - now
    return fields[now]


def gather_nodes(dims, field, row, z):
    cx, cy, cz, ch, nodes = dims
    hits = (iota((cz, nodes), 0) == z).astype(BF16)
    rows = field[HALO:HALO + cx, HALO:HALO + cy].reshape(cx * cy * ch, cz).astype(BF16)
    at_z = jnp.dot(rows, hits, preferred_element_type=F32)
    total = jnp.zeros((ch, nodes), F32)
    for r in range(cx * cy):
        here = jnp.broadcast_to(row == r, (ch, nodes))
        total = jnp.where(here, at_z[r * ch:(r + 1) * ch], total)
    return total.astype(BF16)


def fourth_kernel(dims, regions, nx, ny, place, main, small, strip, *refs):
    cx, cy, cz, ch, nodes = dims
    xrecv, yrecv, refs = refs[:nx], refs[nx:nx + ny], refs[nx + ny:]
    field_out, block_out, send_out, state, kept, c_strip, refs = *refs[:6], refs[6:]
    r, r_strip, fa, fb, sa, sb, kc, kc_strip, codes, strip_codes, side_codes = refs
    even_x = 1 - place[0] % 2
    even_y = 1 - place[1] % 2
    tx, ty = cx + 2 * HALO, cy + 2 * HALO
    width = RHS_HALO
    slab, edge = x_sizes(dims, width)
    blocks, y_edge = y_sizes(dims, width)

    fill_codes(
        dims, small, strip, xrecv, slab + edge, even_x, codes, strip_codes
    )
    kc[...] = jnp.zeros_like(kc)
    kc_strip[...] = jnp.zeros_like(kc_strip)

    def conductivity(code):
        value = jnp.zeros_like(code)
        for region in range(regions):
            coeff = jnp.broadcast_to(small[REGION:REGION + 1, region:region + 1], code.shape)
            value = jnp.where(code == region + 1, coeff, value)
        return value

    kc[1:1 + tx, 8 + HALO:8 + HALO + cy] = conductivity(codes[...]).reshape(tx, cy, cz)
    start = sum(blocks) + y_edge
    for low in (True, False):
        got = pick(yrecv, low, even_y, start, tx * HALO).astype(F32)
        side_codes[...] = conductivity(got)
        y0 = 8 if low else 8 + HALO + cy
        for x in range(tx):
            kc[1 + x, y0:y0 + HALO, :] = side_codes[x * HALO:(x + 1) * HALO, :]
    start += tx * HALO
    low = pick(yrecv, True, even_y, start, 16).astype(F32)
    high = pick(yrecv, False, even_y, start, 16).astype(F32)
    kc_strip[8:8 + tx, :] = conductivity(join_strips(strip_codes[...], low, high, cy))
    coefficients(dims, kc, kc_strip, state, c_strip)

    r_strip[...] = jnp.zeros_like(r_strip)
    weight = sweep_weights(SWEEPS)[0]

    def put(x, y, rows):
        for i in range(rows.shape[0]):
            at = row_of(dims, x, y + i)
            value = rows[i] * coefficient(dims, state, 6, at)
            r[at * ch:(at + 1) * ch, :] = value
            fa[x, y + i] = weight * value
            inside, at = kept_row(dims, x, y + i)
            if inside:
                state[at * ch:(at + 1) * ch, :] = value
            else:
                kept[at * ch:(at + 1) * ch, :] = rows[i].astype(BF16)

    assemble(dims, width, main, strip, xrecv, yrecv, even_x, even_y, put, r_strip)
    tx = cx + 2 * HALO
    kept[kept.shape[0] - tx * ch:, :] = r_strip[...].reshape(tx * ch, cz).astype(BF16)
    for x in range(HALO - width, HALO + cx + width):
        value = r_strip[x] * jnp.broadcast_to(c_strip[6, x:x + 1, :], (ch, cz))
        r_strip[x] = value
        sa[x] = weight * value
    field = smooth(dims, 1, (fa, fb), (sa, sb), r, r_strip, state, c_strip)

    field_out[...] = field[HALO:HALO + cx, HALO:HALO + cy].reshape(cx * cy * ch, cz)
    send_out[...] = strip_rows(lambda x, y: field[HALO + x, HALO + y], cx, cy, cz)
    row, z = node_places(small)
    traces = gather_nodes(dims, field, row, z)
    rows = []
    for axis in range(3):
        value = small[axis:axis + 1, :]
        for _ in range(2):
            part = value.astype(BF16).astype(F32)
            rows.append(part)
            value = value - part
    rows += [row.astype(F32), z.astype(F32)]
    rest = jnp.concatenate([traces.astype(F32)] + rows, axis=0).astype(BF16)
    for other in range(block_out.shape[0]):
        block_out[other] = rest


def tile_kernel(dims, count, scale, small, recv, tiles):
    cx, cy, cz, ch, nodes = dims
    own = [jnp.broadcast_to(small[k:k + 1, :], (nodes, nodes)).T for k in range(3)]

    def block(b, _):
        parts = recv[b].astype(F32)[ch:]
        squared = None
        for k in range(3):
            other = parts[2 * k:2 * k + 1] + parts[2 * k + 1:2 * k + 2]
            delta = own[k] - jnp.broadcast_to(other, (nodes, nodes))
            squared = delta * delta if squared is None else squared + delta * delta
        tile = (scale * lax.rsqrt(squared + SOFTENING * SOFTENING)).astype(BF16)
        tiles[:, pl.ds(pl.multiple_of(b * nodes, nodes), nodes)] = tile
        return _

    lax.fori_loop(0, count, block, 0)


def boundary_kernel(dims, count, scale, small, recv, sum_out, half_out, tiles):
    tile_kernel(dims, count, scale, small, recv, tiles)
    total = product(recv, tiles, count, dims)
    sum_out[...] = total
    for other in range(count):
        half_out[other] = total.astype(BF16)


def product(recv, tiles, count, dims):
    cx, cy, cz, ch, nodes = dims
    group = math.gcd(count, 32)

    def part(at):
        traces = jnp.concatenate([recv[at + i][:ch] for i in range(group)], axis=1)
        start = at * nodes
        if not isinstance(at, int):
            start = pl.multiple_of(start, nodes)
        return lax.dot_general(
            traces, tiles[:, pl.ds(start, group * nodes)], NT, preferred_element_type=F32
        )

    if group == count:
        return part(0)
    return lax.fori_loop(
        0, count // group, lambda i, total: total + part(i * group), jnp.zeros((ch, nodes), F32)
    )


def last_kernel(dims, count, small, recv, tiles, flux_out):
    cx, cy, cz, ch, nodes = dims
    incident = small[INCIDENT:INCIDENT + ch, :]
    flux_out[...] = incident + product(recv, tiles, count, dims)


def fifth_kernel(dims, sizes, nx, ny, place, main, sums, small, recv, blocks, strip, *refs):
    cx, cy, cz, ch, nodes = dims
    xrecv, yrecv, refs = refs[:nx], refs[nx:nx + ny], refs[nx + ny:]
    state, kept, c_strip, refs = *refs[:3], refs[3:]
    field_out, block_out, refs = *refs[:2], refs[2:]
    r, r_strip, fa, fb, sa, sb, left = refs
    even_x = 1 - place[0] % 2
    even_y = 1 - place[1] % 2
    width = RHS_HALO
    tx = cx + 2 * HALO
    for x in range(tx):
        at = kept.shape[0] - (tx - x) * ch
        r_strip[x] = kept[at:at + ch, :].astype(F32) * jnp.broadcast_to(
            c_strip[6, x:x + 1, :], (ch, cz)
        )
    sa[...] = jnp.zeros_like(sa)

    def put(x, y, rows):
        fa[x, y:y + rows.shape[0]] = rows

    assemble(dims, HALO, main, strip, xrecv, yrecv, even_x, even_y, put, sa)

    def neighbour(dx, dy, dz):
        at = [place[i] + d for i, d in enumerate((dx, dy, dz))]
        good = None
        for i, size in enumerate(sizes):
            ok = (at[i] >= 0) & (at[i] < size)
            good = ok if good is None else good & ok
            at[i] = jnp.clip(at[i], 0, size - 1)
        index = (at[0] * sizes[1] + at[1]) * sizes[2] + at[2]
        info = blocks[index].astype(F32)[ch:]
        good = jnp.full((1, nodes), good.astype(jnp.int32), jnp.int32) > 0
        row = jnp.where(good, info[6:7].astype(jnp.int32), -1)
        return recv[index].astype(F32), row, info[7:8].astype(jnp.int32)

    spans = {
        -1: (HALO - width, HALO, cx), 0: (HALO, HALO + cx, 0), 1: (HALO + cx, HALO + cx + width, -cx),
    }
    own_row, own_z = node_places(small)
    strip_lane = iota((cz, nodes), 0)
    starts = held_rows(dims)[0]
    for dx in (-1, 0, 1):
        x0, x1, back_x = spans[dx]
        edge = []
        hits_edge = []
        for dy in (-1, 0, 1):
            y0, y1, back_y = spans[dy]
            parts = []
            if dx == 0 and dy == 0:
                top = sums[...].astype(BF16).astype(F32)
                row, z = own_row, own_z
                parts = [top, sums[...] - top]
            else:
                value, row, z = neighbour(dx, dy, 0)
                parts = [value]
            hits = (iota((cz, nodes), 0) == z).astype(BF16)
            hits = jnp.concatenate([hits] * len(parts), axis=1)
            cells = [
                (x, y) for x in range(x0, x1) for y in range(y0, y1)
                if starts[x][1] <= y < starts[x][2]
            ]
            for at, (x, y) in enumerate(cells):
                wanted = (x - HALO + back_x) * cy + (y - HALO + back_y)
                here = jnp.broadcast_to(row == wanted, (ch, nodes))
                for i, value in enumerate(parts):
                    left[at * ch:(at + 1) * ch, i * nodes:(i + 1) * nodes] = jnp.where(
                        here, value, 0.0
                    ).astype(BF16)
            added = lax.dot_general(
                left[:len(cells) * ch, :len(parts) * nodes], hits, NT, preferred_element_type=F32
            )
            for i, (x, y) in enumerate(cells):
                at = row_of(dims, x, y)
                inverse = coefficient(dims, state, 6, at)
                more = added[i * ch:(i + 1) * ch]
                inside, old = kept_row(dims, x, y)
                if inside:
                    value = state[old * ch:(old + 1) * ch, :] + more * inverse
                else:
                    value = (kept[old * ch:(old + 1) * ch, :].astype(F32) + more) * inverse
                r[at * ch:(at + 1) * ch, :] = value
            for dz in (-1, 1):
                value, row, z = neighbour(dx, dy, dz)
                y = row % cy + cy * dy + HALO
                k = HALO - 1 - z if dz > 0 else HALO + cz - 1 - z
                good = (row >= 0) & (y >= 0) & (y < cy + 2 * HALO) & (k >= 0) & (k < STRIP)
                good = good & ((k < HALO) if dz > 0 else (k >= HALO))
                lane = jnp.where(good, y * STRIP + k, -1)
                hits_edge.append((strip_lane == lane).astype(BF16))
                edge.append((value, jnp.where(row >= 0, row // cy, -1)))
        for x in range(x0, x1):
            at = (x - x0) * ch
            for i, (value, node_x) in enumerate(edge):
                here = jnp.broadcast_to(node_x == x - HALO + back_x, (ch, nodes))
                left[at:at + ch, i * nodes:(i + 1) * nodes] = jnp.where(here, value, 0.0).astype(BF16)
        added = lax.dot_general(
            left[:(x1 - x0) * ch, :len(edge) * nodes], jnp.concatenate(hits_edge, axis=1), NT,
            preferred_element_type=F32,
        )
        for x in range(x0, x1):
            inverse = jnp.broadcast_to(c_strip[6, x:x + 1, :], (ch, cz))
            r_strip[x] += added[(x - x0) * ch:(x - x0 + 1) * ch] * inverse

    field = smooth(dims, 0, (fa, fb), (sa, sb), r, r_strip, state, c_strip)
    for x in range(cx):
        for y in range(cy):
            field_out[pl.ds(x * cy + y, ch, stride=cx * cy), :] = field[HALO + x, HALO + y]
    traces = gather_nodes(dims, field, own_row, own_z)
    for other in range(block_out.shape[0]):
        block_out[other] = traces


def per_device(source, labels, region_coeff, node_cell, node_pos, incident):
    ch, cx, cy, cz = source.shape
    nodes = node_cell.shape[0]
    dims = (cx, cy, cz, ch, nodes)
    sizes = tuple(lax.axis_size(axis) for axis in AXES)
    count = math.prod(sizes)
    nx, ny, nz = (2 if size > 2 else 1 for size in sizes)
    scale = KERNEL_GAIN / math.sqrt(nodes * count)
    tx, ty = cx + 2 * HALO, cy + 2 * HALO
    held = held_rows(dims)[1]
    place = jnp.stack([lax.axis_index(axis) for axis in AXES]).astype(jnp.int32)
    rows = cx * cy * ch
    flat = source.reshape(ch * cx * cy, cz)
    marks = labels.reshape(cx * cy, cz)
    cells = node_cell.reshape(1, nodes)
    shape = jax.ShapeDtypeStruct
    vmem = pltpu.VMEM

    height = INCIDENT + ch + cx * cy
    floats = ((node_pos, 0), (region_coeff[None], REGION), (incident, INCIDENT))
    whole = ((cells, CELL), (marks, INCIDENT + ch))

    def lay(entries, dtype):
        total = jnp.zeros((height, cz), dtype)
        for value, row in entries:
            sides = ((row, height - row - value.shape[0], 0), (0, cz - value.shape[1], 0))
            total += lax.pad(value, jnp.zeros((), dtype), sides)
        return total

    small = lay(floats, F32) + lay(whole, jnp.int32).astype(F32)
    rhs, send = kernel_call(
        functools.partial(first_kernel, dims),
        (shape((rows, cz), F32), shape((cx * ch + 16, cz), BF16)),
        [vmem((rows, 2 * nodes), BF16)],
        operands=(flat, small),
        name="scatter_first",
    )

    def halo(main, send, width, with_labels, between=(lambda x: x, lambda x: x)):
        zrecv = exchange(send, "col")
        zrecv = between[0](zrecv)
        extra = HALO * cy + 16 if with_labels else 0
        strip_rows_ = cx * ch + (16 if with_labels else 0)
        own = (main, small) if with_labels else (main,)
        strip, *sends = kernel_call(
            functools.partial(second_kernel, dims, width, with_labels, nz, nx),
            (shape((strip_rows_, cz), BF16),)
            + (shape((sum(x_sizes(dims, width)) + extra, cz), BF16),) * nx,
            [vmem((32, cz), F32)] if with_labels else [],
            smem=1,
            operands=(place, *own, *zrecv),
            name="pack_x",
        )
        xrecv = exchange(None, "vol", sends)
        xrecv = between[1](xrecv)
        extra = tx * HALO + 16 if with_labels else 0
        blocks, y_edge = y_sizes(dims, width)
        sends = kernel_call(
            functools.partial(third_kernel, dims, width, with_labels, nx, ny),
            (shape((sum(blocks) + y_edge + extra, cz), BF16),) * ny,
            [vmem((tx * cy, cz), F32), vmem((tx, cz), F32), vmem((tx * HALO, cz), F32)]
            if with_labels else [],
            smem=1,
            operands=(place, *own, strip, *xrecv),
            name="pack_y",
        )
        yrecv = exchange(None, "row", sends)
        return strip, xrecv, yrecv

    strip, xrecv, yrecv = halo(rhs, send, RHS_HALO, True)
    field, block, send, state, kept, c_strip = kernel_call(
        functools.partial(fourth_kernel, dims, region_coeff.shape[0], nx, ny),
        (
            shape((rows, cz), F32),
            shape((count, ch + 8, nodes), BF16),
            shape((cx * ch, cz), BF16),
            shape((rows + 7 * held, cz), F32),
            shape(((held - cx * cy + tx) * ch, cz), BF16),
            shape((7, tx, cz), F32),
        ),
        [
            vmem((held * ch, cz), F32),
            vmem((tx, ch, cz), F32),
            vmem((tx, ty, ch, cz), F32),
            vmem((tx, ty, ch, cz), F32),
            vmem((tx, ch, cz), F32),
            vmem((tx, ch, cz), F32),
            vmem((tx + 2, ty + 16, cz), F32),
            vmem((tx + 16, cz), F32),
            vmem((tx * cy, cz), F32),
            vmem((tx, cz), F32),
            vmem((tx * HALO, cz), F32),
        ],
        smem=1,
        operands=(place, rhs, small, strip, *xrecv, *yrecv),
        name="sweeps_first",
    )

    def to_all(value):
        return lax.all_to_all(value, AXES, 0, 0, tiled=True)

    blocks = to_all(block)
    sums, half = kernel_call(
        functools.partial(boundary_kernel, dims, count, scale),
        (
            shape((ch, nodes), F32),
            shape((count, ch, nodes), BF16),
        ),
        [vmem((nodes, count * nodes), BF16)],
        operands=(small, blocks),
        name="boundary",
    )

    def after_boundary(arrays):
        return lax.optimization_barrier((arrays, half))[0]

    strip, xrecv, yrecv = halo(field, send, HALO, False, (lambda x: x, after_boundary))
    recv = to_all(half)
    field, block = kernel_call(
        functools.partial(fifth_kernel, dims, sizes, nx, ny),
        (shape((ch * cx * cy, cz), F32), shape((count, ch, nodes), BF16)),
        [
            vmem((held * ch, cz), F32),
            vmem((tx, ch, cz), F32),
            vmem((tx, ty, ch, cz), F32),
            vmem((tx, ty, ch, cz), F32),
            vmem((tx, ch, cz), F32),
            vmem((tx, ch, cz), F32),
            vmem((rows, 6 * nodes), BF16),
        ],
        smem=1,
        operands=(
            place, field, sums, small, recv, blocks, strip, *xrecv, *yrecv, state, kept, c_strip
        ),
        name="sweeps_last",
    )
    blocks, block = lax.optimization_barrier((blocks, block))
    tiles = kernel_call(
        functools.partial(tile_kernel, dims, count, scale),
        shape((nodes, count * nodes), BF16),
        operands=(small, blocks),
        cost=pl.CostEstimate(flops=10**9, bytes_accessed=10**6, transcendentals=10**6),
        name="tiles_last",
    )
    flux = kernel_call(
        functools.partial(last_kernel, dims, count),
        shape((ch, nodes), F32),
        operands=(small, to_all(block), tiles),
        name="flux_last",
    )
    return field.reshape(source.shape), flux


def solution(mesh):
    placed = (
        P(None, "vol", "row", "col"),
        P("vol", "row", "col"),
        P(),
        P(("vol", "row", "col")),
        P(None, ("vol", "row", "col")),
        P(None, ("vol", "row", "col")),
    )
    return jax.shard_map(
        per_device,
        mesh=mesh,
        in_specs=placed,
        out_specs=(P(None, "vol", "row", "col"), P(None, ("vol", "row", "col"))),
        check_vma=False,
    )
```

```python
import functools
import math

import jax
import jax.numpy as jnp
from jax import lax
from jax.experimental import pallas as pl
from jax.experimental.pallas import tpu as pltpu
from jax.sharding import PartitionSpec as P

SWEEPS = 4
ITERS = 2

MASS_TERM = 0.05
SOFTENING = 0.05
KERNEL_GAIN = 2.0

HALO = SWEEPS
RHS_HALO = SWEEPS - 1
STRIP = 2 * HALO
AXES = ("vol", "row", "col")
F32, BF16 = jnp.float32, jnp.bfloat16
CELL, REGION, INCIDENT = 3, 4, 8
SPARE = 4 * 1024 * 1024
NT = (((1,), (1,)), ((), ()))


def sweep_weights(count):
    return [
        1.0 / (1.05 - 0.95 * math.cos(math.pi * (2 * sweep + 1) / (2 * count)))
        for sweep in range(count)
    ]


def iota(shape, dim):
    return lax.broadcasted_iota(jnp.int32, shape, dim)


def kernel_call(body, out_shape, scratch=(), smem=0, operands=(), cost=None, name=None):
    held = [jnp.shape(leaf) + (leaf.dtype,) for leaf in jax.tree.leaves((out_shape, operands))]
    held += [ref.shape + (ref.dtype,) for ref in scratch]
    need = sum(math.prod(entry[:-1]) * jnp.dtype(entry[-1]).itemsize for entry in held)
    specs = [pl.BlockSpec(memory_space=pltpu.SMEM)] * smem
    specs += [pl.BlockSpec(memory_space=pltpu.VMEM)] * (len(operands) - smem)
    return pl.pallas_call(
        body,
        out_shape=out_shape,
        in_specs=specs,
        out_specs=jax.tree.map(lambda _: pl.BlockSpec(memory_space=pltpu.VMEM), out_shape),
        scratch_shapes=list(scratch),
        compiler_params=pltpu.CompilerParams(vmem_limit_bytes=need + SPARE),
        cost_estimate=cost,
        name=name,
    )(*operands)


def layers_left(dims, x, reach):
    cx = dims[0]
    return reach - max(HALO - x, x - (HALO + cx - 1), 0)


@functools.lru_cache
def held_rows(dims):
    cx, cy, cz, ch, nodes = dims
    starts, total = {}, 0
    for x in range(cx + 2 * HALO):
        far = layers_left(dims, x, RHS_HALO)
        if far >= 0:
            starts[x] = (total, HALO - far, HALO + cy + far)
            total += cy + 2 * far
    return starts, total


def row_of(dims, x, y):
    first, y0, y1 = held_rows(dims)[0][x]
    return first + y - y0


@functools.lru_cache(maxsize=None)
def kept_row(dims, x, y):
    cx, cy, cz, ch, nodes = dims
    starts, total = held_rows(dims)
    if HALO <= x < HALO + cx and HALO <= y < HALO + cy:
        return True, (x - HALO) * cy + y - HALO
    before = 0
    for other in sorted(starts):
        first, y0, y1 = starts[other]
        for at in range(y0, y1):
            if (other, at) == (x, y):
                return False, before
            before += not (HALO <= other < HALO + cx and HALO <= at < HALO + cy)
    raise KeyError(x, y)


def x_sizes(dims, width):
    cx, cy, cz, ch, nodes = dims
    return width * cy * ch, (width - 1) * ch


def y_sizes(dims, width):
    cx, cy, cz, ch, nodes = dims
    return [(cx + 2 * (width - d)) * ch for d in range(1, width + 1)], (cx + 2 * (width - 2)) * ch


def pick(refs, low, even, rows, size):
    first = refs[0][pl.ds(rows, size), :]
    flag = jnp.full(first.shape, even, jnp.int32).astype(first.dtype)
    mine, other = (1 - flag, flag) if low else (flag, 1 - flag)
    if len(refs) == 1:
        return first * mine
    return first * mine + refs[1][pl.ds(rows, size), :] * other


def exchange(array, axis, arrays=None):
    count = lax.axis_size(axis)
    arrays = arrays or [array] * 2
    out = []
    for which in range(2 if count > 2 else 1):
        pairs = []
        for i in range(which, count - 1, 2):
            pairs += [(i, i + 1), (i + 1, i)]
        out.append(lax.ppermute(arrays[which], axis, pairs))
    return out


def edge_picker(cz, lanes):
    z, lane = iota((cz, lanes), 0), iota((cz, lanes), 1)
    k = lane % STRIP
    wanted = jnp.where(k < HALO, HALO - 1 - k, cz - 1 - k + HALO)
    return (z == wanted).astype(F32), lane // STRIP - HALO


def strip_rows(read, cx, cy, cz):
    base, lane_y = edge_picker(cz, cz)
    total = None
    for y in range(cy):
        rows = jnp.concatenate([read(x, y).astype(BF16) for x in range(cx)], axis=0)
        picked = jnp.where(lane_y == y, base, 0.0).astype(BF16)
        part = jnp.dot(rows, picked, preferred_element_type=F32)
        total = part if total is None else total + part
    return total.astype(BF16)


def node_places(small):
    cell = small[CELL:CELL + 1, :].astype(jnp.int32)
    cz = small.shape[1]
    return cell // cz, cell % cz


def first_kernel(dims, source, small, rhs_out, send_out, left):
    cx, cy, cz, ch, nodes = dims
    row, z = node_places(small)
    hits = (iota((cz, nodes), 0) == z).astype(BF16)
    flux = small[INCIDENT:INCIDENT + ch, :]
    top = flux.astype(BF16).astype(F32)
    rest = flux - top
    for r in range(cx * cy):
        here = jnp.broadcast_to(row == r, (ch, nodes))
        left[r * ch:(r + 1) * ch, :nodes] = jnp.where(here, top, 0.0).astype(BF16)
        left[r * ch:(r + 1) * ch, nodes:] = jnp.where(here, rest, 0.0).astype(BF16)
    added = lax.dot_general(
        left[...], jnp.concatenate([hits, hits], axis=1), NT, preferred_element_type=F32
    )
    rhs_out[...] = added
    for r in range(cx * cy):
        rhs_out[r * ch:(r + 1) * ch, :] += source[pl.ds(r, ch, stride=cx * cy), :]

    def read(x, y):
        start = (x * cy + y) * ch
        return rhs_out[start:start + ch, :]

    send_out[:cx * ch, :] = strip_rows(read, cx, cy, cz)
    base, lane_y = edge_picker(cz, cz)
    codes = (small[INCIDENT + ch:, :] + 1.0).astype(BF16)
    strips = jnp.dot(codes, base.astype(BF16), preferred_element_type=F32)
    own = (iota(strips.shape, 0) % cy) == lane_y[:1, :]
    strips = jnp.where(own, strips, 0.0).reshape(cx, cy, cz).sum(axis=1)
    send_out[cx * ch:, :] = jnp.concatenate(
        [strips, jnp.zeros((16 - cx, cz), F32)], axis=0
    ).astype(BF16)


def second_kernel(dims, width, with_labels, nz, nx, place, *refs):
    cx, cy, cz, ch, nodes = dims
    main, refs = refs[0], refs[1:]
    if with_labels:
        small, refs = refs[0], refs[1:]
    zrecv, refs = refs[:nz], refs[nz:]
    strip_out, sends, refs = refs[0], refs[1:1 + nx], refs[1 + nx:]
    even_x = 1 - place[0] % 2
    even_z = 1 - place[2] % 2
    rows = cx * ch + (16 if with_labels else 0)
    lane = iota((rows, cz), 1)
    upper = pick(zrecv, False, even_z, 0, rows)
    lower = pick(zrecv, True, even_z, 0, rows)
    strip_out[...] = jnp.where(
        lane % STRIP < HALO, upper.astype(F32), lower.astype(F32)
    ).astype(BF16)
    if with_labels:
        (codes,) = refs
        codes[...] = jnp.zeros_like(codes)
        codes[:16, :] = strip_out[cx * ch:, :].astype(F32)
    slab, edge = x_sizes(dims, width)
    for which in range(nx):
        upward = even_x if which == 0 else 1 - even_x
        x0 = upward * (cx - width)
        send = sends[which]
        send[:slab, :] = main[pl.ds(pl.multiple_of(x0 * (cy * ch), 16), slab), :].astype(BF16)
        x0 = upward * (cx - width + 1)
        send[slab:slab + edge, :] = strip_out[pl.ds(pl.multiple_of(x0 * ch, 16), edge), :]
        if with_labels:
            start = slab + edge
            x0 = upward * (cx - HALO)
            send[start:start + HALO * cy, :] = (
                small[pl.ds(pl.multiple_of(INCIDENT + ch + x0 * cy, 8), HALO * cy), :] + 1.0
            ).astype(BF16)
            send[start + HALO * cy:, :] = codes[pl.ds(x0, 16), :].astype(BF16)


def third_kernel(dims, width, with_labels, nx, ny, place, *refs):
    cx, cy, cz, ch, nodes = dims
    main, refs = refs[0], refs[1:]
    if with_labels:
        small, refs = refs[0], refs[1:]
    strip, refs = refs[0], refs[1:]
    xrecv, refs = refs[:nx], refs[nx:]
    sends, refs = refs[:ny], refs[ny:]
    even_x = 1 - place[0] % 2
    even_y = 1 - place[1] % 2
    slab, edge = x_sizes(dims, width)
    if with_labels:
        codes, strip_codes, picked = refs
        fill_codes(dims, small, strip, xrecv, slab + edge, even_x, codes, strip_codes)
    for which in range(ny):
        send = sends[which]
        upward = even_y if which == 0 else 1 - even_y
        start = 0
        for d in range(1, width + 1):
            y = d - 1 + upward * (cy - 2 * d + 1)
            for x in range(d - width, cx + width - d):
                if 0 <= x < cx:
                    at = pl.multiple_of((x * cy + y) * ch, 16)
                    piece = main[pl.ds(at, ch), :].astype(BF16)
                else:
                    at = pl.multiple_of(((x + width if x < 0 else x - cx) * cy + y) * ch, 16)
                    piece = pick(xrecv, x < 0, even_x, at, ch)
                send[start:start + ch, :] = piece
                start += ch
        side = (width - 2) * ch
        send[start:start + side, :] = pick(xrecv, True, even_x, slab + edge - side, side)
        send[start + side:start + side + cx * ch, :] = strip[:cx * ch, :]
        start += side + cx * ch
        send[start:start + side, :] = pick(xrecv, False, even_x, slab, side)
        start += side
        if with_labels:
            y0 = upward * (cy - HALO)
            tall = cx + 2 * HALO
            for x in range(tall):
                picked[x * HALO:(x + 1) * HALO, :] = codes[pl.ds(x * cy + y0, HALO), :]
            send[start:start + tall * HALO, :] = picked[...].astype(BF16)
            send[start + tall * HALO:, :] = strip_codes[...].astype(BF16)


def fill_codes(dims, small, strip, xrecv, start, even_x, codes, strip_codes):
    cx, cy, cz, ch, nodes = dims
    side = HALO * cy
    codes[:side, :] = pick(xrecv, True, even_x, start, side).astype(F32)
    codes[side:side + cx * cy, :] = small[INCIDENT + ch:, :] + 1.0
    codes[side + cx * cy:, :] = pick(xrecv, False, even_x, start, side).astype(F32)
    strip_codes[:HALO, :] = pick(xrecv, True, even_x, start + side, 16).astype(F32)[:HALO]
    strip_codes[HALO:HALO + cx, :] = strip[cx * ch:cx * ch + 16, :].astype(F32)[:cx]
    strip_codes[HALO + cx:, :] = pick(xrecv, False, even_x, start + side, 16).astype(F32)[:HALO]


def assemble(dims, width, main, strip, xrecv, yrecv, even_x, even_y, put, out_strip):
    cx, cy, cz, ch, nodes = dims
    slab, edge = x_sizes(dims, width)
    blocks, y_edge = y_sizes(dims, width)
    column = cy * ch
    for x in range(cx):
        put(HALO + x, HALO, main[x * column:(x + 1) * column, :].reshape(cy, ch, cz))
    for low in (True, False):
        x0 = HALO - width if low else HALO + cx
        for i in range(width):
            got = pick(xrecv, low, even_x, i * column, column).astype(F32)
            put(x0 + i, HALO, got.reshape(cy, ch, cz))
        start = 0
        for d, size in enumerate(blocks, 1):
            got = pick(yrecv, low, even_y, start, size).astype(F32).reshape(size // ch, 1, ch, cz)
            for i in range(size // ch):
                put(HALO + d - width + i, HALO - d if low else HALO + cy + d - 1, got[i])
            start += size
    own = jnp.concatenate(
        [
            pick(xrecv, True, even_x, slab, edge),
            strip[:cx * ch, :],
            pick(xrecv, False, even_x, slab, edge),
        ],
        axis=0,
    ).astype(F32)
    blank = jnp.zeros((ch, cz), F32)
    low, high = (
        jnp.concatenate([blank, pick(yrecv, low, even_y, start, y_edge).astype(F32), blank], axis=0)
        for low in (True, False)
    )
    full = join_strips(own, low, high, cy)
    out_strip[HALO - width + 1:HALO + cx + width - 1] = full.reshape(cx + 2 * width - 2, ch, cz)


def join_strips(own, low, high, cy):
    lane = iota(own.shape, 1)
    shift = cy * STRIP
    lanes = own.shape[1]
    low = pltpu.roll(low, lanes - shift, 1)
    high = pltpu.roll(high, shift, 1)
    return jnp.where(
        lane < HALO * STRIP, low, jnp.where(lane < (HALO + cy) * STRIP, own, high)
    )


def coefficient(dims, state, k, at):
    cx, cy, cz, ch, nodes = dims
    at += cx * cy * ch + held_rows(dims)[1] * k
    return jnp.broadcast_to(state[at:at + 1, :], (ch, cz))


def sweep(dims, reach, weight, src, src_strip, dst, dst_strip, r, r_strip, state, c_strip):
    cx, cy, cz, ch, nodes = dims
    lane = iota((ch, cz), 1)
    first, last = lane == 0, lane == cz - 1
    k = lane % STRIP
    group = lane // STRIP
    touching = (k == HALO) | (k == HALO - 1)

    def column(x):
        far = layers_left(dims, x, reach)
        low, high = HALO - far, HALO + cy + far
        beyond = src_strip[x]
        ends = jnp.zeros_like(beyond)
        behind, here = src[x, low - 1], src[x, low]
        for y in range(low, high):
            ahead = src[x, y + 1]
            mirror = 2 * HALO + cy - 1 - y
            shared = far > 0 and low < y < high - 1
            both = jnp.where(first | last, src[x, mirror], beyond) if shared else beyond
            edge = pltpu.roll(both, (2 * cz - (y * STRIP + HALO)) % cz, 1)
            if shared:
                ends = jnp.where(touching & (group == mirror), edge, ends)
            above = jnp.where(last, edge, pltpu.roll(here, cz - 1, 1))
            below = jnp.where(first, edge, pltpu.roll(here, 1, 1))
            at = row_of(dims, x, y)
            total = r[at * ch:(at + 1) * ch, :] - here
            total += coefficient(dims, state, 0, at) * src[x + 1, y]
            total += coefficient(dims, state, 1, at) * src[x - 1, y]
            total += coefficient(dims, state, 2, at) * ahead
            total += coefficient(dims, state, 3, at) * behind
            total += coefficient(dims, state, 4, at) * above
            total += coefficient(dims, state, 5, at) * below
            dst[x, y] = here + weight * total
            behind, here = here, ahead
        if far > 0:
            strip_column(x, beyond, ends)

    def strip_column(x, here, ends):
        def spread_strip(k):
            return jnp.broadcast_to(c_strip[k, x:x + 1, :], (ch, cz))

        above = jnp.where(k == HALO, ends, pltpu.roll(here, 1, 1))
        below = jnp.where(k == HALO - 1, ends, pltpu.roll(here, cz - 1, 1))
        total = r_strip[x] - here
        total += spread_strip(0) * src_strip[x + 1]
        total += spread_strip(1) * src_strip[x - 1]
        total += spread_strip(2) * pltpu.roll(here, cz - STRIP, 1)
        total += spread_strip(3) * pltpu.roll(here, STRIP, 1)
        total += spread_strip(4) * above
        total += spread_strip(5) * below
        dst_strip[x] = here + weight * total

    for x in range(HALO - reach, HALO + cx + reach):
        column(x)


def coefficients(dims, kc, kc_strip, state, c_strip):
    cx, cy, cz, ch, nodes = dims
    tx, ty = cx + 2 * HALO, cy + 2 * HALO
    lane = iota((ty, cz), 1)
    y = iota((ty, cz), 0)
    here = kc_strip[8:8 + tx, :]
    group = lane // STRIP
    k = lane % STRIP
    touching = ((k == HALO) | (k == HALO - 1)) & (group == y)
    starts, total = held_rows(dims)
    ends = [jnp.zeros((1, cz), F32)]
    for x in range(1, tx - 1):
        own = kc[x + 1, 8:8 + ty, :]
        moved = pltpu.roll(own, HALO, 1, stride=STRIP, stride_axis=0)
        ends.append(jnp.sum(jnp.where(touching, moved, 0.0), axis=0, keepdims=True))
        beyond = jnp.broadcast_to(kc_strip[8 + x:9 + x, :], (ty, cz))
        upper = jnp.where((group == y) & (k == HALO - 1), beyond, 0.0).sum(axis=1, keepdims=True)
        lower = jnp.where((group == y) & (k == HALO), beyond, 0.0).sum(axis=1, keepdims=True)
        others = [
            kc[x + 2, 8:8 + ty, :],
            kc[x, 8:8 + ty, :],
            kc[x + 1, 9:9 + ty, :],
            kc[x + 1, 7:7 + ty, :],
            jnp.where(lane == cz - 1, upper, pltpu.roll(own, cz - 1, 1)),
            jnp.where(lane == 0, lower, pltpu.roll(own, 1, 1)),
        ]
        first, y0, y1 = starts[x]
        for i, value in enumerate(finish(own, others)):
            at = cx * cy * ch + total * i + first
            state[at:at + y1 - y0, :] = value[y0:y1, :]
    ends = jnp.concatenate(ends + [jnp.zeros((1, cz), F32)], axis=0)
    lane = iota((tx, cz), 1)
    k = lane % STRIP
    others = [
        kc_strip[9:9 + tx, :],
        kc_strip[7:7 + tx, :],
        pltpu.roll(here, cz - STRIP, 1),
        pltpu.roll(here, STRIP, 1),
        jnp.where(k == HALO, ends, pltpu.roll(here, 1, 1)),
        jnp.where(k == HALO - 1, ends, pltpu.roll(here, cz - 1, 1)),
    ]
    for i, value in enumerate(finish(here, others)):
        c_strip[i] = value


def finish(own, others):
    faces = [0.5 * (own + other) for other in others]
    diag = MASS_TERM + faces[0]
    for face in faces[1:]:
        diag = diag + face
    inverse = jnp.where(own > 0.0, 1.0 / diag, 0.0)
    return [face * inverse for face in faces] + [inverse]


def smooth(dims, start, fields, strips, r, r_strip, state, c_strip):
    weights = sweep_weights(SWEEPS)
    now = 0
    for number in range(start, SWEEPS):
        sweep(
            dims, SWEEPS - 1 - number, weights[number], fields[now], strips[now],
            fields[1 - now], strips[1 - now], r, r_strip, state, c_strip,
        )
        now = 1 - now
    return fields[now]


def gather_nodes(dims, field, row, z):
    cx, cy, cz, ch, nodes = dims
    hits = (iota((cz, nodes), 0) == z).astype(BF16)
    rows = field[HALO:HALO + cx, HALO:HALO + cy].reshape(cx * cy * ch, cz).astype(BF16)
    at_z = jnp.dot(rows, hits, preferred_element_type=F32)
    total = jnp.zeros((ch, nodes), F32)
    for r in range(cx * cy):
        here = jnp.broadcast_to(row == r, (ch, nodes))
        total = jnp.where(here, at_z[r * ch:(r + 1) * ch], total)
    return total.astype(BF16)


def fourth_kernel(dims, regions, nx, ny, place, main, small, strip, *refs):
    cx, cy, cz, ch, nodes = dims
    xrecv, yrecv, refs = refs[:nx], refs[nx:nx + ny], refs[nx + ny:]
    field_out, block_out, send_out, state, kept, c_strip, refs = *refs[:6], refs[6:]
    r, r_strip, fa, fb, sa, sb, kc, kc_strip, codes, strip_codes, side_codes = refs
    even_x = 1 - place[0] % 2
    even_y = 1 - place[1] % 2
    tx, ty = cx + 2 * HALO, cy + 2 * HALO
    width = RHS_HALO
    slab, edge = x_sizes(dims, width)
    blocks, y_edge = y_sizes(dims, width)

    fill_codes(
        dims, small, strip, xrecv, slab + edge, even_x, codes, strip_codes
    )
    kc[...] = jnp.zeros_like(kc)
    kc_strip[...] = jnp.zeros_like(kc_strip)

    def conductivity(code):
        value = jnp.zeros_like(code)
        for region in range(regions):
            coeff = jnp.broadcast_to(small[REGION:REGION + 1, region:region + 1], code.shape)
            value = jnp.where(code == region + 1, coeff, value)
        return value

    kc[1:1 + tx, 8 + HALO:8 + HALO + cy] = conductivity(codes[...]).reshape(tx, cy, cz)
    start = sum(blocks) + y_edge
    for low in (True, False):
        got = pick(yrecv, low, even_y, start, tx * HALO).astype(F32)
        side_codes[...] = conductivity(got)
        y0 = 8 if low else 8 + HALO + cy
        for x in range(tx):
            kc[1 + x, y0:y0 + HALO, :] = side_codes[x * HALO:(x + 1) * HALO, :]
    start += tx * HALO
    low = pick(yrecv, True, even_y, start, 16).astype(F32)
    high = pick(yrecv, False, even_y, start, 16).astype(F32)
    kc_strip[8:8 + tx, :] = conductivity(join_strips(strip_codes[...], low, high, cy))
    coefficients(dims, kc, kc_strip, state, c_strip)

    r_strip[...] = jnp.zeros_like(r_strip)
    weight = sweep_weights(SWEEPS)[0]

    def put(x, y, rows):
        for i in range(rows.shape[0]):
            at = row_of(dims, x, y + i)
            value = rows[i] * coefficient(dims, state, 6, at)
            r[at * ch:(at + 1) * ch, :] = value
            fa[x, y + i] = weight * value
            inside, at = kept_row(dims, x, y + i)
            if inside:
                state[at * ch:(at + 1) * ch, :] = value
            else:
                kept[at * ch:(at + 1) * ch, :] = rows[i].astype(BF16)

    assemble(dims, width, main, strip, xrecv, yrecv, even_x, even_y, put, r_strip)
    tx = cx + 2 * HALO
    kept[kept.shape[0] - tx * ch:, :] = r_strip[...].reshape(tx * ch, cz).astype(BF16)
    for x in range(HALO - width, HALO + cx + width):
        value = r_strip[x] * jnp.broadcast_to(c_strip[6, x:x + 1, :], (ch, cz))
        r_strip[x] = value
        sa[x] = weight * value
    field = smooth(dims, 1, (fa, fb), (sa, sb), r, r_strip, state, c_strip)

    field_out[...] = field[HALO:HALO + cx, HALO:HALO + cy].reshape(cx * cy * ch, cz)
    send_out[...] = strip_rows(lambda x, y: field[HALO + x, HALO + y], cx, cy, cz)
    row, z = node_places(small)
    traces = gather_nodes(dims, field, row, z)
    rows = []
    for axis in range(3):
        value = small[axis:axis + 1, :]
        for _ in range(2):
            part = value.astype(BF16).astype(F32)
            rows.append(part)
            value = value - part
    rows += [row.astype(F32), z.astype(F32)]
    rest = jnp.concatenate([traces.astype(F32)] + rows, axis=0).astype(BF16)
    for other in range(block_out.shape[0]):
        block_out[other] = rest


def tile_kernel(dims, count, scale, small, recv, tiles):
    cx, cy, cz, ch, nodes = dims
    own = [jnp.broadcast_to(small[k:k + 1, :], (nodes, nodes)).T for k in range(3)]

    def block(b, _):
        parts = recv[b].astype(F32)[ch:]
        squared = None
        for k in range(3):
            other = parts[2 * k:2 * k + 1] + parts[2 * k + 1:2 * k + 2]
            delta = own[k] - jnp.broadcast_to(other, (nodes, nodes))
            squared = delta * delta if squared is None else squared + delta * delta
        tile = (scale * lax.rsqrt(squared + SOFTENING * SOFTENING)).astype(BF16)
        tiles[:, pl.ds(pl.multiple_of(b * nodes, nodes), nodes)] = tile
        return _

    lax.fori_loop(0, count, block, 0)


def boundary_kernel(dims, count, scale, small, recv, sum_out, half_out, tiles):
    tile_kernel(dims, count, scale, small, recv, tiles)
    total = product(recv, tiles, count, dims)
    sum_out[...] = total
    for other in range(count):
        half_out[other] = total.astype(BF16)


def product(recv, tiles, count, dims):
    cx, cy, cz, ch, nodes = dims
    group = math.gcd(count, 32)

    def part(at):
        traces = jnp.concatenate([recv[at + i][:ch] for i in range(group)], axis=1)
        start = at * nodes
        if not isinstance(at, int):
            start = pl.multiple_of(start, nodes)
        return lax.dot_general(
            traces, tiles[:, pl.ds(start, group * nodes)], NT, preferred_element_type=F32
        )

    if group == count:
        return part(0)
    return lax.fori_loop(
        0, count // group, lambda i, total: total + part(i * group), jnp.zeros((ch, nodes), F32)
    )


def last_kernel(dims, count, small, recv, tiles, flux_out):
    cx, cy, cz, ch, nodes = dims
    incident = small[INCIDENT:INCIDENT + ch, :]
    flux_out[...] = incident + product(recv, tiles, count, dims)


def fifth_kernel(dims, sizes, nx, ny, place, main, sums, small, recv, blocks, strip, *refs):
    cx, cy, cz, ch, nodes = dims
    xrecv, yrecv, refs = refs[:nx], refs[nx:nx + ny], refs[nx + ny:]
    state, kept, c_strip, refs = *refs[:3], refs[3:]
    field_out, block_out, refs = *refs[:2], refs[2:]
    r, r_strip, fa, fb, sa, sb, left = refs
    even_x = 1 - place[0] % 2
    even_y = 1 - place[1] % 2
    width = RHS_HALO
    tx = cx + 2 * HALO
    for x in range(tx):
        at = kept.shape[0] - (tx - x) * ch
        r_strip[x] = kept[at:at + ch, :].astype(F32) * jnp.broadcast_to(
            c_strip[6, x:x + 1, :], (ch, cz)
        )
    sa[...] = jnp.zeros_like(sa)

    def put(x, y, rows):
        fa[x, y:y + rows.shape[0]] = rows

    assemble(dims, HALO, main, strip, xrecv, yrecv, even_x, even_y, put, sa)

    def neighbour(dx, dy, dz):
        at = [place[i] + d for i, d in enumerate((dx, dy, dz))]
        good = None
        for i, size in enumerate(sizes):
            ok = (at[i] >= 0) & (at[i] < size)
            good = ok if good is None else good & ok
            at[i] = jnp.clip(at[i], 0, size - 1)
        index = (at[0] * sizes[1] + at[1]) * sizes[2] + at[2]
        info = blocks[index].astype(F32)[ch:]
        good = jnp.full((1, nodes), good.astype(jnp.int32), jnp.int32) > 0
        row = jnp.where(good, info[6:7].astype(jnp.int32), -1)
        return recv[index].astype(F32), row, info[7:8].astype(jnp.int32)

    spans = {
        -1: (HALO - width, HALO, cx), 0: (HALO, HALO + cx, 0), 1: (HALO + cx, HALO + cx + width, -cx),
    }
    own_row, own_z = node_places(small)
    strip_lane = iota((cz, nodes), 0)
    starts = held_rows(dims)[0]
    for dx in (-1, 0, 1):
        x0, x1, back_x = spans[dx]
        edge = []
        hits_edge = []
        for dy in (-1, 0, 1):
            y0, y1, back_y = spans[dy]
            parts = []
            if dx == 0 and dy == 0:
                top = sums[...].astype(BF16).astype(F32)
                row, z = own_row, own_z
                parts = [top, sums[...] - top]
            else:
                value, row, z = neighbour(dx, dy, 0)
                parts = [value]
            hits = (iota((cz, nodes), 0) == z).astype(BF16)
            hits = jnp.concatenate([hits] * len(parts), axis=1)
            cells = [
                (x, y) for x in range(x0, x1) for y in range(y0, y1)
                if starts[x][1] <= y < starts[x][2]
            ]
            for at, (x, y) in enumerate(cells):
                wanted = (x - HALO + back_x) * cy + (y - HALO + back_y)
                here = jnp.broadcast_to(row == wanted, (ch, nodes))
                for i, value in enumerate(parts):
                    left[at * ch:(at + 1) * ch, i * nodes:(i + 1) * nodes] = jnp.where(
                        here, value, 0.0
                    ).astype(BF16)
            added = lax.dot_general(
                left[:len(cells) * ch, :len(parts) * nodes], hits, NT, preferred_element_type=F32
            )
            for i, (x, y) in enumerate(cells):
                at = row_of(dims, x, y)
                inverse = coefficient(dims, state, 6, at)
                more = added[i * ch:(i + 1) * ch]
                inside, old = kept_row(dims, x, y)
                if inside:
                    value = state[old * ch:(old + 1) * ch, :] + more * inverse
                else:
                    value = (kept[old * ch:(old + 1) * ch, :].astype(F32) + more) * inverse
                r[at * ch:(at + 1) * ch, :] = value
            for dz in (-1, 1):
                value, row, z = neighbour(dx, dy, dz)
                y = row % cy + cy * dy + HALO
                k = HALO - 1 - z if dz > 0 else HALO + cz - 1 - z
                good = (row >= 0) & (y >= 0) & (y < cy + 2 * HALO) & (k >= 0) & (k < STRIP)
                good = good & ((k < HALO) if dz > 0 else (k >= HALO))
                lane = jnp.where(good, y * STRIP + k, -1)
                hits_edge.append((strip_lane == lane).astype(BF16))
                edge.append((value, jnp.where(row >= 0, row // cy, -1)))
        for x in range(x0, x1):
            at = (x - x0) * ch
            for i, (value, node_x) in enumerate(edge):
                here = jnp.broadcast_to(node_x == x - HALO + back_x, (ch, nodes))
                left[at:at + ch, i * nodes:(i + 1) * nodes] = jnp.where(here, value, 0.0).astype(BF16)
        added = lax.dot_general(
            left[:(x1 - x0) * ch, :len(edge) * nodes], jnp.concatenate(hits_edge, axis=1), NT,
            preferred_element_type=F32,
        )
        for x in range(x0, x1):
            inverse = jnp.broadcast_to(c_strip[6, x:x + 1, :], (ch, cz))
            r_strip[x] += added[(x - x0) * ch:(x - x0 + 1) * ch] * inverse

    field = smooth(dims, 0, (fa, fb), (sa, sb), r, r_strip, state, c_strip)
    for x in range(cx):
        for y in range(cy):
            field_out[pl.ds(x * cy + y, ch, stride=cx * cy), :] = field[HALO + x, HALO + y]
    traces = gather_nodes(dims, field, own_row, own_z)
    for other in range(block_out.shape[0]):
        block_out[other] = traces


def per_device(source, labels, region_coeff, node_cell, node_pos, incident):
    ch, cx, cy, cz = source.shape
    nodes = node_cell.shape[0]
    dims = (cx, cy, cz, ch, nodes)
    sizes = tuple(lax.axis_size(axis) for axis in AXES)
    count = math.prod(sizes)
    nx, ny, nz = (2 if size > 2 else 1 for size in sizes)
    scale = KERNEL_GAIN / math.sqrt(nodes * count)
    tx, ty = cx + 2 * HALO, cy + 2 * HALO
    held = held_rows(dims)[1]
    place = jnp.stack([lax.axis_index(axis) for axis in AXES]).astype(jnp.int32)
    rows = cx * cy * ch
    flat = source.reshape(ch * cx * cy, cz)
    marks = labels.reshape(cx * cy, cz)
    cells = node_cell.reshape(1, nodes)
    shape = jax.ShapeDtypeStruct
    vmem = pltpu.VMEM

    height = INCIDENT + ch + cx * cy
    floats = ((node_pos, 0), (region_coeff[None], REGION), (incident, INCIDENT))
    whole = ((cells, CELL), (marks, INCIDENT + ch))

    def lay(entries, dtype):
        total = jnp.zeros((height, cz), dtype)
        for value, row in entries:
            sides = ((row, height - row - value.shape[0], 0), (0, cz - value.shape[1], 0))
            total += lax.pad(value, jnp.zeros((), dtype), sides)
        return total

    small = lay(floats, F32) + lay(whole, jnp.int32).astype(F32)
    rhs, send = kernel_call(
        functools.partial(first_kernel, dims),
        (shape((rows, cz), F32), shape((cx * ch + 16, cz), BF16)),
        [vmem((rows, 2 * nodes), BF16)],
        operands=(flat, small),
        name="scatter_first",
    )

    def halo(main, send, width, with_labels, between=(lambda x: x, lambda x: x)):
        zrecv = exchange(send, "col")
        zrecv = between[0](zrecv)
        extra = HALO * cy + 16 if with_labels else 0
        strip_rows_ = cx * ch + (16 if with_labels else 0)
        own = (main, small) if with_labels else (main,)
        strip, *sends = kernel_call(
            functools.partial(second_kernel, dims, width, with_labels, nz, nx),
            (shape((strip_rows_, cz), BF16),)
            + (shape((sum(x_sizes(dims, width)) + extra, cz), BF16),) * nx,
            [vmem((32, cz), F32)] if with_labels else [],
            smem=1,
            operands=(place, *own, *zrecv),
            name="pack_x",
        )
        xrecv = exchange(None, "vol", sends)
        xrecv = between[1](xrecv)
        extra = tx * HALO + 16 if with_labels else 0
        blocks, y_edge = y_sizes(dims, width)
        sends = kernel_call(
            functools.partial(third_kernel, dims, width, with_labels, nx, ny),
            (shape((sum(blocks) + y_edge + extra, cz), BF16),) * ny,
            [vmem((tx * cy, cz), F32), vmem((tx, cz), F32), vmem((tx * HALO, cz), F32)]
            if with_labels else [],
            smem=1,
            operands=(place, *own, strip, *xrecv),
            name="pack_y",
        )
        yrecv = exchange(None, "row", sends)
        return strip, xrecv, yrecv

    strip, xrecv, yrecv = halo(rhs, send, RHS_HALO, True)
    field, block, send, state, kept, c_strip = kernel_call(
        functools.partial(fourth_kernel, dims, region_coeff.shape[0], nx, ny),
        (
            shape((rows, cz), F32),
            shape((count, ch + 8, nodes), BF16),
            shape((cx * ch, cz), BF16),
            shape((rows + 7 * held, cz), F32),
            shape(((held - cx * cy + tx) * ch, cz), BF16),
            shape((7, tx, cz), F32),
        ),
        [
            vmem((held * ch, cz), F32),
            vmem((tx, ch, cz), F32),
            vmem((tx, ty, ch, cz), F32),
            vmem((tx, ty, ch, cz), F32),
            vmem((tx, ch, cz), F32),
            vmem((tx, ch, cz), F32),
            vmem((tx + 2, ty + 16, cz), F32),
            vmem((tx + 16, cz), F32),
            vmem((tx * cy, cz), F32),
            vmem((tx, cz), F32),
            vmem((tx * HALO, cz), F32),
        ],
        smem=1,
        operands=(place, rhs, small, strip, *xrecv, *yrecv),
        name="sweeps_first",
    )

    def to_all(value):
        return lax.all_to_all(value, AXES, 0, 0, tiled=True)

    blocks = to_all(block)
    sums, half = kernel_call(
        functools.partial(boundary_kernel, dims, count, scale),
        (
            shape((ch, nodes), F32),
            shape((count, ch, nodes), BF16),
        ),
        [vmem((nodes, count * nodes), BF16)],
        operands=(small, blocks),
        name="boundary",
    )

    def after_boundary(arrays):
        return lax.optimization_barrier((arrays, half))[0]

    strip, xrecv, yrecv = halo(field, send, HALO, False, (lambda x: x, after_boundary))
    recv = to_all(half)
    field, block = kernel_call(
        functools.partial(fifth_kernel, dims, sizes, nx, ny),
        (shape((ch * cx * cy, cz), F32), shape((count, ch, nodes), BF16)),
        [
            vmem((held * ch, cz), F32),
            vmem((tx, ch, cz), F32),
            vmem((tx, ty, ch, cz), F32),
            vmem((tx, ty, ch, cz), F32),
            vmem((tx, ch, cz), F32),
            vmem((tx, ch, cz), F32),
            vmem((rows, 6 * nodes), BF16),
        ],
        smem=1,
        operands=(
            place, field, sums, small, recv, blocks, strip, *xrecv, *yrecv, state, kept, c_strip
        ),
        name="sweeps_last",
    )
    blocks, block = lax.optimization_barrier((blocks, block))
    tiles = kernel_call(
        functools.partial(tile_kernel, dims, count, scale),
        shape((nodes, count * nodes), BF16),
        operands=(small, blocks),
        cost=pl.CostEstimate(flops=10**9, bytes_accessed=10**6, transcendentals=10**6),
        name="tiles_last",
    )
    flux = kernel_call(
        functools.partial(last_kernel, dims, count),
        shape((ch, nodes), F32),
        operands=(small, to_all(block), tiles),
        name="flux_last",
    )
    return field.reshape(source.shape), flux


def solution(mesh):
    placed = (
        P(None, "vol", "row", "col"),
        P("vol", "row", "col"),
        P(),
        P(("vol", "row", "col")),
        P(None, ("vol", "row", "col")),
        P(None, ("vol", "row", "col")),
    )
    return jax.shard_map(
        per_device,
        mesh=mesh,
        in_specs=placed,
        out_specs=(P(None, "vol", "row", "col"), P(None, ("vol", "row", "col"))),
        check_vma=False,
    )
```

```python
import functools
import math

import jax
import jax.numpy as jnp
from jax import lax
from jax.experimental import pallas as pl
from jax.experimental.pallas import tpu as pltpu
from jax.sharding import PartitionSpec as P

SWEEPS = 4
ITERS = 2

MASS_TERM = 0.05
SOFTENING = 0.05
KERNEL_GAIN = 2.0

HALO = SWEEPS
RHS_HALO = SWEEPS - 1
STRIP = 2 * HALO
AXES = ("vol", "row", "col")
F32, BF16 = jnp.float32, jnp.bfloat16
CELL, REGION, INCIDENT = 3, 4, 8
SPARE = 4 * 1024 * 1024
NT = (((1,), (1,)), ((), ()))


def sweep_weights(count):
    return [
        1.0 / (1.05 - 0.95 * math.cos(math.pi * (2 * sweep + 1) / (2 * count)))
        for sweep in range(count)
    ]


def iota(shape, dim):
    return lax.broadcasted_iota(jnp.int32, shape, dim)


def kernel_call(body, out_shape, scratch=(), smem=0, operands=(), cost=None, name=None):
    held = [jnp.shape(leaf) + (leaf.dtype,) for leaf in jax.tree.leaves((out_shape, operands))]
    held += [ref.shape + (ref.dtype,) for ref in scratch]
    need = sum(math.prod(entry[:-1]) * jnp.dtype(entry[-1]).itemsize for entry in held)
    specs = [pl.BlockSpec(memory_space=pltpu.SMEM)] * smem
    specs += [pl.BlockSpec(memory_space=pltpu.VMEM)] * (len(operands) - smem)
    return pl.pallas_call(
        body,
        out_shape=out_shape,
        in_specs=specs,
        out_specs=jax.tree.map(lambda _: pl.BlockSpec(memory_space=pltpu.VMEM), out_shape),
        scratch_shapes=list(scratch),
        compiler_params=pltpu.CompilerParams(vmem_limit_bytes=need + SPARE),
        cost_estimate=cost,
        name=name,
    )(*operands)


def layers_left(dims, x, reach):
    cx = dims[0]
    return reach - max(HALO - x, x - (HALO + cx - 1), 0)


@functools.lru_cache
def held_rows(dims):
    cx, cy, cz, ch, nodes = dims
    starts, total = {}, 0
    for x in range(cx + 2 * HALO):
        far = layers_left(dims, x, RHS_HALO)
        if far >= 0:
            starts[x] = (total, HALO - far, HALO + cy + far)
            total += cy + 2 * far
    return starts, total


def row_of(dims, x, y):
    first, y0, y1 = held_rows(dims)[0][x]
    return first + y - y0


@functools.lru_cache(maxsize=None)
def kept_row(dims, x, y):
    cx, cy, cz, ch, nodes = dims
    starts, total = held_rows(dims)
    if HALO <= x < HALO + cx and HALO <= y < HALO + cy:
        return True, (x - HALO) * cy + y - HALO
    before = 0
    for other in sorted(starts):
        first, y0, y1 = starts[other]
        for at in range(y0, y1):
            if (other, at) == (x, y):
                return False, before
            before += not (HALO <= other < HALO + cx and HALO <= at < HALO + cy)
    raise KeyError(x, y)


def x_sizes(dims, width):
    cx, cy, cz, ch, nodes = dims
    return width * cy * ch, (width - 1) * ch


def y_sizes(dims, width):
    cx, cy, cz, ch, nodes = dims
    return [(cx + 2 * (width - d)) * ch for d in range(1, width + 1)], (cx + 2 * (width - 2)) * ch


def pick(refs, low, even, rows, size):
    first = refs[0][pl.ds(rows, size), :]
    flag = jnp.full(first.shape, even, jnp.int32).astype(first.dtype)
    mine, other = (1 - flag, flag) if low else (flag, 1 - flag)
    if len(refs) == 1:
        return first * mine
    return first * mine + refs[1][pl.ds(rows, size), :] * other


def exchange(array, axis, arrays=None):
    count = lax.axis_size(axis)
    arrays = arrays or [array] * 2
    out = []
    for which in range(2 if count > 2 else 1):
        pairs = []
        for i in range(which, count - 1, 2):
            pairs += [(i, i + 1), (i + 1, i)]
        out.append(lax.ppermute(arrays[which], axis, pairs))
    return out


def edge_picker(cz, lanes):
    z, lane = iota((cz, lanes), 0), iota((cz, lanes), 1)
    k = lane % STRIP
    wanted = jnp.where(k < HALO, HALO - 1 - k, cz - 1 - k + HALO)
    return (z == wanted).astype(F32), lane // STRIP - HALO


def strip_rows(read, cx, cy, cz):
    base, lane_y = edge_picker(cz, cz)
    total = None
    for y in range(cy):
        rows = jnp.concatenate([read(x, y).astype(BF16) for x in range(cx)], axis=0)
        picked = jnp.where(lane_y == y, base, 0.0).astype(BF16)
        part = jnp.dot(rows, picked, preferred_element_type=F32)
        total = part if total is None else total + part
    return total.astype(BF16)


def node_places(small):
    cell = small[CELL:CELL + 1, :].astype(jnp.int32)
    cz = small.shape[1]
    return cell // cz, cell % cz


def first_kernel(dims, source, small, rhs_out, send_out, left):
    cx, cy, cz, ch, nodes = dims
    row, z = node_places(small)
    hits = (iota((cz, nodes), 0) == z).astype(BF16)
    flux = small[INCIDENT:INCIDENT + ch, :]
    top = flux.astype(BF16).astype(F32)
    rest = flux - top
    for r in range(cx * cy):
        here = jnp.broadcast_to(row == r, (ch, nodes))
        left[r * ch:(r + 1) * ch, :nodes] = jnp.where(here, top, 0.0).astype(BF16)
        left[r * ch:(r + 1) * ch, nodes:] = jnp.where(here, rest, 0.0).astype(BF16)
    added = lax.dot_general(
        left[...], jnp.concatenate([hits, hits], axis=1), NT, preferred_element_type=F32
    )
    rhs_out[...] = added
    for r in range(cx * cy):
        rhs_out[r * ch:(r + 1) * ch, :] += source[pl.ds(r, ch, stride=cx * cy), :]

    def read(x, y):
        start = (x * cy + y) * ch
        return rhs_out[start:start + ch, :]

    send_out[:cx * ch, :] = strip_rows(read, cx, cy, cz)
    base, lane_y = edge_picker(cz, cz)
    codes = (small[INCIDENT + ch:, :] + 1.0).astype(BF16)
    strips = jnp.dot(codes, base.astype(BF16), preferred_element_type=F32)
    own = (iota(strips.shape, 0) % cy) == lane_y[:1, :]
    strips = jnp.where(own, strips, 0.0).reshape(cx, cy, cz).sum(axis=1)
    send_out[cx * ch:, :] = jnp.concatenate(
        [strips, jnp.zeros((16 - cx, cz), F32)], axis=0
    ).astype(BF16)


def second_kernel(dims, width, with_labels, nz, nx, place, *refs):
    cx, cy, cz, ch, nodes = dims
    main, refs = refs[0], refs[1:]
    if with_labels:
        small, refs = refs[0], refs[1:]
    zrecv, refs = refs[:nz], refs[nz:]
    strip_out, sends, refs = refs[0], refs[1:1 + nx], refs[1 + nx:]
    even_x = 1 - place[0] % 2
    even_z = 1 - place[2] % 2
    rows = cx * ch + (16 if with_labels else 0)
    lane = iota((rows, cz), 1)
    upper = pick(zrecv, False, even_z, 0, rows)
    lower = pick(zrecv, True, even_z, 0, rows)
    strip_out[...] = jnp.where(
        lane % STRIP < HALO, upper.astype(F32), lower.astype(F32)
    ).astype(BF16)
    if with_labels:
        (codes,) = refs
        codes[...] = jnp.zeros_like(codes)
        codes[:16, :] = strip_out[cx * ch:, :].astype(F32)
    slab, edge = x_sizes(dims, width)
    for which in range(nx):
        upward = even_x if which == 0 else 1 - even_x
        x0 = upward * (cx - width)
        send = sends[which]
        send[:slab, :] = main[pl.ds(pl.multiple_of(x0 * (cy * ch), 16), slab), :].astype(BF16)
        x0 = upward * (cx - width + 1)
        send[slab:slab + edge, :] = strip_out[pl.ds(pl.multiple_of(x0 * ch, 16), edge), :]
        if with_labels:
            start = slab + edge
            x0 = upward * (cx - HALO)
            send[start:start + HALO * cy, :] = (
                small[pl.ds(pl.multiple_of(INCIDENT + ch + x0 * cy, 8), HALO * cy), :] + 1.0
            ).astype(BF16)
            send[start + HALO * cy:, :] = codes[pl.ds(x0, 16), :].astype(BF16)


def third_kernel(dims, width, with_labels, nx, ny, place, *refs):
    cx, cy, cz, ch, nodes = dims
    main, refs = refs[0], refs[1:]
    if with_labels:
        small, refs = refs[0], refs[1:]
    strip, refs = refs[0], refs[1:]
    xrecv, refs = refs[:nx], refs[nx:]
    sends, refs = refs[:ny], refs[ny:]
    even_x = 1 - place[0] % 2
    even_y = 1 - place[1] % 2
    slab, edge = x_sizes(dims, width)
    if with_labels:
        codes, strip_codes, picked = refs
        fill_codes(dims, small, strip, xrecv, slab + edge, even_x, codes, strip_codes)
    for which in range(ny):
        send = sends[which]
        upward = even_y if which == 0 else 1 - even_y
        start = 0
        for d in range(1, width + 1):
            y = d - 1 + upward * (cy - 2 * d + 1)
            for x in range(d - width, cx + width - d):
                if 0 <= x < cx:
                    at = pl.multiple_of((x * cy + y) * ch, 16)
                    piece = main[pl.ds(at, ch), :].astype(BF16)
                else:
                    at = pl.multiple_of(((x + width if x < 0 else x - cx) * cy + y) * ch, 16)
                    piece = pick(xrecv, x < 0, even_x, at, ch)
                send[start:start + ch, :] = piece
                start += ch
        side = (width - 2) * ch
        send[start:start + side, :] = pick(xrecv, True, even_x, slab + edge - side, side)
        send[start + side:start + side + cx * ch, :] = strip[:cx * ch, :]
        start += side + cx * ch
        send[start:start + side, :] = pick(xrecv, False, even_x, slab, side)
        start += side
        if with_labels:
            y0 = upward * (cy - HALO)
            tall = cx + 2 * HALO
            for x in range(tall):
                picked[x * HALO:(x + 1) * HALO, :] = codes[pl.ds(x * cy + y0, HALO), :]
            send[start:start + tall * HALO, :] = picked[...].astype(BF16)
            send[start + tall * HALO:, :] = strip_codes[...].astype(BF16)


def fill_codes(dims, small, strip, xrecv, start, even_x, codes, strip_codes):
    cx, cy, cz, ch, nodes = dims
    side = HALO * cy
    codes[:side, :] = pick(xrecv, True, even_x, start, side).astype(F32)
    codes[side:side + cx * cy, :] = small[INCIDENT + ch:, :] + 1.0
    codes[side + cx * cy:, :] = pick(xrecv, False, even_x, start, side).astype(F32)
    strip_codes[:HALO, :] = pick(xrecv, True, even_x, start + side, 16).astype(F32)[:HALO]
    strip_codes[HALO:HALO + cx, :] = strip[cx * ch:cx * ch + 16, :].astype(F32)[:cx]
    strip_codes[HALO + cx:, :] = pick(xrecv, False, even_x, start + side, 16).astype(F32)[:HALO]


def assemble(dims, width, main, strip, xrecv, yrecv, even_x, even_y, put, out_strip):
    cx, cy, cz, ch, nodes = dims
    slab, edge = x_sizes(dims, width)
    blocks, y_edge = y_sizes(dims, width)
    column = cy * ch
    for x in range(cx):
        put(HALO + x, HALO, main[x * column:(x + 1) * column, :].reshape(cy, ch, cz))
    for low in (True, False):
        x0 = HALO - width if low else HALO + cx
        for i in range(width):
            got = pick(xrecv, low, even_x, i * column, column).astype(F32)
            put(x0 + i, HALO, got.reshape(cy, ch, cz))
        start = 0
        for d, size in enumerate(blocks, 1):
            got = pick(yrecv, low, even_y, start, size).astype(F32).reshape(size // ch, 1, ch, cz)
            for i in range(size // ch):
                put(HALO + d - width + i, HALO - d if low else HALO + cy + d - 1, got[i])
            start += size
    own = jnp.concatenate(
        [
            pick(xrecv, True, even_x, slab, edge),
            strip[:cx * ch, :],
            pick(xrecv, False, even_x, slab, edge),
        ],
        axis=0,
    ).astype(F32)
    blank = jnp.zeros((ch, cz), F32)
    low, high = (
        jnp.concatenate([blank, pick(yrecv, low, even_y, start, y_edge).astype(F32), blank], axis=0)
        for low in (True, False)
    )
    full = join_strips(own, low, high, cy)
    out_strip[HALO - width + 1:HALO + cx + width - 1] = full.reshape(cx + 2 * width - 2, ch, cz)


def join_strips(own, low, high, cy):
    lane = iota(own.shape, 1)
    shift = cy * STRIP
    lanes = own.shape[1]
    low = pltpu.roll(low, lanes - shift, 1)
    high = pltpu.roll(high, shift, 1)
    return jnp.where(
        lane < HALO * STRIP, low, jnp.where(lane < (HALO + cy) * STRIP, own, high)
    )


def coefficient(dims, state, k, at):
    cx, cy, cz, ch, nodes = dims
    at += cx * cy * ch + held_rows(dims)[1] * k
    return jnp.broadcast_to(state[at:at + 1, :], (ch, cz))


def sweep(dims, reach, weight, src, src_strip, dst, dst_strip, r, r_strip, state, c_strip):
    cx, cy, cz, ch, nodes = dims
    lane = iota((ch, cz), 1)
    first, last = lane == 0, lane == cz - 1
    k = lane % STRIP
    group = lane // STRIP
    touching = (k == HALO) | (k == HALO - 1)

    def column(x):
        far = layers_left(dims, x, reach)
        low, high = HALO - far, HALO + cy + far
        beyond = src_strip[x]
        ends = jnp.zeros_like(beyond)
        behind, here = src[x, low - 1], src[x, low]
        for y in range(low, high):
            ahead = src[x, y + 1]
            mirror = 2 * HALO + cy - 1 - y
            shared = far > 0 and low < y < high - 1
            both = jnp.where(first | last, src[x, mirror], beyond) if shared else beyond
            edge = pltpu.roll(both, (2 * cz - (y * STRIP + HALO)) % cz, 1)
            if shared:
                ends = jnp.where(touching & (group == mirror), edge, ends)
            above = jnp.where(last, edge, pltpu.roll(here, cz - 1, 1))
            below = jnp.where(first, edge, pltpu.roll(here, 1, 1))
            at = row_of(dims, x, y)
            total = r[at * ch:(at + 1) * ch, :] - here
            total += coefficient(dims, state, 0, at) * src[x + 1, y]
            total += coefficient(dims, state, 1, at) * src[x - 1, y]
            total += coefficient(dims, state, 2, at) * ahead
            total += coefficient(dims, state, 3, at) * behind
            total += coefficient(dims, state, 4, at) * above
            total += coefficient(dims, state, 5, at) * below
            dst[x, y] = here + weight * total
            behind, here = here, ahead
        if far > 0:
            strip_column(x, beyond, ends)

    def strip_column(x, here, ends):
        def spread_strip(k):
            return jnp.broadcast_to(c_strip[k, x:x + 1, :], (ch, cz))

        above = jnp.where(k == HALO, ends, pltpu.roll(here, 1, 1))
        below = jnp.where(k == HALO - 1, ends, pltpu.roll(here, cz - 1, 1))
        total = r_strip[x] - here
        total += spread_strip(0) * src_strip[x + 1]
        total += spread_strip(1) * src_strip[x - 1]
        total += spread_strip(2) * pltpu.roll(here, cz - STRIP, 1)
        total += spread_strip(3) * pltpu.roll(here, STRIP, 1)
        total += spread_strip(4) * above
        total += spread_strip(5) * below
        dst_strip[x] = here + weight * total

    for x in range(HALO - reach, HALO + cx + reach):
        column(x)


def coefficients(dims, kc, kc_strip, state, c_strip):
    cx, cy, cz, ch, nodes = dims
    tx, ty = cx + 2 * HALO, cy + 2 * HALO
    lane = iota((ty, cz), 1)
    y = iota((ty, cz), 0)
    here = kc_strip[8:8 + tx, :]
    group = lane // STRIP
    k = lane % STRIP
    touching = ((k == HALO) | (k == HALO - 1)) & (group == y)
    starts, total = held_rows(dims)
    ends = [jnp.zeros((1, cz), F32)]
    for x in range(1, tx - 1):
        own = kc[x + 1, 8:8 + ty, :]
        moved = pltpu.roll(own, HALO, 1, stride=STRIP, stride_axis=0)
        ends.append(jnp.sum(jnp.where(touching, moved, 0.0), axis=0, keepdims=True))
        beyond = jnp.broadcast_to(kc_strip[8 + x:9 + x, :], (ty, cz))
        upper = jnp.where((group == y) & (k == HALO - 1), beyond, 0.0).sum(axis=1, keepdims=True)
        lower = jnp.where((group == y) & (k == HALO), beyond, 0.0).sum(axis=1, keepdims=True)
        others = [
            kc[x + 2, 8:8 + ty, :],
            kc[x, 8:8 + ty, :],
            kc[x + 1, 9:9 + ty, :],
            kc[x + 1, 7:7 + ty, :],
            jnp.where(lane == cz - 1, upper, pltpu.roll(own, cz - 1, 1)),
            jnp.where(lane == 0, lower, pltpu.roll(own, 1, 1)),
        ]
        first, y0, y1 = starts[x]
        for i, value in enumerate(finish(own, others)):
            at = cx * cy * ch + total * i + first
            state[at:at + y1 - y0, :] = value[y0:y1, :]
    ends = jnp.concatenate(ends + [jnp.zeros((1, cz), F32)], axis=0)
    lane = iota((tx, cz), 1)
    k = lane % STRIP
    others = [
        kc_strip[9:9 + tx, :],
        kc_strip[7:7 + tx, :],
        pltpu.roll(here, cz - STRIP, 1),
        pltpu.roll(here, STRIP, 1),
        jnp.where(k == HALO, ends, pltpu.roll(here, 1, 1)),
        jnp.where(k == HALO - 1, ends, pltpu.roll(here, cz - 1, 1)),
    ]
    for i, value in enumerate(finish(here, others)):
        c_strip[i] = value


def finish(own, others):
    faces = [0.5 * (own + other) for other in others]
    diag = MASS_TERM + faces[0]
    for face in faces[1:]:
        diag = diag + face
    inverse = jnp.where(own > 0.0, 1.0 / diag, 0.0)
    return [face * inverse for face in faces] + [inverse]


def smooth(dims, start, fields, strips, r, r_strip, state, c_strip):
    weights = sweep_weights(SWEEPS)
    now = 0
    for number in range(start, SWEEPS):
        sweep(
            dims, SWEEPS - 1 - number, weights[number], fields[now], strips[now],
            fields[1 - now], strips[1 - now], r, r_strip, state, c_strip,
        )
        now = 1 - now
    return fields[now]


def gather_nodes(dims, field, row, z):
    cx, cy, cz, ch, nodes = dims
    hits = (iota((cz, nodes), 0) == z).astype(BF16)
    rows = field[HALO:HALO + cx, HALO:HALO + cy].reshape(cx * cy * ch, cz).astype(BF16)
    at_z = jnp.dot(rows, hits, preferred_element_type=F32)
    total = jnp.zeros((ch, nodes), F32)
    for r in range(cx * cy):
        here = jnp.broadcast_to(row == r, (ch, nodes))
        total = jnp.where(here, at_z[r * ch:(r + 1) * ch], total)
    return total.astype(BF16)


def fourth_kernel(dims, regions, nx, ny, place, main, small, strip, *refs):
    cx, cy, cz, ch, nodes = dims
    xrecv, yrecv, refs = refs[:nx], refs[nx:nx + ny], refs[nx + ny:]
    field_out, block_out, send_out, state, kept, c_strip, refs = *refs[:6], refs[6:]
    r, r_strip, fa, fb, sa, sb, kc, kc_strip, codes, strip_codes, side_codes = refs
    even_x = 1 - place[0] % 2
    even_y = 1 - place[1] % 2
    tx, ty = cx + 2 * HALO, cy + 2 * HALO
    width = RHS_HALO
    slab, edge = x_sizes(dims, width)
    blocks, y_edge = y_sizes(dims, width)

    fill_codes(
        dims, small, strip, xrecv, slab + edge, even_x, codes, strip_codes
    )
    kc[...] = jnp.zeros_like(kc)
    kc_strip[...] = jnp.zeros_like(kc_strip)

    def conductivity(code):
        value = jnp.zeros_like(code)
        for region in range(regions):
            coeff = jnp.broadcast_to(small[REGION:REGION + 1, region:region + 1], code.shape)
            value = jnp.where(code == region + 1, coeff, value)
        return value

    kc[1:1 + tx, 8 + HALO:8 + HALO + cy] = conductivity(codes[...]).reshape(tx, cy, cz)
    start = sum(blocks) + y_edge
    for low in (True, False):
        got = pick(yrecv, low, even_y, start, tx * HALO).astype(F32)
        side_codes[...] = conductivity(got)
        y0 = 8 if low else 8 + HALO + cy
        for x in range(tx):
            kc[1 + x, y0:y0 + HALO, :] = side_codes[x * HALO:(x + 1) * HALO, :]
    start += tx * HALO
    low = pick(yrecv, True, even_y, start, 16).astype(F32)
    high = pick(yrecv, False, even_y, start, 16).astype(F32)
    kc_strip[8:8 + tx, :] = conductivity(join_strips(strip_codes[...], low, high, cy))
    coefficients(dims, kc, kc_strip, state, c_strip)

    r_strip[...] = jnp.zeros_like(r_strip)
    weight = sweep_weights(SWEEPS)[0]

    def put(x, y, rows):
        for i in range(rows.shape[0]):
            at = row_of(dims, x, y + i)
            value = rows[i] * coefficient(dims, state, 6, at)
            r[at * ch:(at + 1) * ch, :] = value
            fa[x, y + i] = weight * value
            inside, at = kept_row(dims, x, y + i)
            if inside:
                state[at * ch:(at + 1) * ch, :] = value
            else:
                kept[at * ch:(at + 1) * ch, :] = rows[i].astype(BF16)

    assemble(dims, width, main, strip, xrecv, yrecv, even_x, even_y, put, r_strip)
    tx = cx + 2 * HALO
    kept[kept.shape[0] - tx * ch:, :] = r_strip[...].reshape(tx * ch, cz).astype(BF16)
    for x in range(HALO - width, HALO + cx + width):
        value = r_strip[x] * jnp.broadcast_to(c_strip[6, x:x + 1, :], (ch, cz))
        r_strip[x] = value
        sa[x] = weight * value
    field = smooth(dims, 1, (fa, fb), (sa, sb), r, r_strip, state, c_strip)

    field_out[...] = field[HALO:HALO + cx, HALO:HALO + cy].reshape(cx * cy * ch, cz)
    send_out[...] = strip_rows(lambda x, y: field[HALO + x, HALO + y], cx, cy, cz)
    row, z = node_places(small)
    traces = gather_nodes(dims, field, row, z)
    rows = []
    for axis in range(3):
        value = small[axis:axis + 1, :]
        for _ in range(2):
            part = value.astype(BF16).astype(F32)
            rows.append(part)
            value = value - part
    rows += [row.astype(F32), z.astype(F32)]
    rest = jnp.concatenate([traces.astype(F32)] + rows, axis=0).astype(BF16)
    for other in range(block_out.shape[0]):
        block_out[other] = rest


def tile_kernel(dims, count, scale, small, recv, tiles):
    cx, cy, cz, ch, nodes = dims
    own = [jnp.broadcast_to(small[k:k + 1, :], (nodes, nodes)).T for k in range(3)]

    def block(b, _):
        parts = recv[b].astype(F32)[ch:]
        squared = None
        for k in range(3):
            other = parts[2 * k:2 * k + 1] + parts[2 * k + 1:2 * k + 2]
            delta = own[k] - jnp.broadcast_to(other, (nodes, nodes))
            squared = delta * delta if squared is None else squared + delta * delta
        tile = (scale * lax.rsqrt(squared + SOFTENING * SOFTENING)).astype(BF16)
        tiles[:, pl.ds(pl.multiple_of(b * nodes, nodes), nodes)] = tile
        return _

    lax.fori_loop(0, count, block, 0, unroll=math.gcd(count, 4))


def boundary_kernel(dims, count, scale, small, recv, sum_out, half_out, tiles):
    tile_kernel(dims, count, scale, small, recv, tiles)
    total = product(recv, tiles, count, dims)
    sum_out[...] = total
    for other in range(count):
        half_out[other] = total.astype(BF16)


def product(recv, tiles, count, dims):
    cx, cy, cz, ch, nodes = dims
    group = math.gcd(count, 32)

    def part(at):
        traces = jnp.concatenate([recv[at + i][:ch] for i in range(group)], axis=1)
        start = at * nodes
        if not isinstance(at, int):
            start = pl.multiple_of(start, nodes)
        return lax.dot_general(
            traces, tiles[:, pl.ds(start, group * nodes)], NT, preferred_element_type=F32
        )

    if group == count:
        return part(0)
    return lax.fori_loop(
        0, count // group, lambda i, total: total + part(i * group), jnp.zeros((ch, nodes), F32)
    )


def last_kernel(dims, count, small, recv, tiles, flux_out):
    cx, cy, cz, ch, nodes = dims
    incident = small[INCIDENT:INCIDENT + ch, :]
    flux_out[...] = incident + product(recv, tiles, count, dims)


def fifth_kernel(dims, sizes, nx, ny, place, main, sums, small, recv, blocks, strip, *refs):
    cx, cy, cz, ch, nodes = dims
    xrecv, yrecv, refs = refs[:nx], refs[nx:nx + ny], refs[nx + ny:]
    state, kept, c_strip, refs = *refs[:3], refs[3:]
    field_out, block_out, refs = *refs[:2], refs[2:]
    r, r_strip, fa, fb, sa, sb, left = refs
    even_x = 1 - place[0] % 2
    even_y = 1 - place[1] % 2
    width = RHS_HALO
    tx = cx + 2 * HALO
    for x in range(tx):
        at = kept.shape[0] - (tx - x) * ch
        r_strip[x] = kept[at:at + ch, :].astype(F32) * jnp.broadcast_to(
            c_strip[6, x:x + 1, :], (ch, cz)
        )
    sa[...] = jnp.zeros_like(sa)

    def put(x, y, rows):
        fa[x, y:y + rows.shape[0]] = rows

    assemble(dims, HALO, main, strip, xrecv, yrecv, even_x, even_y, put, sa)

    def neighbour(dx, dy, dz):
        at = [place[i] + d for i, d in enumerate((dx, dy, dz))]
        good = None
        for i, size in enumerate(sizes):
            ok = (at[i] >= 0) & (at[i] < size)
            good = ok if good is None else good & ok
            at[i] = jnp.clip(at[i], 0, size - 1)
        index = (at[0] * sizes[1] + at[1]) * sizes[2] + at[2]
        info = blocks[index].astype(F32)[ch:]
        good = jnp.full((1, nodes), good.astype(jnp.int32), jnp.int32) > 0
        row = jnp.where(good, info[6:7].astype(jnp.int32), -1)
        return recv[index].astype(F32), row, info[7:8].astype(jnp.int32)

    spans = {
        -1: (HALO - width, HALO, cx), 0: (HALO, HALO + cx, 0), 1: (HALO + cx, HALO + cx + width, -cx),
    }
    own_row, own_z = node_places(small)
    strip_lane = iota((cz, nodes), 0)
    starts = held_rows(dims)[0]
    for dx in (-1, 0, 1):
        x0, x1, back_x = spans[dx]
        edge = []
        hits_edge = []
        for dy in (-1, 0, 1):
            y0, y1, back_y = spans[dy]
            parts = []
            if dx == 0 and dy == 0:
                top = sums[...].astype(BF16).astype(F32)
                row, z = own_row, own_z
                parts = [top, sums[...] - top]
            else:
                value, row, z = neighbour(dx, dy, 0)
                parts = [value]
            hits = (iota((cz, nodes), 0) == z).astype(BF16)
            hits = jnp.concatenate([hits] * len(parts), axis=1)
            cells = [
                (x, y) for x in range(x0, x1) for y in range(y0, y1)
                if starts[x][1] <= y < starts[x][2]
            ]
            for at, (x, y) in enumerate(cells):
                wanted = (x - HALO + back_x) * cy + (y - HALO + back_y)
                here = jnp.broadcast_to(row == wanted, (ch, nodes))
                for i, value in enumerate(parts):
                    left[at * ch:(at + 1) * ch, i * nodes:(i + 1) * nodes] = jnp.where(
                        here, value, 0.0
                    ).astype(BF16)
            added = lax.dot_general(
                left[:len(cells) * ch, :len(parts) * nodes], hits, NT, preferred_element_type=F32
            )
            for i, (x, y) in enumerate(cells):
                at = row_of(dims, x, y)
                inverse = coefficient(dims, state, 6, at)
                more = added[i * ch:(i + 1) * ch]
                inside, old = kept_row(dims, x, y)
                if inside:
                    value = state[old * ch:(old + 1) * ch, :] + more * inverse
                else:
                    value = (kept[old * ch:(old + 1) * ch, :].astype(F32) + more) * inverse
                r[at * ch:(at + 1) * ch, :] = value
            for dz in (-1, 1):
                value, row, z = neighbour(dx, dy, dz)
                y = row % cy + cy * dy + HALO
                k = HALO - 1 - z if dz > 0 else HALO + cz - 1 - z
                good = (row >= 0) & (y >= 0) & (y < cy + 2 * HALO) & (k >= 0) & (k < STRIP)
                good = good & ((k < HALO) if dz > 0 else (k >= HALO))
                lane = jnp.where(good, y * STRIP + k, -1)
                hits_edge.append((strip_lane == lane).astype(BF16))
                edge.append((value, jnp.where(row >= 0, row // cy, -1)))
        for x in range(x0, x1):
            at = (x - x0) * ch
            for i, (value, node_x) in enumerate(edge):
                here = jnp.broadcast_to(node_x == x - HALO + back_x, (ch, nodes))
                left[at:at + ch, i * nodes:(i + 1) * nodes] = jnp.where(here, value, 0.0).astype(BF16)
        added = lax.dot_general(
            left[:(x1 - x0) * ch, :len(edge) * nodes], jnp.concatenate(hits_edge, axis=1), NT,
            preferred_element_type=F32,
        )
        for x in range(x0, x1):
            inverse = jnp.broadcast_to(c_strip[6, x:x + 1, :], (ch, cz))
            r_strip[x] += added[(x - x0) * ch:(x - x0 + 1) * ch] * inverse

    field = smooth(dims, 0, (fa, fb), (sa, sb), r, r_strip, state, c_strip)
    for x in range(cx):
        for y in range(cy):
            field_out[pl.ds(x * cy + y, ch, stride=cx * cy), :] = field[HALO + x, HALO + y]
    traces = gather_nodes(dims, field, own_row, own_z)
    for other in range(block_out.shape[0]):
        block_out[other] = traces


def per_device(source, labels, region_coeff, node_cell, node_pos, incident):
    ch, cx, cy, cz = source.shape
    nodes = node_cell.shape[0]
    dims = (cx, cy, cz, ch, nodes)
    sizes = tuple(lax.axis_size(axis) for axis in AXES)
    count = math.prod(sizes)
    nx, ny, nz = (2 if size > 2 else 1 for size in sizes)
    scale = KERNEL_GAIN / math.sqrt(nodes * count)
    tx, ty = cx + 2 * HALO, cy + 2 * HALO
    held = held_rows(dims)[1]
    place = jnp.stack([lax.axis_index(axis) for axis in AXES]).astype(jnp.int32)
    rows = cx * cy * ch
    flat = source.reshape(ch * cx * cy, cz)
    marks = labels.reshape(cx * cy, cz)
    cells = node_cell.reshape(1, nodes)
    shape = jax.ShapeDtypeStruct
    vmem = pltpu.VMEM

    height = INCIDENT + ch + cx * cy
    floats = ((node_pos, 0), (region_coeff[None], REGION), (incident, INCIDENT))
    whole = ((cells, CELL), (marks, INCIDENT + ch))

    def lay(entries, dtype):
        total = jnp.zeros((height, cz), dtype)
        for value, row in entries:
            sides = ((row, height - row - value.shape[0], 0), (0, cz - value.shape[1], 0))
            total += lax.pad(value, jnp.zeros((), dtype), sides)
        return total

    small = lay(floats, F32) + lay(whole, jnp.int32).astype(F32)
    rhs, send = kernel_call(
        functools.partial(first_kernel, dims),
        (shape((rows, cz), F32), shape((cx * ch + 16, cz), BF16)),
        [vmem((rows, 2 * nodes), BF16)],
        operands=(flat, small),
        name="scatter_first",
    )

    def halo(main, send, width, with_labels, between=(lambda x: x, lambda x: x)):
        zrecv = exchange(send, "col")
        zrecv = between[0](zrecv)
        extra = HALO * cy + 16 if with_labels else 0
        strip_rows_ = cx * ch + (16 if with_labels else 0)
        own = (main, small) if with_labels else (main,)
        strip, *sends = kernel_call(
            functools.partial(second_kernel, dims, width, with_labels, nz, nx),
            (shape((strip_rows_, cz), BF16),)
            + (shape((sum(x_sizes(dims, width)) + extra, cz), BF16),) * nx,
            [vmem((32, cz), F32)] if with_labels else [],
            smem=1,
            operands=(place, *own, *zrecv),
            name="pack_x",
        )
        xrecv = exchange(None, "vol", sends)
        xrecv = between[1](xrecv)
        extra = tx * HALO + 16 if with_labels else 0
        blocks, y_edge = y_sizes(dims, width)
        sends = kernel_call(
            functools.partial(third_kernel, dims, width, with_labels, nx, ny),
            (shape((sum(blocks) + y_edge + extra, cz), BF16),) * ny,
            [vmem((tx * cy, cz), F32), vmem((tx, cz), F32), vmem((tx * HALO, cz), F32)]
            if with_labels else [],
            smem=1,
            operands=(place, *own, strip, *xrecv),
            name="pack_y",
        )
        yrecv = exchange(None, "row", sends)
        return strip, xrecv, yrecv

    strip, xrecv, yrecv = halo(rhs, send, RHS_HALO, True)
    field, block, send, state, kept, c_strip = kernel_call(
        functools.partial(fourth_kernel, dims, region_coeff.shape[0], nx, ny),
        (
            shape((rows, cz), F32),
            shape((count, ch + 8, nodes), BF16),
            shape((cx * ch, cz), BF16),
            shape((rows + 7 * held, cz), F32),
            shape(((held - cx * cy + tx) * ch, cz), BF16),
            shape((7, tx, cz), F32),
        ),
        [
            vmem((held * ch, cz), F32),
            vmem((tx, ch, cz), F32),
            vmem((tx, ty, ch, cz), F32),
            vmem((tx, ty, ch, cz), F32),
            vmem((tx, ch, cz), F32),
            vmem((tx, ch, cz), F32),
            vmem((tx + 2, ty + 16, cz), F32),
            vmem((tx + 16, cz), F32),
            vmem((tx * cy, cz), F32),
            vmem((tx, cz), F32),
            vmem((tx * HALO, cz), F32),
        ],
        smem=1,
        operands=(place, rhs, small, strip, *xrecv, *yrecv),
        name="sweeps_first",
    )

    def to_all(value):
        return lax.all_to_all(value, AXES, 0, 0, tiled=True)

    blocks = to_all(block)
    sums, half = kernel_call(
        functools.partial(boundary_kernel, dims, count, scale),
        (
            shape((ch, nodes), F32),
            shape((count, ch, nodes), BF16),
        ),
        [vmem((nodes, count * nodes), BF16)],
        operands=(small, blocks),
        name="boundary",
    )

    def after_boundary(arrays):
        return lax.optimization_barrier((arrays, half))[0]

    strip, xrecv, yrecv = halo(field, send, HALO, False, (lambda x: x, after_boundary))
    recv = to_all(half)
    field, block = kernel_call(
        functools.partial(fifth_kernel, dims, sizes, nx, ny),
        (shape((ch * cx * cy, cz), F32), shape((count, ch, nodes), BF16)),
        [
            vmem((held * ch, cz), F32),
            vmem((tx, ch, cz), F32),
            vmem((tx, ty, ch, cz), F32),
            vmem((tx, ty, ch, cz), F32),
            vmem((tx, ch, cz), F32),
            vmem((tx, ch, cz), F32),
            vmem((rows, 6 * nodes), BF16),
        ],
        smem=1,
        operands=(
            place, field, sums, small, recv, blocks, strip, *xrecv, *yrecv, state, kept, c_strip
        ),
        name="sweeps_last",
    )
    blocks, block = lax.optimization_barrier((blocks, block))
    tiles = kernel_call(
        functools.partial(tile_kernel, dims, count, scale),
        shape((nodes, count * nodes), BF16),
        operands=(small, blocks),
        cost=pl.CostEstimate(flops=10**9, bytes_accessed=10**6, transcendentals=10**6),
        name="tiles_last",
    )
    flux = kernel_call(
        functools.partial(last_kernel, dims, count),
        shape((ch, nodes), F32),
        operands=(small, to_all(block), tiles),
        name="flux_last",
    )
    return field.reshape(source.shape), flux


def solution(mesh):
    placed = (
        P(None, "vol", "row", "col"),
        P("vol", "row", "col"),
        P(),
        P(("vol", "row", "col")),
        P(None, ("vol", "row", "col")),
        P(None, ("vol", "row", "col")),
    )
    return jax.shard_map(
        per_device,
        mesh=mesh,
        in_specs=placed,
        out_specs=(P(None, "vol", "row", "col"), P(None, ("vol", "row", "col"))),
        check_vma=False,
    )
```
